128 devices in a mesh: gx: 8 (over z, core), gy: 16 (over y, x).
Axes of the slice: x: 4, y: 4, z: 4, core: 2. Of those that a mesh axis runs over, the one named last changes fastest.
Arguments:
- features: bfloat16 [8, 16, 4, 512, 128], P('gx', 'gy'), may hold values from -6 to 6
- slot_cell: int32 [8, 16, 4], P('gx', 'gy'), may hold values from -1 to 7, as said below
- neighbours: int32 [8, 16, 4, 26], P('gx', 'gy'), may hold values from -1 to 35, as said below
- first_weight: bfloat16 [3, 3, 3, 128, 128], replicated, may hold values from -0.109375 to 0.109375
- first_bias: float32 [128], replicated, may hold values from -3 to 3
- second_weight: bfloat16 [3, 3, 3, 128, 128], replicated, may hold values from -0.109375 to 0.109375
- second_bias: float32 [128], replicated, may hold values from -3 to 3
- coarse_weight: bfloat16 [3, 3, 3, 128, 256], replicated, may hold values from -0.109375 to 0.109375
- coarse_bias: float32 [256], replicated, may hold values from -3 to 3
- lift_weight: bfloat16 [256, 128], replicated, may hold values from -0.375 to 0.375
Outputs:
- output: float32 [8, 16, 4, 512, 128], P('gx', 'gy')
The draws below stay inside these ranges and needn't reach their ends.
Inputs may be any that keep to these rules, and one draw needn't show every extreme that they name: `slot_cell`: in every tile the live slots are slots 0 to n - 1, with n from 1 to 4, and name distinct cells of the tile's 2 x 2 x 2 cells; the other slots hold -1; some tile holds 4 live bricks in every draw, and some tile only one. `neighbours`: the entries agree with slot_cell: entry k of a live slot names the live brick at that brick offset, which lies in the tile itself or one of its 8 neighbour tiles, and is -1 where that cell is empty or outside the scene; all entries of empty slots are -1.
All inputs are finite; a program needn't handle non-finite values.
Results may differ from the reference program's by a relative error of at most 0.0022.
Values may be sent and summed in bfloat16 or wider, within the bound.
A program may use at most 128 MiB of HBM per device.

```python
import jax
import jax.numpy as jnp

C1 = 128
C2 = 256
VOX = 512
BR_DEV = 4
TX = 8
TY = 16


OFFSETS = [(step_x, step_y, step_z) for step_x in (-1, 0, 1) for step_y in (-1, 0, 1) for step_z in (-1, 0, 1) if (step_x, step_y, step_z) != (0, 0, 0)]


def brick_cells(key):
    tile_count = TX * TY
    cell_total = 2 * BR_DEV
    key_count, key_full, key_order = jax.random.split(key, 3)
    live_counts = jax.random.randint(key_count, (tile_count,), 1, BR_DEV + 1)
    full_tile = jax.random.randint(key_full, (), 0, tile_count)
    sparse_tile = (full_tile + 1) % tile_count
    tile_ids = jnp.arange(tile_count)
    live_counts = jnp.where(tile_ids == full_tile, BR_DEV, live_counts)
    live_counts = jnp.where(tile_ids == sparse_tile, 1, live_counts)
    scores = jax.random.randint(key_order, (tile_count, cell_total), 0, 1 << 20) * cell_total + jnp.arange(cell_total)[None, :]
    last_cell = (tile_ids[:, None] == full_tile) & (jnp.arange(cell_total)[None, :] == cell_total - 1)
    scores = jnp.where(last_cell, -1, scores)
    ranking = jnp.argsort(scores, axis=1)[:, :BR_DEV].astype(jnp.int32)
    slot_ids = jnp.arange(BR_DEV)[None, :]
    cell_codes = jnp.where(slot_ids < live_counts[:, None], ranking, -1)
    return cell_codes.reshape(TX, TY, BR_DEV).astype(jnp.int32)


def neighbour_table(cell_codes):
    layers = BR_DEV // 2
    alive_slot = cell_codes >= 0
    safe_codes = jnp.maximum(cell_codes, 0)
    column_a = safe_codes // (2 * layers)
    column_b = safe_codes // layers % 2
    height = safe_codes % layers
    tile_x = jnp.arange(TX, dtype=jnp.int32)[:, None, None]
    tile_y = jnp.arange(TY, dtype=jnp.int32)[None, :, None]
    pos_x = 2 * tile_x + column_a
    pos_y = 2 * tile_y + column_b
    slot_ids = jnp.broadcast_to(jnp.arange(BR_DEV, dtype=jnp.int32)[None, None, :], cell_codes.shape)
    occupancy = jnp.full((2 * TX + 2, 2 * TY + 2, layers + 2), -1, jnp.int32)
    occupancy = occupancy.at[jnp.where(alive_slot, pos_x + 1, 0), jnp.where(alive_slot, pos_y + 1, 0), jnp.where(alive_slot, height + 1, 0)].set(jnp.where(alive_slot, slot_ids, -1).astype(jnp.int32))
    columns = []
    for step_x, step_y, step_z in OFFSETS:
        near_x = pos_x + step_x
        near_y = pos_y + step_y
        near_z = height + step_z
        found_slot = occupancy[near_x + 1, near_y + 1, near_z + 1]
        block_id = (near_x // 2 - tile_x + 1) * 3 + (near_y // 2 - tile_y + 1)
        columns.append(jnp.where(alive_slot & (found_slot >= 0), block_id * BR_DEV + found_slot, -1))
    return jnp.stack(columns, axis=-1).astype(jnp.int32)


def draw_slot_cell(key, part):
    return brick_cells(key)


def draw_neighbours(key, part):
    return neighbour_table(brick_cells(key))


def shard_levels(key, dims, cuts, least, high):
    loudness = 1.0
    for axis_at, shards_of in cuts:
        heights = jax.random.uniform(jax.random.fold_in(jax.random.fold_in(key, 6), axis_at), (shards_of,), jnp.float32, least / len(cuts), high / len(cuts))
        loudness = loudness * jnp.repeat(jnp.exp(heights), dims[axis_at] // shards_of).reshape((-1,) + (1,) * (len(dims) - 1 - axis_at))
    return loudness


def normal_values(own_key, shape, deviation, bound, shards=(), kind=jnp.bfloat16):
    values = jax.random.normal(own_key, shape, jnp.float32) * deviation
    if len(shards) > 0:
        values = shard_levels(own_key, shape, shards, -0.22, 0.18) * values
    return jnp.clip(values, min=-bound, max=bound).astype(kind)


def setup_inputs(seed: int = 0) -> dict:
    key_list = jax.random.split(jax.random.key(seed), 11)
    features = normal_values(key_list[0], (TX, TY, BR_DEV, VOX, C1), 1.0, 6.0, ((0, 8), (1, 16)))
    slot_cell = draw_slot_cell(jax.random.fold_in(key_list[10], 71), 0)
    neighbours = draw_neighbours(jax.random.fold_in(key_list[10], 71), 0)
    first_weight = normal_values(key_list[3], (3, 3, 3, C1, C1), (27 * C1) ** -0.5, 0.109375)
    first_bias = normal_values(key_list[4], (C1,), 0.5, 3.0, (), jnp.float32)
    second_weight = normal_values(key_list[5], (3, 3, 3, C1, C1), (27 * C1) ** -0.5, 0.109375)
    second_bias = normal_values(key_list[6], (C1,), 0.5, 3.0, (), jnp.float32)
    coarse_weight = normal_values(key_list[7], (3, 3, 3, C1, C2), (27 * C1) ** -0.5, 0.109375)
    coarse_bias = normal_values(key_list[8], (C2,), 0.5, 3.0, (), jnp.float32)
    lift_weight = normal_values(key_list[9], (C2, C1), C2 ** -0.5, 0.375)
    return dict(features=features, slot_cell=slot_cell, neighbours=neighbours, first_weight=first_weight, first_bias=first_bias, second_weight=second_weight, second_bias=second_bias, coarse_weight=coarse_weight, coarse_bias=coarse_bias, lift_weight=lift_weight)


OFFSETS = [(step_x, step_y, step_z) for step_x in (-1, 0, 1) for step_y in (-1, 0, 1) for step_z in (-1, 0, 1) if (step_x, step_y, step_z) != (0, 0, 0)]


def window(offset):
    if offset < 0:
        return slice(7, 8)
    if offset > 0:
        return slice(0, 1)
    return slice(0, 8)


def assemble(own_bricks, slab_source, neighbour_ids):
    pieces = {}
    for number, offset in enumerate(OFFSETS):
        source = slab_source(offset)
        entries = neighbour_ids[:, number]
        picked = jnp.take(source, jnp.clip(entries, 0, source.shape[0] - 1), axis=0)
        pieces[offset] = jnp.where((entries >= 0)[:, None, None, None, None], picked, jnp.zeros_like(picked))
    pieces[(0, 0, 0)] = own_bricks
    planes = []
    for step_x in (-1, 0, 1):
        strips = []
        for step_y in (-1, 0, 1):
            strips.append(jnp.concatenate([pieces[(step_x, step_y, step_z)] for step_z in (-1, 0, 1)], axis=3))
        planes.append(jnp.concatenate(strips, axis=2))
    return jnp.concatenate(planes, axis=1)


def convolve(padded, weight):
    batch_size = padded.shape[0]
    size_x, size_y, size_z = padded.shape[1] - 2, padded.shape[2] - 2, padded.shape[3] - 2
    channels = padded.shape[4]
    outputs = weight.shape[4]
    summed = jnp.zeros((batch_size * size_x * size_y * size_z, outputs), jnp.float32)
    for kernel_x in range(3):
        for kernel_y in range(3):
            patches = jnp.concatenate([padded[:, kernel_x:kernel_x + size_x, kernel_y:kernel_y + size_y, kernel_z:kernel_z + size_z] for kernel_z in range(3)], axis=4)
            summed = summed + jnp.dot(patches.reshape(-1, 3 * channels), weight[kernel_x, kernel_y].reshape(3 * channels, outputs), preferred_element_type=jnp.float32)
    return summed.reshape(batch_size, size_x, size_y, size_z, outputs)


def pool_tile(fine_field, cell_codes):
    slot_count = cell_codes.shape[0]
    channels = fine_field.shape[-1]
    layer_count = slot_count // 2
    averaged = fine_field.reshape(slot_count, 4, 2, 4, 2, 4, 2, channels).mean(axis=(2, 4, 6)).astype(jnp.bfloat16)
    one_hot = (jnp.arange(2 * slot_count, dtype=jnp.int32)[:, None] == cell_codes[None, :]).astype(jnp.bfloat16)
    placed = jnp.dot(one_hot, averaged.reshape(slot_count, -1), preferred_element_type=jnp.float32).astype(jnp.bfloat16)
    placed = placed.reshape(2, 2, layer_count, 4, 4, 4, channels).transpose(0, 3, 1, 4, 2, 5, 6)
    return placed.reshape(8, 8, 4 * layer_count, channels)


def coarse_mask(cell_codes):
    slot_count = cell_codes.shape[0]
    layer_count = slot_count // 2
    cell_hits = (jnp.arange(2 * slot_count, dtype=jnp.int32)[:, None] == cell_codes[None, :]).astype(jnp.int32).sum(axis=1)
    per_layer = cell_hits.reshape(2, 2, layer_count).sum(axis=(0, 1)).reshape(layer_count // 2, 2).sum(axis=1)
    layer_live = (per_layer > 0).astype(jnp.float32)
    return jnp.broadcast_to(jnp.repeat(layer_live, 8)[None, None, :], (8, 8, 4 * layer_count))


def lift_tile(lifted, cell_codes):
    channels = lifted.shape[-1]
    layer_count = lifted.shape[2] // 4
    grouped = lifted.reshape(2, 4, 2, 4, layer_count, 4, channels).transpose(0, 2, 4, 1, 3, 5, 6).reshape(4 * layer_count, 4, 4, 4, channels)
    picked = jnp.take(grouped, jnp.maximum(cell_codes, 0), axis=0)
    return jnp.repeat(jnp.repeat(jnp.repeat(picked, 2, axis=1), 2, axis=2), 2, axis=3)


def reference(features, slot_cell, neighbours, first_weight, first_bias, second_weight, second_bias, coarse_weight, coarse_bias, lift_weight):
    channels = features.shape[-1]
    bricks = TX * TY * BR_DEV
    live_mask = (slot_cell >= 0).astype(jnp.float32).reshape(bricks, 1, 1, 1, 1)
    tile_x = jnp.arange(TX, dtype=jnp.int32)[:, None, None, None]
    tile_y = jnp.arange(TY, dtype=jnp.int32)[None, :, None, None]
    block_id = neighbours // BR_DEV
    within = neighbours % BR_DEV
    global_id = ((tile_x + block_id // 3) * (TY + 2) + (tile_y + block_id % 3)) * BR_DEV + within
    neighbour_ids = jnp.where(neighbours >= 0, global_id, -1).reshape(bricks, 26).astype(jnp.int32)

    def sparse_conv(brick_field, weight):
        width = brick_field.shape[-1]
        tile_grid = brick_field.reshape(TX, TY, BR_DEV, 8, 8, 8, width)
        tile_grid = jnp.pad(tile_grid, ((1, 1), (1, 1), (0, 0), (0, 0), (0, 0), (0, 0), (0, 0)))
        flat_grid = tile_grid.reshape(-1, 8, 8, 8, width)

        def slab_source(offset):
            return flat_grid[:, window(offset[0]), window(offset[1]), window(offset[2])]

        return convolve(assemble(brick_field, slab_source, neighbour_ids), weight)

    inputs = features.reshape(bricks, 8, 8, 8, channels)
    hidden = (jax.nn.relu(sparse_conv(inputs, first_weight) + first_bias) * live_mask).astype(jnp.bfloat16)
    fine_field = (sparse_conv(hidden, second_weight) + second_bias + inputs.astype(jnp.float32)) * live_mask
    fine_tiles = fine_field.reshape(TX, TY, BR_DEV, 8, 8, 8, channels)
    pooled = jax.vmap(jax.vmap(pool_tile))(fine_tiles, slot_cell)
    masks = jax.vmap(jax.vmap(coarse_mask))(slot_cell)
    layers = pooled.shape[4]
    pooled_grid = pooled.transpose(0, 2, 1, 3, 4, 5).reshape(1, 8 * TX, 8 * TY, layers, channels)
    mask_grid = masks.transpose(0, 2, 1, 3, 4).reshape(8 * TX, 8 * TY, layers, 1)
    padded = jnp.pad(pooled_grid, ((0, 0), (1, 1), (1, 1), (1, 1), (0, 0)))
    coarse = (jax.nn.relu(convolve(padded, coarse_weight)[0] + coarse_bias) * mask_grid).astype(jnp.bfloat16)
    lifted = jnp.dot(coarse.reshape(-1, coarse.shape[-1]), lift_weight, preferred_element_type=jnp.float32)
    lifted = lifted.reshape(TX, 8, TY, 8, layers, channels).transpose(0, 2, 1, 3, 4, 5)
    raised = jax.vmap(jax.vmap(lift_tile))(lifted, slot_cell)
    output = (fine_tiles + raised) * live_mask.reshape(TX, TY, BR_DEV, 1, 1, 1, 1)
    return output.reshape(TX, TY, BR_DEV, VOX, channels)
```

```python
import functools

import jax
import jax.numpy as jnp
from jax import lax
from jax.experimental import pallas as pl
from jax.experimental.pallas import tpu as pltpu
from jax.sharding import PartitionSpec as P

MESH = pl.DeviceIdType.MESH
F32 = jnp.float32
BF16 = jnp.bfloat16

OFFSETS = [
    (ox, oy, oz)
    for ox in (-1, 0, 1)
    for oy in (-1, 0, 1)
    for oz in (-1, 0, 1)
    if (ox, oy, oz) != (0, 0, 0)
]
NUMBER = {offset: k for k, offset in enumerate(OFFSETS)}
SIDES = [(-1, 0), (1, 0), (0, -1), (0, 1)]
EDGES = [(-1, -1), (-1, 1), (1, -1), (1, 1)]
ALL = SIDES + EDGES


def edge_of(step, last):
    return last if step < 0 else 0


def kernel(
    gx,
    gy,
    cell,
    nbr,
    feat,
    w1,
    b1,
    w2,
    b2,
    wc,
    bc,
    wl,
    out,
    staged,
    field,
    hidden,
    coarse_field,
    side_src,
    edge_src,
    cside_src,
    cedge_src,
    zin,
    zhid,
    zc,
    w1p,
    w2p,
    wcv,
    wlv,
    joined,
    send_side,
    send_edge,
    recv_side,
    recv_edge,
    csend_side,
    csend_edge,
    crecv_side,
    crecv_edge,
    local_sem,
    out_sem,
    send_sem,
    recv_sem,
):
    mx = lax.axis_index("gx")
    my = lax.axis_index("gy")

    copies = [
        pltpu.make_async_copy(feat, staged, local_sem.at[0]),
        pltpu.make_async_copy(w1, w1p.at[0:3, :, :, 0:128], local_sem.at[1]),
        pltpu.make_async_copy(w1, w1p.at[1:4, :, :, 128:256], local_sem.at[2]),
        pltpu.make_async_copy(w2, w2p.at[0:3, :, :, 0:128], local_sem.at[3]),
        pltpu.make_async_copy(w2, w2p.at[1:4, :, :, 128:256], local_sem.at[4]),
        pltpu.make_async_copy(wc, wcv, local_sem.at[5]),
        pltpu.make_async_copy(wl, wlv, local_sem.at[6]),
    ]
    for copy in copies:
        copy.start()

    def device_at(ox, oy):
        return (lax.rem(mx + ox + gx, gx), lax.rem(my + oy + gy, gy))

    barrier = pltpu.get_barrier_semaphore()
    for ox, oy in ALL:
        pl.semaphore_signal(
            barrier, inc=1, device_id=device_at(ox, oy), device_id_type=MESH
        )

    for wp in (w1p, w2p):
        wp[3, :, :, 0:128] = jnp.zeros((3, 384, 128), BF16)
        wp[0, :, :, 128:256] = jnp.zeros((3, 384, 128), BF16)
    field[4] = jnp.zeros((8, 8, 8, 128), F32)
    hidden[4] = jnp.zeros((8, 8, 8, 128), F32)
    coarse_field[4] = jnp.zeros((4, 4, 8, 128), F32)
    for d in range(4):
        side_src[d, 8] = jnp.zeros((8, 8, 128), F32)
        cside_src[d, 8] = jnp.zeros((4, 8, 128), F32)
        edge_src[d, 16] = jnp.zeros((1, 8, 128), F32)
        cedge_src[d, 16] = jnp.zeros((1, 8, 128), F32)

    live = [jnp.where(cell[s] >= 0, 1.0, 0.0).astype(F32) for s in range(4)]

    def index(s, ox, oy, oz):
        if (ox, oy, oz) == (0, 0, 0):
            return s
        entry = nbr[s, NUMBER[ox, oy, oz]]
        safe = jnp.maximum(entry, 0)
        block = lax.shift_right_logical(safe, 2)
        slot = lax.bitwise_and(safe, 3)
        if (ox, oy) == (0, 0):
            return jnp.where(entry < 0, 4, slot)
        if ox == 0 or oy == 0:
            place = slot + jnp.where(block == 4, 0, 4)
            return jnp.where(entry < 0, 8, place)
        beside_x = (ox + 1) * 3 + 1
        beside_y = 3 + (oy + 1)
        place = slot + jnp.where(
            block == 4,
            0,
            jnp.where(block == beside_x, 4, jnp.where(block == beside_y, 8, 12)),
        )
        return jnp.where(entry < 0, 16, place)

    where = {
        (s, ox, oy, oz): index(s, ox, oy, oz)
        for s in range(4)
        for ox in (-1, 0, 1)
        for oy in (-1, 0, 1)
        for oz in (-1, 0, 1)
    }

    def shifted(low, own, high, step):
        row = lax.broadcasted_iota(jnp.int32, own.shape, own.ndim - 2)
        axis = own.ndim - 2
        down = pltpu.roll(jnp.where(row >= 8 - step, low, own), step, axis)
        up = pltpu.roll(jnp.where(row < step, high, own), 8 - step, axis)
        return down, own, up

    def pair(fetch, ox, oy, step):
        for half in (0, 1):
            parts = [
                shifted(
                    *[fetch(where[s, ox, oy, oz]) for oz in (-1, 0, 1)], step
                )
                for s in (2 * half, 2 * half + 1)
            ]
            for kz in range(3):
                both = jnp.concatenate([parts[0][kz], parts[1][kz]], axis=-2)
                yield slice(16 * half, 16 * half + 16), slice(
                    128 * kz, 128 * kz + 128
                ), both.astype(BF16)

    def fine_centre(source, z):
        def body(m, carry):
            for parity in (0, 1):
                x = 2 * m + parity
                for rows, lanes, value in pair(lambda q: source[q, x], 0, 0, 1):
                    if parity == 0:
                        z[1, m, 1:9, rows, lanes] = value
                    else:
                        z[0, m + 1, 1:9, rows, lanes] = value
            return carry

        lax.fori_loop(0, 4, body, 0)

    def fine_rim(z):
        for d, (ox, oy) in enumerate(SIDES):
            for rows, lanes, value in pair(lambda q: side_src[d, q], ox, oy, 1):
                if ox < 0:
                    z[0, 0, 1:9, rows, lanes] = value
                elif ox > 0:
                    z[1, 4, 1:9, rows, lanes] = value
                else:
                    y = 0 if oy < 0 else 9
                    split = value.reshape(4, 2, 16, 128)
                    z[1, 0:4, y, rows, lanes] = split[:, 0]
                    z[0, 1:5, y, rows, lanes] = split[:, 1]
        for d, (ox, oy) in enumerate(EDGES):
            for rows, lanes, value in pair(lambda q: edge_src[d, q], ox, oy, 1):
                y = 0 if oy < 0 else 9
                if ox < 0:
                    z[0, 0, y, rows, lanes] = value[0]
                else:
                    z[1, 4, y, rows, lanes] = value[0]

    def exchange(number, source, last, sides, edges, rsides, redges):
        rows = 8 * (last + 1)
        for d, (ox, oy) in enumerate(SIDES):
            for s in range(4):
                if oy == 0:
                    face = source[s, edge_of(ox, last)]
                else:
                    face = source[s, :, edge_of(oy, last)]
                sides[d, s] = face.reshape(rows, 128).astype(BF16)
        for d, (ox, oy) in enumerate(EDGES):
            edges[d] = jnp.concatenate(
                [source[s, edge_of(ox, last), edge_of(oy, last)] for s in range(4)],
                axis=0,
            ).astype(BF16)
        started = []
        for k, (ox, oy) in enumerate(ALL):
            if k < 4:
                src, dst = sides.at[k], rsides.at[k]
            else:
                src, dst = edges.at[k - 4], redges.at[k - 4]
            started.append(
                pltpu.make_async_remote_copy(
                    src_ref=src,
                    dst_ref=dst,
                    send_sem=send_sem.at[number, k],
                    recv_sem=recv_sem.at[number, k],
                    device_id=device_at(-ox, -oy),
                    device_id_type=MESH,
                )
            )
        return started

    def own_sources(source, last, sides, edges):
        for d, (ox, oy) in enumerate(SIDES):
            for s in range(4):
                if oy == 0:
                    sides[d, s] = source[s, edge_of(ox, last)]
                else:
                    sides[d, s] = source[s, :, edge_of(oy, last)]
        for d, (ox, oy) in enumerate(EDGES):
            for s in range(4):
                edges[d, s, 0] = source[s, edge_of(ox, last), edge_of(oy, last)]

    def received_sources(last, sides, edges, rsides, redges):
        for d in range(4):
            for s in range(4):
                sides[d, 4 + s] = rsides[d, s].astype(F32).reshape(last + 1, 8, 128)
        for d, (ox, oy) in enumerate(EDGES):
            dx = SIDES.index((ox, 0))
            dy = SIDES.index((0, oy))
            column = redges[d].astype(F32)
            for s in range(4):
                edges[d, 4 + s, 0] = sides[dx, 4 + s, edge_of(oy, last)]
                edges[d, 8 + s, 0] = sides[dy, 4 + s, edge_of(ox, last)]
                edges[d, 12 + s, 0] = column[8 * s : 8 * s + 8]

    def fine_pair(z, wp, i):
        lhs = jnp.concatenate(
            [
                z[p % 2, i + p // 2, ky : ky + 8].reshape(256, 384)
                for ky in range(3)
                for p in range(4)
            ],
            axis=1,
        )
        rhs = jnp.concatenate(
            [wp[p, ky] for ky in range(3) for p in range(4)], axis=0
        )
        return jnp.dot(lhs, rhs, preferred_element_type=F32)

    copies[0].wait()
    for s in range(4):
        for x in range(8):
            field[s, x] = staged[s, x].astype(F32).reshape(8, 8, 128)
    sent = exchange(0, field, 7, send_side.at[0], send_edge.at[0], recv_side.at[0], recv_edge.at[0])
    pl.semaphore_wait(barrier, 8)
    for copy in sent:
        copy.start()
    own_sources(field, 7, side_src, edge_src)
    fine_centre(field, zin)
    for copy in sent:
        copy.wait_recv()
    received_sources(7, side_src, edge_src, recv_side.at[0], recv_edge.at[0])
    fine_rim(zin)
    copies[1].wait()
    copies[2].wait()

    bias1 = b1[...].reshape(1, 1, 128)

    def first(i, carry):
        acc = fine_pair(zin, w1p, i)
        for h in (0, 1):
            part = acc[:, 128 * h : 128 * h + 128].reshape(8, 4, 8, 128)
            for s in range(4):
                value = jnp.maximum(part[:, s] + bias1, 0.0) * live[s]
                hidden[s, 2 * i + h] = value.astype(BF16).astype(F32)
        return carry

    lax.fori_loop(0, 4, first, 0)
    sent_hidden = exchange(1, hidden, 7, send_side.at[1], send_edge.at[1], recv_side.at[1], recv_edge.at[1])
    for copy in sent_hidden:
        copy.start()
    own_sources(hidden, 7, side_src, edge_src)
    fine_centre(hidden, zhid)
    for copy in sent_hidden:
        copy.wait_recv()
    received_sources(7, side_src, edge_src, recv_side.at[1], recv_edge.at[1])
    fine_rim(zhid)
    copies[3].wait()
    copies[4].wait()

    bias2 = b2[...].reshape(1, 1, 128)

    def second(i, carry):
        acc = fine_pair(zhid, w2p, i)
        for s in range(4):
            summed = None
            for h in (0, 1):
                part = acc[:, 128 * h : 128 * h + 128].reshape(8, 4, 8, 128)
                value = (part[:, s] + bias2 + field[s, 2 * i + h]) * live[s]
                joined[s, 2 * i + h] = value
                summed = value if summed is None else summed + value
            rows = summed.reshape(4, 2, 8, 128)
            rows = rows[:, 0] + rows[:, 1]
            even = lax.broadcasted_iota(jnp.int32, rows.shape, 1) % 2 == 0
            other = jnp.where(even, pltpu.roll(rows, 7, 1), pltpu.roll(rows, 1, 1))
            mean = (rows + other) * 0.125
            coarse_field[s, i] = mean.astype(BF16).astype(F32)
        return carry

    lax.fori_loop(0, 4, second, 0)
    sent_coarse = exchange(2, coarse_field, 3, csend_side, csend_edge, crecv_side, crecv_edge)
    for copy in sent_coarse:
        copy.start()
    own_sources(coarse_field, 3, cside_src, cedge_src)
    for x in range(4):
        for rows, lanes, value in pair(lambda q: coarse_field[q, x], 0, 0, 2):
            zc[x + 1, 1:5, rows, lanes] = value
    for copy in sent_coarse:
        copy.wait_recv()
    received_sources(3, cside_src, cedge_src, crecv_side, crecv_edge)
    for d, (ox, oy) in enumerate(SIDES):
        for rows, lanes, value in pair(lambda q: cside_src[d, q], ox, oy, 2):
            if oy == 0:
                zc[0 if ox < 0 else 5, 1:5, rows, lanes] = value
            else:
                zc[1:5, 0 if oy < 0 else 5, rows, lanes] = value
    for d, (ox, oy) in enumerate(EDGES):
        for rows, lanes, value in pair(lambda q: cedge_src[d, q], ox, oy, 2):
            zc[0 if ox < 0 else 5, 0 if oy < 0 else 5, rows, lanes] = value[0]

    copies[5].wait()
    copies[6].wait()
    bias = bc[...]

    def last(x, carry):
        lhs = jnp.concatenate(
            [
                zc[x + kx, ky : ky + 4].reshape(128, 384)
                for kx in range(3)
                for ky in range(3)
            ],
            axis=1,
        )
        acc = jnp.dot(lhs, wcv[...], preferred_element_type=F32)
        acc = jnp.maximum(acc + bias, 0.0).reshape(4, 4, 8, 256)
        acc = jnp.concatenate(
            [(acc[:, s] * live[s])[:, None] for s in range(4)], axis=1
        )
        lifted = jnp.dot(
            acc.reshape(128, 256).astype(BF16), wlv[...], preferred_element_type=F32
        ).reshape(4, 1, 4, 8, 128)
        for s in range(4):
            raised = jnp.broadcast_to(lifted[:, :, s], (4, 2, 8, 128)).reshape(8, 8, 128)
            for h in (0, 1):
                joined[s, 2 * x + h] = (joined[s, 2 * x + h] + raised) * live[s]
        return carry

    lax.fori_loop(0, 4, last, 0)
    done = pltpu.make_async_copy(joined, out, out_sem)
    done.start()
    for copy in sent + sent_hidden + sent_coarse:
        copy.wait_send()
    done.wait()


def local(gx, gy, features, slot_cell, neighbours, w1, b1, w2, b2, wc, bc, wl):
    smem = pl.BlockSpec(memory_space=pltpu.SMEM)
    vmem = pl.BlockSpec(memory_space=pltpu.VMEM)
    hbm = pl.BlockSpec(memory_space=pl.ANY)
    result = pl.pallas_call(
        functools.partial(kernel, gx, gy),
        out_shape=jax.ShapeDtypeStruct((4, 8, 8, 8, 128), F32),
        in_specs=[smem, smem, hbm, hbm, vmem, hbm, vmem, hbm, vmem, hbm],
        out_specs=hbm,
        scratch_shapes=[
            pltpu.VMEM((4, 8, 64, 128), BF16),
            pltpu.VMEM((5, 8, 8, 8, 128), F32),
            pltpu.VMEM((5, 8, 8, 8, 128), F32),
            pltpu.VMEM((5, 4, 4, 8, 128), F32),
            pltpu.VMEM((4, 9, 8, 8, 128), F32),
            pltpu.VMEM((4, 17, 1, 8, 128), F32),
            pltpu.VMEM((4, 9, 4, 8, 128), F32),
            pltpu.VMEM((4, 17, 1, 8, 128), F32),
            pltpu.VMEM((2, 5, 10, 32, 384), BF16),
            pltpu.VMEM((2, 5, 10, 32, 384), BF16),
            pltpu.VMEM((6, 6, 32, 384), BF16),
            pltpu.VMEM((4, 3, 384, 256), BF16),
            pltpu.VMEM((4, 3, 384, 256), BF16),
            pltpu.VMEM((3456, 256), BF16),
            pltpu.VMEM((256, 128), BF16),
            pltpu.VMEM((4, 8, 8, 8, 128), F32),
            pltpu.VMEM((2, 4, 4, 64, 128), BF16),
            pltpu.VMEM((2, 4, 32, 128), BF16),
            pltpu.VMEM((2, 4, 4, 64, 128), BF16),
            pltpu.VMEM((2, 4, 32, 128), BF16),
            pltpu.VMEM((4, 4, 32, 128), BF16),
            pltpu.VMEM((4, 32, 128), BF16),
            pltpu.VMEM((4, 4, 32, 128), BF16),
            pltpu.VMEM((4, 32, 128), BF16),
            pltpu.SemaphoreType.DMA((7,)),
            pltpu.SemaphoreType.DMA,
            pltpu.SemaphoreType.DMA((3, 8)),
            pltpu.SemaphoreType.DMA((3, 8)),
        ],
        compiler_params=pltpu.CompilerParams(
            collective_id=0, has_side_effects=True, vmem_limit_bytes=48 * 2**20
        ),
        cost_estimate=pl.CostEstimate(
            flops=8_000_000_000, bytes_accessed=8_000_000, transcendentals=0
        ),
        name="unet_window",
    )(
        slot_cell.reshape(4),
        neighbours.reshape(4, 26),
        features.reshape(4, 8, 64, 128),
        w1.reshape(3, 3, 384, 128),
        b1.reshape(1, 128),
        w2.reshape(3, 3, 384, 128),
        b2.reshape(1, 128),
        wc.reshape(3456, 256),
        bc.reshape(1, 256),
        wl,
    )
    return result.reshape(1, 1, 4, 512, 128)


def solution(mesh):
    placed = (
        P("gx", "gy", None, None, None),
        P("gx", "gy", None),
        P("gx", "gy", None, None),
    ) + (P(),) * 7
    return jax.shard_map(
        functools.partial(local, mesh.shape["gx"], mesh.shape["gy"]),
        mesh=mesh,
        in_specs=placed,
        out_specs=P("gx", "gy", None, None, None),
        check_vma=False,
    )
```

```python
import functools

import jax
import jax.numpy as jnp
from jax import lax
from jax.experimental import pallas as pl
from jax.experimental.pallas import tpu as pltpu
from jax.sharding import PartitionSpec as P

MESH = pl.DeviceIdType.MESH
F32 = jnp.float32
BF16 = jnp.bfloat16

OFFSETS = [
    (ox, oy, oz)
    for ox in (-1, 0, 1)
    for oy in (-1, 0, 1)
    for oz in (-1, 0, 1)
    if (ox, oy, oz) != (0, 0, 0)
]
NUMBER = {offset: k for k, offset in enumerate(OFFSETS)}
SIDES = [(-1, 0), (1, 0), (0, -1), (0, 1)]
EDGES = [(-1, -1), (-1, 1), (1, -1), (1, 1)]
ALL = SIDES + EDGES


def edge_of(step, last):
    return last if step < 0 else 0


def kernel(
    gx,
    gy,
    cell_hbm,
    nbr_hbm,
    feat,
    w1,
    b1_hbm,
    w2,
    b2_hbm,
    wc,
    bc_hbm,
    wl,
    out,
    cell,
    nbr,
    b1,
    b2,
    bc,
    staged,
    field,
    hidden,
    coarse_field,
    side_src,
    edge_src,
    cside_src,
    cedge_src,
    zin,
    zhid,
    zx,
    zy,
    zc,
    w1p,
    w2p,
    wcv,
    wlv,
    total,
    send_side,
    send_edge,
    recv_side,
    recv_edge,
    csend_side,
    csend_edge,
    crecv_side,
    crecv_edge,
    local_sem,
    send_sem,
    recv_sem,
):
    mx = lax.axis_index("gx")
    my = lax.axis_index("gy")

    def device_at(ox, oy):
        return (lax.rem(mx + ox + gx, gx), lax.rem(my + oy + gy, gy))

    barrier = pltpu.get_barrier_semaphore()
    for ox, oy in ALL:
        pl.semaphore_signal(
            barrier, inc=1, device_id=device_at(ox, oy), device_id_type=MESH
        )

    pairs = [
        (feat, staged),
        (cell_hbm, cell),
        (nbr_hbm, nbr),
        (b1_hbm, b1),
        (w1, w1p.at[0:3, :, :, 0:128]),
        (w1, w1p.at[1:4, :, :, 128:256]),
        (w2, w2p.at[0:3, :, :, 0:128]),
        (w2, w2p.at[1:4, :, :, 128:256]),
        (b2_hbm, b2),
        (wc, wcv),
        (wl, wlv),
        (bc_hbm, bc),
    ]
    copies = [
        pltpu.make_async_copy(src, dst, local_sem.at[k])
        for k, (src, dst) in enumerate(pairs)
    ]
    for copy in copies:
        copy.start()

    for wp in (w1p, w2p):
        wp[3, :, :, 0:128] = jnp.zeros((3, 384, 128), BF16)
        wp[0, :, :, 128:256] = jnp.zeros((3, 384, 128), BF16)
    field[4] = jnp.zeros((4, 2, 8, 8, 128), F32)
    hidden[4] = jnp.zeros((4, 2, 8, 8, 128), F32)
    coarse_field[4] = jnp.zeros((4, 4, 8, 128), F32)
    for d in range(4):
        side_src[d, 8] = jnp.zeros((8, 8, 128), F32)
        cside_src[d, 8] = jnp.zeros((4, 8, 128), F32)
        edge_src[d, 16] = jnp.zeros((1, 8, 128), F32)
        cedge_src[d, 16] = jnp.zeros((1, 8, 128), F32)
    for z in (zin, zhid):
        z[:, :, 0] = jnp.zeros((2, 4, 32, 384), BF16)
        z[:, :, 9] = jnp.zeros((2, 4, 32, 384), BF16)
    zy[:, 0, 0] = jnp.zeros((2, 32, 384), BF16)
    zy[:, 1, 4] = jnp.zeros((2, 32, 384), BF16)

    copies[0].wait()
    for s in range(4):
        for x in range(8):
            field[s, x // 2, x % 2] = staged[s, x].astype(F32).reshape(8, 8, 128)

    def plane(source, s, x):
        if source is coarse_field:
            return source[s, x]
        return source[s, x // 2, x % 2]

    def across(source, s, y):
        if source is coarse_field:
            return source[s, :, y]
        return source[s, :, :, y].reshape(8, 8, 128)

    def column(source, s, x, y):
        if source is coarse_field:
            return source[s, x, y]
        return source[s, x // 2, x % 2, y]

    def exchange(number, source, last, sides, edges, rsides, redges):
        rows = 8 * (last + 1)
        for d, (ox, oy) in enumerate(SIDES):
            if number == 0 and oy == 0:
                continue
            for s in range(4):
                if oy == 0:
                    face = plane(source, s, edge_of(ox, last))
                else:
                    face = across(source, s, edge_of(oy, last))
                sides[d, s] = face.reshape(rows, 128).astype(BF16)
        for d, (ox, oy) in enumerate(EDGES):
            edges[d] = jnp.concatenate(
                [
                    column(source, s, edge_of(ox, last), edge_of(oy, last))
                    for s in range(4)
                ],
                axis=0,
            ).astype(BF16)
        described = []
        for k, (ox, oy) in enumerate(ALL):
            if k < 4:
                src, dst = sides.at[k], rsides.at[k]
                if number == 0 and oy == 0:
                    src = feat.at[:, edge_of(ox, last)]
            else:
                src, dst = edges.at[k - 4], redges.at[k - 4]
            described.append(
                pltpu.make_async_remote_copy(
                    src_ref=src,
                    dst_ref=dst,
                    send_sem=send_sem.at[number, k],
                    recv_sem=recv_sem.at[number, k],
                    device_id=device_at(-ox, -oy),
                    device_id_type=MESH,
                )
            )
        return described

    sent = exchange(
        0, field, 7, send_side.at[0], send_edge.at[0], recv_side.at[0], recv_edge.at[0]
    )
    pl.semaphore_wait(barrier, 8)
    for copy in sent:
        copy.start()

    for k in (1, 2, 3):
        copies[k].wait()
    live = [jnp.where(cell[s] >= 0, 1.0, 0.0).astype(F32) for s in range(4)]

    def index(s, ox, oy, oz):
        if (ox, oy, oz) == (0, 0, 0):
            return s
        entry = nbr[s, NUMBER[ox, oy, oz]]
        safe = jnp.maximum(entry, 0)
        block = lax.shift_right_logical(safe, 2)
        slot = lax.bitwise_and(safe, 3)
        if (ox, oy) == (0, 0):
            return jnp.where(entry < 0, 4, slot)
        if ox == 0 or oy == 0:
            place = slot + jnp.where(block == 4, 0, 4)
            return jnp.where(entry < 0, 8, place)
        beside_x = (ox + 1) * 3 + 1
        beside_y = 3 + (oy + 1)
        place = slot + jnp.where(
            block == 4,
            0,
            jnp.where(block == beside_x, 4, jnp.where(block == beside_y, 8, 12)),
        )
        return jnp.where(entry < 0, 16, place)

    where = {
        (s, ox, oy, oz): index(s, ox, oy, oz)
        for s in range(4)
        for ox in (-1, 0, 1)
        for oy in (-1, 0, 1)
        for oz in (-1, 0, 1)
    }

    def shifted(low, own, high, step):
        row = lax.broadcasted_iota(jnp.int32, own.shape, own.ndim - 2)
        axis = own.ndim - 2
        down = pltpu.roll(jnp.where(row >= 8 - step, low, own), step, axis)
        up = pltpu.roll(jnp.where(row < step, high, own), 8 - step, axis)
        return down, own, up

    def pair(fetch, ox, oy, step):
        for half in (0, 1):
            parts = [
                shifted(*[fetch(where[s, ox, oy, oz]) for oz in (-1, 0, 1)], step)
                for s in (2 * half, 2 * half + 1)
            ]
            for kz in range(3):
                both = jnp.concatenate([parts[0][kz], parts[1][kz]], axis=-2)
                yield slice(16 * half, 16 * half + 16), slice(
                    128 * kz, 128 * kz + 128
                ), both.astype(BF16)

    def fine_centre(source, z):
        def body(m, carry):
            for h in (0, 1):
                for rows, lanes, value in pair(lambda q: source[q, m, h], 0, 0, 1):
                    z[h, m, 1:9, rows, lanes] = value
            return carry

        lax.fori_loop(0, 4, body, 0)

    def fine_rim():
        for d, (ox, oy) in enumerate(SIDES):
            for rows, lanes, value in pair(lambda q: side_src[d, q], ox, oy, 1):
                if oy == 0:
                    zx[d, 1:9, rows, lanes] = value
                else:
                    split = value.reshape(4, 2, 16, 128)
                    zy[d - 2, 1, 0:4, rows, lanes] = split[:, 0]
                    zy[d - 2, 0, 1:5, rows, lanes] = split[:, 1]
        for d, (ox, oy) in enumerate(EDGES):
            for rows, lanes, value in pair(lambda q: edge_src[d, q], ox, oy, 1):
                zx[0 if ox < 0 else 1, 0 if oy < 0 else 9, rows, lanes] = value[0]

    def own_sources(source, last, sides, edges):
        for d, (ox, oy) in enumerate(SIDES):
            for s in range(4):
                if oy == 0:
                    sides[d, s] = plane(source, s, edge_of(ox, last))
                else:
                    sides[d, s] = across(source, s, edge_of(oy, last))
        for d, (ox, oy) in enumerate(EDGES):
            for s in range(4):
                edges[d, s, 0] = column(
                    source, s, edge_of(ox, last), edge_of(oy, last)
                )

    def received_sources(last, sides, edges, rsides, redges):
        for d in range(4):
            for s in range(4):
                sides[d, 4 + s] = rsides[d, s].astype(F32).reshape(last + 1, 8, 128)
        for d, (ox, oy) in enumerate(EDGES):
            dx = SIDES.index((ox, 0))
            dy = SIDES.index((0, oy))
            far = redges[d].astype(F32)
            for s in range(4):
                edges[d, 4 + s, 0] = sides[dx, 4 + s, edge_of(oy, last)]
                edges[d, 8 + s, 0] = sides[dy, 4 + s, edge_of(ox, last)]
                edges[d, 12 + s, 0] = far[8 * s : 8 * s + 8]

    def centre_conv(z, wp, i):
        planes = [(1, i - 1), (0, i), (1, i), (0, i + 1)]
        used = [p for p in range(4) if 0 <= planes[p][1] < 4]
        lhs = jnp.concatenate(
            [
                z[planes[p][0], planes[p][1], ky : ky + 8].reshape(256, 384)
                for ky in range(3)
                for p in used
            ],
            axis=1,
        )
        rhs = jnp.concatenate([wp[p, ky] for ky in range(3) for p in used], axis=0)
        return jnp.dot(lhs, rhs, preferred_element_type=F32)

    def convolve(z, wp, finish):
        for i in range(4):
            acc = centre_conv(z, wp, i)
            for h in (0, 1):
                part = acc[:, 128 * h : 128 * h + 128].reshape(8, 32, 128)
                total[i, h] = part
                if 0 < 2 * i + h < 7:
                    inner = part[1:7].reshape(6, 4, 8, 128)
                    for s in range(4):
                        finish(s, (i, h, slice(1, 7)), inner[:, s])

    def add_rim(wp, finish):
        for d in (0, 1):
            y, ky = (0, 0) if d == 0 else (7, 2)
            lhs = jnp.concatenate(
                [
                    zy[d, p % 2, p // 2 : p // 2 + 4].reshape(128, 384)
                    for p in range(4)
                ],
                axis=1,
            )
            rhs = jnp.concatenate([wp[p, ky] for p in range(4)], axis=0)
            add = jnp.dot(lhs, rhs, preferred_element_type=F32)
            for h in (0, 1):
                part = add[:, 128 * h : 128 * h + 128].reshape(4, 32, 128)
                part = total[:, h, y] + part
                if h == 0:
                    total[0, h, y] = part[0]
                else:
                    total[3, h, y] = part[3]
                inner = part.reshape(4, 4, 8, 128)
                for s in range(4):
                    finish(s, (slice(0, 4), h, y), inner[:, s])
        for d in (0, 1):
            i, h, p = (0, 0, 0) if d == 0 else (3, 1, 3)
            lhs = jnp.concatenate(
                [zx[d, ky : ky + 8].reshape(256, 384) for ky in range(3)], axis=1
            )
            rhs = jnp.concatenate(
                [wp[p, ky][:, 128 * h : 128 * h + 128] for ky in range(3)], axis=0
            )
            add = jnp.dot(lhs, rhs, preferred_element_type=F32).reshape(8, 32, 128)
            part = (total[i, h] + add).reshape(8, 4, 8, 128)
            for s in range(4):
                finish(s, (i, h, slice(0, 8)), part[:, s])

    own_sources(field, 7, side_src, edge_src)
    fine_centre(field, zin)

    copies[4].wait()
    copies[5].wait()

    def to_hidden(s, at, value):
        value = jnp.maximum(value + b1[...].reshape(1, 1, 128), 0.0) * live[s]
        hidden[(s,) + at] = value.astype(BF16).astype(F32)

    convolve(zin, w1p, to_hidden)
    for copy in sent:
        copy.wait_recv()
    received_sources(7, side_src, edge_src, recv_side.at[0], recv_edge.at[0])
    fine_rim()
    add_rim(w1p, to_hidden)
    sent_hidden = exchange(
        1, hidden, 7, send_side.at[1], send_edge.at[1], recv_side.at[1], recv_edge.at[1]
    )
    for copy in sent_hidden:
        copy.start()
    own_sources(hidden, 7, side_src, edge_src)
    fine_centre(hidden, zhid)

    for k in (6, 7, 8):
        copies[k].wait()

    def to_fine(s, at, value):
        value = value + b2[...].reshape(1, 1, 128) + field[(s,) + at]
        out[(s,) + at] = value * live[s]

    convolve(zhid, w2p, to_fine)
    for copy in sent_hidden:
        copy.wait_recv()
    received_sources(7, side_src, edge_src, recv_side.at[1], recv_edge.at[1])
    fine_rim()
    add_rim(w2p, to_fine)

    for s in range(4):
        for i in range(4):
            rows = (out[s, i, 0] + out[s, i, 1]).reshape(4, 2, 8, 128)
            rows = rows[:, 0] + rows[:, 1]
            even = lax.broadcasted_iota(jnp.int32, rows.shape, 1) % 2 == 0
            other = jnp.where(even, pltpu.roll(rows, 7, 1), pltpu.roll(rows, 1, 1))
            mean = (rows + other) * 0.125
            coarse_field[s, i] = mean.astype(BF16).astype(F32)
    sent_coarse = exchange(
        2, coarse_field, 3, csend_side, csend_edge, crecv_side, crecv_edge
    )
    for copy in sent_coarse:
        copy.start()
    own_sources(coarse_field, 3, cside_src, cedge_src)
    for x in range(4):
        for rows, lanes, value in pair(lambda q: coarse_field[q, x], 0, 0, 2):
            zc[x + 1, 1:5, rows, lanes] = value
    for k in (9, 10, 11):
        copies[k].wait()
    for copy in sent_coarse:
        copy.wait_recv()
    received_sources(3, cside_src, cedge_src, crecv_side, crecv_edge)
    for d, (ox, oy) in enumerate(SIDES):
        for rows, lanes, value in pair(lambda q: cside_src[d, q], ox, oy, 2):
            if oy == 0:
                zc[0 if ox < 0 else 5, 1:5, rows, lanes] = value
            else:
                zc[1:5, 0 if oy < 0 else 5, rows, lanes] = value
    for d, (ox, oy) in enumerate(EDGES):
        for rows, lanes, value in pair(lambda q: cedge_src[d, q], ox, oy, 2):
            zc[0 if ox < 0 else 5, 0 if oy < 0 else 5, rows, lanes] = value[0]

    lhs = jnp.concatenate(
        [
            zc[kx : kx + 4, ky : ky + 4].reshape(512, 384)
            for kx in range(3)
            for ky in range(3)
        ],
        axis=1,
    )
    acc = jnp.dot(lhs, wcv[...], preferred_element_type=F32)
    acc = jnp.maximum(acc + bc[...], 0.0).reshape(16, 4, 8, 256)
    acc = jnp.concatenate([(acc[:, s] * live[s])[:, None] for s in range(4)], axis=1)
    lifted = jnp.dot(
        acc.reshape(512, 256).astype(BF16), wlv[...], preferred_element_type=F32
    ).reshape(4, 4, 1, 4, 8, 128)
    for s in range(4):
        for x in range(4):
            raised = jnp.broadcast_to(lifted[x, :, :, s], (4, 2, 8, 128))
            raised = raised.reshape(8, 8, 128)
            for h in (0, 1):
                out[s, x, h] = (out[s, x, h] + raised) * live[s]
    for copy in sent + sent_hidden + sent_coarse:
        copy.wait_send()


def local(gx, gy, features, slot_cell, neighbours, w1, b1, w2, b2, wc, bc, wl):
    operands = [
        pltpu.with_memory_space_constraint(operand, pltpu.HBM)
        for operand in (
            slot_cell.reshape(4),
            neighbours.reshape(4, 26),
            features.reshape(4, 8, 64, 128),
            w1.reshape(3, 3, 384, 128),
            b1.reshape(1, 128),
            w2.reshape(3, 3, 384, 128),
            b2.reshape(1, 128),
            wc.reshape(3456, 256),
            bc.reshape(1, 256),
            wl,
        )
    ]
    result = pl.pallas_call(
        functools.partial(kernel, gx, gy),
        out_shape=jax.ShapeDtypeStruct((4, 4, 2, 8, 8, 128), F32),
        in_specs=[pl.BlockSpec(memory_space=pl.ANY)] * 10,
        out_specs=pl.BlockSpec(memory_space=pltpu.VMEM),
        scratch_shapes=[
            pltpu.SMEM((4,), jnp.int32),
            pltpu.SMEM((4, 26), jnp.int32),
            pltpu.VMEM((1, 128), F32),
            pltpu.VMEM((1, 128), F32),
            pltpu.VMEM((1, 256), F32),
            pltpu.VMEM((4, 8, 64, 128), BF16),
            pltpu.VMEM((5, 4, 2, 8, 8, 128), F32),
            pltpu.VMEM((5, 4, 2, 8, 8, 128), F32),
            pltpu.VMEM((5, 4, 4, 8, 128), F32),
            pltpu.VMEM((4, 9, 8, 8, 128), F32),
            pltpu.VMEM((4, 17, 1, 8, 128), F32),
            pltpu.VMEM((4, 9, 4, 8, 128), F32),
            pltpu.VMEM((4, 17, 1, 8, 128), F32),
            pltpu.VMEM((2, 4, 10, 32, 384), BF16),
            pltpu.VMEM((2, 4, 10, 32, 384), BF16),
            pltpu.VMEM((2, 10, 32, 384), BF16),
            pltpu.VMEM((2, 2, 5, 32, 384), BF16),
            pltpu.VMEM((6, 6, 32, 384), BF16),
            pltpu.VMEM((4, 3, 384, 256), BF16),
            pltpu.VMEM((4, 3, 384, 256), BF16),
            pltpu.VMEM((3456, 256), BF16),
            pltpu.VMEM((256, 128), BF16),
            pltpu.VMEM((4, 2, 8, 32, 128), F32),
            pltpu.VMEM((2, 4, 4, 64, 128), BF16),
            pltpu.VMEM((2, 4, 32, 128), BF16),
            pltpu.VMEM((2, 4, 4, 64, 128), BF16),
            pltpu.VMEM((2, 4, 32, 128), BF16),
            pltpu.VMEM((4, 4, 32, 128), BF16),
            pltpu.VMEM((4, 32, 128), BF16),
            pltpu.VMEM((4, 4, 32, 128), BF16),
            pltpu.VMEM((4, 32, 128), BF16),
            pltpu.SemaphoreType.DMA((12,)),
            pltpu.SemaphoreType.DMA((3, 8)),
            pltpu.SemaphoreType.DMA((3, 8)),
        ],
        compiler_params=pltpu.CompilerParams(
            collective_id=0, has_side_effects=True, vmem_limit_bytes=48 * 2**20
        ),
        cost_estimate=pl.CostEstimate(
            flops=8_000_000_000, bytes_accessed=8_000_000, transcendentals=0
        ),
        name="unet_window",
    )(*operands)
    return result.reshape(1, 1, 4, 512, 128)


def solution(mesh):
    placed = (
        P("gx", "gy", None, None, None),
        P("gx", "gy", None),
        P("gx", "gy", None, None),
    ) + (P(),) * 7
    return jax.shard_map(
        functools.partial(local, mesh.shape["gx"], mesh.shape["gy"]),
        mesh=mesh,
        in_specs=placed,
        out_specs=P("gx", "gy", None, None, None),
        check_vma=False,
    )
```

```python
import functools

import jax
import jax.numpy as jnp
from jax import lax
from jax.experimental import pallas as pl
from jax.experimental.pallas import tpu as pltpu
from jax.sharding import PartitionSpec as P

MESH = pl.DeviceIdType.MESH
F32 = jnp.float32
BF16 = jnp.bfloat16

OFFSETS = [
    (ox, oy, oz)
    for ox in (-1, 0, 1)
    for oy in (-1, 0, 1)
    for oz in (-1, 0, 1)
    if (ox, oy, oz) != (0, 0, 0)
]
NUMBER = {offset: k for k, offset in enumerate(OFFSETS)}
SIDES = [(-1, 0), (1, 0), (0, -1), (0, 1)]
EDGES = [(-1, -1), (-1, 1), (1, -1), (1, 1)]
ALL = SIDES + EDGES


def edge_of(step, last):
    return last if step < 0 else 0


def kernel(
    gx,
    gy,
    cell_hbm,
    nbr_hbm,
    feat,
    w1,
    b1_hbm,
    w2,
    b2_hbm,
    wc,
    bc_hbm,
    wl,
    out,
    cell,
    nbr,
    b1,
    b2,
    bc,
    staged,
    field,
    hidden,
    coarse_field,
    side_src,
    edge_src,
    cside_src,
    cedge_src,
    zin,
    zhid,
    zx,
    zy,
    zc,
    w1p,
    w2p,
    wcv,
    wlv,
    total,
    send_side,
    send_edge,
    recv_side,
    recv_edge,
    csend_side,
    csend_edge,
    crecv_side,
    crecv_edge,
    local_sem,
    send_sem,
    recv_sem,
):
    mx = lax.axis_index("gx")
    my = lax.axis_index("gy")

    def device_at(ox, oy):
        return (lax.rem(mx + ox + gx, gx), lax.rem(my + oy + gy, gy))

    barrier = pltpu.get_barrier_semaphore()
    for ox, oy in ALL:
        pl.semaphore_signal(
            barrier, inc=1, device_id=device_at(ox, oy), device_id_type=MESH
        )

    pairs = [
        (feat, staged),
        (cell_hbm, cell),
        (nbr_hbm, nbr),
        (b1_hbm, b1),
        (w1, w1p.at[0:3, :, :, 0:128]),
        (w1, w1p.at[1:4, :, :, 128:256]),
        (w2, w2p.at[0:3, :, :, 0:128]),
        (w2, w2p.at[1:4, :, :, 128:256]),
        (b2_hbm, b2),
        (wc, wcv),
        (wl, wlv),
        (bc_hbm, bc),
    ]
    copies = [
        pltpu.make_async_copy(src, dst, local_sem.at[k])
        for k, (src, dst) in enumerate(pairs)
    ]
    for copy in copies[:6]:
        copy.start()

    for wp in (w1p, w2p):
        wp[3, :, :, 0:128] = jnp.zeros((3, 384, 128), BF16)
        wp[0, :, :, 128:256] = jnp.zeros((3, 384, 128), BF16)
    field[4] = jnp.zeros((4, 2, 8, 8, 128), F32)
    hidden[4] = jnp.zeros((4, 2, 8, 8, 128), F32)
    coarse_field[4] = jnp.zeros((4, 4, 8, 128), F32)
    for d in range(4):
        side_src[d, 8] = jnp.zeros((8, 8, 128), F32)
        cside_src[d, 8] = jnp.zeros((4, 8, 128), F32)
        edge_src[d, 16] = jnp.zeros((1, 8, 128), F32)
        cedge_src[d, 16] = jnp.zeros((1, 8, 128), F32)
    for z in (zin, zhid):
        z[:, :, 0] = jnp.zeros((2, 4, 32, 384), BF16)
        z[:, :, 9] = jnp.zeros((2, 4, 32, 384), BF16)
    zy[:, 0, 0] = jnp.zeros((2, 32, 384), BF16)
    zy[:, 1, 4] = jnp.zeros((2, 32, 384), BF16)

    copies[0].wait()
    for s in range(4):
        for x in range(8):
            field[s, x // 2, x % 2] = staged[s, x].astype(F32).reshape(8, 8, 128)

    def plane(source, s, x):
        if source is coarse_field:
            return source[s, x]
        return source[s, x // 2, x % 2]

    def across(source, s, y):
        if source is coarse_field:
            return source[s, :, y]
        return source[s, :, :, y].reshape(8, 8, 128)

    def column(source, s, x, y):
        if source is coarse_field:
            return source[s, x, y]
        return source[s, x // 2, x % 2, y]

    def exchange(number, source, last, sides, edges, rsides, redges):
        rows = 8 * (last + 1)
        for d, (ox, oy) in enumerate(SIDES):
            if number == 0 and oy == 0:
                continue
            for s in range(4):
                if oy == 0:
                    face = plane(source, s, edge_of(ox, last))
                else:
                    face = across(source, s, edge_of(oy, last))
                sides[d, s] = face.reshape(rows, 128).astype(BF16)
        for d, (ox, oy) in enumerate(EDGES):
            edges[d] = jnp.concatenate(
                [
                    column(source, s, edge_of(ox, last), edge_of(oy, last))
                    for s in range(4)
                ],
                axis=0,
            ).astype(BF16)
        described = []
        for k in (4, 5, 6, 7, 2, 3, 0, 1):
            ox, oy = ALL[k]
            if k < 4:
                src, dst = sides.at[k], rsides.at[k]
                if number == 0 and oy == 0:
                    src = feat.at[:, edge_of(ox, last)]
            else:
                src, dst = edges.at[k - 4], redges.at[k - 4]
            described.append(
                pltpu.make_async_remote_copy(
                    src_ref=src,
                    dst_ref=dst,
                    send_sem=send_sem.at[number, k],
                    recv_sem=recv_sem.at[number, k],
                    device_id=device_at(-ox, -oy),
                    device_id_type=MESH,
                )
            )
        return described

    sent = exchange(
        0, field, 7, send_side.at[0], send_edge.at[0], recv_side.at[0], recv_edge.at[0]
    )
    pl.semaphore_wait(barrier, 8)
    for copy in sent:
        copy.start()

    for k in (1, 2, 3):
        copies[k].wait()
    live = [jnp.where(cell[s] >= 0, 1.0, 0.0).astype(F32) for s in range(4)]

    def index(s, ox, oy, oz):
        if (ox, oy, oz) == (0, 0, 0):
            return s
        entry = nbr[s, NUMBER[ox, oy, oz]]
        safe = jnp.maximum(entry, 0)
        block = lax.shift_right_logical(safe, 2)
        slot = lax.bitwise_and(safe, 3)
        if (ox, oy) == (0, 0):
            return jnp.where(entry < 0, 4, slot)
        if ox == 0 or oy == 0:
            place = slot + jnp.where(block == 4, 0, 4)
            return jnp.where(entry < 0, 8, place)
        beside_x = (ox + 1) * 3 + 1
        beside_y = 3 + (oy + 1)
        place = slot + jnp.where(
            block == 4,
            0,
            jnp.where(block == beside_x, 4, jnp.where(block == beside_y, 8, 12)),
        )
        return jnp.where(entry < 0, 16, place)

    where = {
        (s, ox, oy, oz): index(s, ox, oy, oz)
        for s in range(4)
        for ox in (-1, 0, 1)
        for oy in (-1, 0, 1)
        for oz in (-1, 0, 1)
    }

    def shifted(low, own, high, step):
        row = lax.broadcasted_iota(jnp.int32, own.shape, own.ndim - 2)
        axis = own.ndim - 2
        down = pltpu.roll(jnp.where(row >= 8 - step, low, own), step, axis)
        up = pltpu.roll(jnp.where(row < step, high, own), 8 - step, axis)
        return down, own, up

    def pair(fetch, ox, oy, step):
        for half in (0, 1):
            parts = [
                shifted(*[fetch(where[s, ox, oy, oz]) for oz in (-1, 0, 1)], step)
                for s in (2 * half, 2 * half + 1)
            ]
            for kz in range(3):
                both = jnp.concatenate([parts[0][kz], parts[1][kz]], axis=-2)
                yield slice(16 * half, 16 * half + 16), slice(
                    128 * kz, 128 * kz + 128
                ), both.astype(BF16)

    def fine_centre(source, z):
        def body(m, carry):
            for h in (0, 1):
                for rows, lanes, value in pair(lambda q: source[q, m, h], 0, 0, 1):
                    z[h, m, 1:9, rows, lanes] = value
            return carry

        lax.fori_loop(0, 4, body, 0)

    def fine_rim():
        for d, (ox, oy) in enumerate(SIDES):
            for rows, lanes, value in pair(lambda q: side_src[d, q], ox, oy, 1):
                if oy == 0:
                    zx[d, 1:9, rows, lanes] = value
                else:
                    split = value.reshape(4, 2, 16, 128)
                    zy[d - 2, 1, 0:4, rows, lanes] = split[:, 0]
                    zy[d - 2, 0, 1:5, rows, lanes] = split[:, 1]
        for d, (ox, oy) in enumerate(EDGES):
            for rows, lanes, value in pair(lambda q: edge_src[d, q], ox, oy, 1):
                zx[0 if ox < 0 else 1, 0 if oy < 0 else 9, rows, lanes] = value[0]

    def own_sources(source, last, sides, edges):
        for d, (ox, oy) in enumerate(SIDES):
            for s in range(4):
                if oy == 0:
                    sides[d, s] = plane(source, s, edge_of(ox, last))
                else:
                    sides[d, s] = across(source, s, edge_of(oy, last))
        for d, (ox, oy) in enumerate(EDGES):
            for s in range(4):
                edges[d, s, 0] = column(
                    source, s, edge_of(ox, last), edge_of(oy, last)
                )

    def received_sources(last, sides, edges, rsides, redges):
        for d in range(4):
            for s in range(4):
                sides[d, 4 + s] = rsides[d, s].astype(F32).reshape(last + 1, 8, 128)
        for d, (ox, oy) in enumerate(EDGES):
            dx = SIDES.index((ox, 0))
            dy = SIDES.index((0, oy))
            far = redges[d].astype(F32)
            for s in range(4):
                edges[d, 4 + s, 0] = sides[dx, 4 + s, edge_of(oy, last)]
                edges[d, 8 + s, 0] = sides[dy, 4 + s, edge_of(ox, last)]
                edges[d, 12 + s, 0] = far[8 * s : 8 * s + 8]

    def centre_conv(z, wp, i):
        planes = [(1, i - 1), (0, i), (1, i), (0, i + 1)]
        used = [p for p in range(4) if 0 <= planes[p][1] < 4]
        lhs = jnp.concatenate(
            [
                z[planes[p][0], planes[p][1], ky : ky + 8].reshape(256, 384)
                for ky in range(3)
                for p in used
            ],
            axis=1,
        )
        rhs = jnp.concatenate([wp[p, ky] for ky in range(3) for p in used], axis=0)
        return jnp.dot(lhs, rhs, preferred_element_type=F32)

    def convolve(z, wp, finish):
        for i in range(4):
            acc = centre_conv(z, wp, i)
            for h in (0, 1):
                part = acc[:, 128 * h : 128 * h + 128].reshape(8, 32, 128)
                total[i, h] = part
                if 0 < 2 * i + h < 7:
                    inner = part[1:7].reshape(6, 4, 8, 128)
                    for s in range(4):
                        finish(s, (i, h, slice(1, 7)), inner[:, s])

    def add_rim(wp, finish):
        for d in (0, 1):
            y, ky = (0, 0) if d == 0 else (7, 2)
            lhs = jnp.concatenate(
                [
                    zy[d, p % 2, p // 2 : p // 2 + 4].reshape(128, 384)
                    for p in range(4)
                ],
                axis=1,
            )
            rhs = jnp.concatenate([wp[p, ky] for p in range(4)], axis=0)
            add = jnp.dot(lhs, rhs, preferred_element_type=F32)
            for h in (0, 1):
                part = add[:, 128 * h : 128 * h + 128].reshape(4, 32, 128)
                part = total[:, h, y] + part
                if h == 0:
                    total[0, h, y] = part[0]
                else:
                    total[3, h, y] = part[3]
                inner = part.reshape(4, 4, 8, 128)
                for s in range(4):
                    finish(s, (slice(0, 4), h, y), inner[:, s])
        for d in (0, 1):
            i, h, p = (0, 0, 0) if d == 0 else (3, 1, 3)
            lhs = jnp.concatenate(
                [zx[d, ky : ky + 8].reshape(256, 384) for ky in range(3)], axis=1
            )
            rhs = jnp.concatenate(
                [wp[p, ky][:, 128 * h : 128 * h + 128] for ky in range(3)], axis=0
            )
            add = jnp.dot(lhs, rhs, preferred_element_type=F32).reshape(8, 32, 128)
            part = (total[i, h] + add).reshape(8, 4, 8, 128)
            for s in range(4):
                finish(s, (i, h, slice(0, 8)), part[:, s])

    own_sources(field, 7, side_src, edge_src)
    fine_centre(field, zin)

    copies[4].wait()
    copies[5].wait()
    for copy in copies[6:]:
        copy.start()

    def to_hidden(s, at, value):
        value = jnp.maximum(value + b1[...].reshape(1, 1, 128), 0.0) * live[s]
        hidden[(s,) + at] = value.astype(BF16).astype(F32)

    convolve(zin, w1p, to_hidden)
    for copy in sent:
        copy.wait_recv()
    received_sources(7, side_src, edge_src, recv_side.at[0], recv_edge.at[0])
    fine_rim()
    add_rim(w1p, to_hidden)
    sent_hidden = exchange(
        1, hidden, 7, send_side.at[1], send_edge.at[1], recv_side.at[1], recv_edge.at[1]
    )
    for copy in sent_hidden:
        copy.start()
    own_sources(hidden, 7, side_src, edge_src)
    fine_centre(hidden, zhid)

    for k in (6, 7, 8):
        copies[k].wait()

    def to_fine(s, at, value):
        value = value + b2[...].reshape(1, 1, 128) + field[(s,) + at]
        out[(s,) + at] = value * live[s]

    convolve(zhid, w2p, to_fine)
    for copy in sent_hidden:
        copy.wait_recv()
    received_sources(7, side_src, edge_src, recv_side.at[1], recv_edge.at[1])
    fine_rim()
    add_rim(w2p, to_fine)

    for s in range(4):
        for i in range(4):
            rows = (out[s, i, 0] + out[s, i, 1]).reshape(4, 2, 8, 128)
            rows = rows[:, 0] + rows[:, 1]
            even = lax.broadcasted_iota(jnp.int32, rows.shape, 1) % 2 == 0
            other = jnp.where(even, pltpu.roll(rows, 7, 1), pltpu.roll(rows, 1, 1))
            mean = (rows + other) * 0.125
            coarse_field[s, i] = mean.astype(BF16).astype(F32)
    sent_coarse = exchange(
        2, coarse_field, 3, csend_side, csend_edge, crecv_side, crecv_edge
    )
    for copy in sent_coarse:
        copy.start()
    own_sources(coarse_field, 3, cside_src, cedge_src)
    for x in range(4):
        for rows, lanes, value in pair(lambda q: coarse_field[q, x], 0, 0, 2):
            zc[x + 1, 1:5, rows, lanes] = value
    for k in (9, 10, 11):
        copies[k].wait()
    for copy in sent_coarse:
        copy.wait_recv()
    received_sources(3, cside_src, cedge_src, crecv_side, crecv_edge)
    for d, (ox, oy) in enumerate(SIDES):
        for rows, lanes, value in pair(lambda q: cside_src[d, q], ox, oy, 2):
            if oy == 0:
                zc[0 if ox < 0 else 5, 1:5, rows, lanes] = value
            else:
                zc[1:5, 0 if oy < 0 else 5, rows, lanes] = value
    for d, (ox, oy) in enumerate(EDGES):
        for rows, lanes, value in pair(lambda q: cedge_src[d, q], ox, oy, 2):
            zc[0 if ox < 0 else 5, 0 if oy < 0 else 5, rows, lanes] = value[0]

    lhs = jnp.concatenate(
        [
            zc[kx : kx + 4, ky : ky + 4].reshape(512, 384)
            for kx in range(3)
            for ky in range(3)
        ],
        axis=1,
    )
    acc = jnp.dot(lhs, wcv[...], preferred_element_type=F32)
    acc = jnp.maximum(acc + bc[...], 0.0).reshape(16, 4, 8, 256)
    acc = jnp.concatenate([(acc[:, s] * live[s])[:, None] for s in range(4)], axis=1)
    lifted = jnp.dot(
        acc.reshape(512, 256).astype(BF16), wlv[...], preferred_element_type=F32
    ).reshape(4, 4, 1, 4, 8, 128)
    for s in range(4):
        for x in range(4):
            raised = jnp.broadcast_to(lifted[x, :, :, s], (4, 2, 8, 128))
            raised = raised.reshape(8, 8, 128)
            for h in (0, 1):
                out[s, x, h] = (out[s, x, h] + raised) * live[s]
    for copy in sent + sent_hidden + sent_coarse:
        copy.wait_send()


def local(gx, gy, features, slot_cell, neighbours, w1, b1, w2, b2, wc, bc, wl):
    operands = [
        pltpu.with_memory_space_constraint(operand, pltpu.HBM)
        for operand in (
            slot_cell.reshape(4),
            neighbours.reshape(4, 26),
            features.reshape(4, 8, 64, 128),
            w1.reshape(3, 3, 384, 128),
            b1.reshape(1, 128),
            w2.reshape(3, 3, 384, 128),
            b2.reshape(1, 128),
            wc.reshape(3456, 256),
            bc.reshape(1, 256),
            wl,
        )
    ]
    result = pl.pallas_call(
        functools.partial(kernel, gx, gy),
        out_shape=jax.ShapeDtypeStruct((4, 4, 2, 8, 8, 128), F32),
        in_specs=[pl.BlockSpec(memory_space=pl.ANY)] * 10,
        out_specs=pl.BlockSpec(memory_space=pltpu.VMEM),
        scratch_shapes=[
            pltpu.SMEM((4,), jnp.int32),
            pltpu.SMEM((4, 26), jnp.int32),
            pltpu.VMEM((1, 128), F32),
            pltpu.VMEM((1, 128), F32),
            pltpu.VMEM((1, 256), F32),
            pltpu.VMEM((4, 8, 64, 128), BF16),
            pltpu.VMEM((5, 4, 2, 8, 8, 128), F32),
            pltpu.VMEM((5, 4, 2, 8, 8, 128), F32),
            pltpu.VMEM((5, 4, 4, 8, 128), F32),
            pltpu.VMEM((4, 9, 8, 8, 128), F32),
            pltpu.VMEM((4, 17, 1, 8, 128), F32),
            pltpu.VMEM((4, 9, 4, 8, 128), F32),
            pltpu.VMEM((4, 17, 1, 8, 128), F32),
            pltpu.VMEM((2, 4, 10, 32, 384), BF16),
            pltpu.VMEM((2, 4, 10, 32, 384), BF16),
            pltpu.VMEM((2, 10, 32, 384), BF16),
            pltpu.VMEM((2, 2, 5, 32, 384), BF16),
            pltpu.VMEM((6, 6, 32, 384), BF16),
            pltpu.VMEM((4, 3, 384, 256), BF16),
            pltpu.VMEM((4, 3, 384, 256), BF16),
            pltpu.VMEM((3456, 256), BF16),
            pltpu.VMEM((256, 128), BF16),
            pltpu.VMEM((4, 2, 8, 32, 128), F32),
            pltpu.VMEM((2, 4, 4, 64, 128), BF16),
            pltpu.VMEM((2, 4, 32, 128), BF16),
            pltpu.VMEM((2, 4, 4, 64, 128), BF16),
            pltpu.VMEM((2, 4, 32, 128), BF16),
            pltpu.VMEM((4, 4, 32, 128), BF16),
            pltpu.VMEM((4, 32, 128), BF16),
            pltpu.VMEM((4, 4, 32, 128), BF16),
            pltpu.VMEM((4, 32, 128), BF16),
            pltpu.SemaphoreType.DMA((12,)),
            pltpu.SemaphoreType.DMA((3, 8)),
            pltpu.SemaphoreType.DMA((3, 8)),
        ],
        compiler_params=pltpu.CompilerParams(
            collective_id=0, has_side_effects=True, vmem_limit_bytes=48 * 2**20
        ),
        cost_estimate=pl.CostEstimate(
            flops=8_000_000_000, bytes_accessed=8_000_000, transcendentals=0
        ),
        name="unet_window",
    )(*operands)
    return result.reshape(1, 1, 4, 512, 128)


def solution(mesh):
    placed = (
        P("gx", "gy", None, None, None),
        P("gx", "gy", None),
        P("gx", "gy", None, None),
    ) + (P(),) * 7
    return jax.shard_map(
        functools.partial(local, mesh.shape["gx"], mesh.shape["gy"]),
        mesh=mesh,
        in_specs=placed,
        out_specs=P("gx", "gy", None, None, None),
        check_vma=False,
    )
```

```python
import functools

import jax
import jax.numpy as jnp
from jax import lax
from jax.experimental import pallas as pl
from jax.experimental.pallas import tpu as pltpu
from jax.sharding import PartitionSpec as P

MESH = pl.DeviceIdType.MESH
F32 = jnp.float32
BF16 = jnp.bfloat16

OFFSETS = [
    (ox, oy, oz)
    for ox in (-1, 0, 1)
    for oy in (-1, 0, 1)
    for oz in (-1, 0, 1)
    if (ox, oy, oz) != (0, 0, 0)
]
NUMBER = {offset: k for k, offset in enumerate(OFFSETS)}
SIDES = [(-1, 0), (1, 0), (0, -1), (0, 1)]
EDGES = [(-1, -1), (-1, 1), (1, -1), (1, 1)]
ALL = SIDES + EDGES


def edge_of(step, last):
    return last if step < 0 else 0


def kernel(
    gx,
    gy,
    cell_hbm,
    nbr_hbm,
    feat,
    w1,
    b1_hbm,
    w2,
    b2_hbm,
    wc,
    bc_hbm,
    wl,
    out,
    cell,
    nbr,
    b1,
    b2,
    bc,
    staged,
    field,
    hidden,
    coarse_field,
    side_src,
    edge_src,
    cside_src,
    cedge_src,
    zin,
    zhid,
    zx,
    zy,
    zc,
    w1p,
    w2p,
    wcv,
    wlv,
    total,
    send_side,
    send_edge,
    recv_side,
    recv_edge,
    csend_side,
    csend_edge,
    crecv_side,
    crecv_edge,
    local_sem,
    send_sem,
    recv_sem,
):
    mx = lax.axis_index("gx")
    my = lax.axis_index("gy")

    def device_at(ox, oy):
        return (lax.rem(mx + ox + gx, gx), lax.rem(my + oy + gy, gy))

    def inside(ox, oy):
        found = None
        for at, step, size in ((mx, ox, gx), (my, oy, gy)):
            if step != 0:
                here = at > 0 if step < 0 else at < size - 1
                found = here if found is None else jnp.logical_and(found, here)
        return found

    def when_inside(ox, oy, act):
        @pl.when(inside(ox, oy))
        def _():
            act()

    def signal_to(ox, oy):
        pl.semaphore_signal(
            barrier, inc=1, device_id=device_at(ox, oy), device_id_type=MESH
        )

    barrier = pltpu.get_barrier_semaphore()
    for ox, oy in ALL:
        when_inside(ox, oy, functools.partial(signal_to, ox, oy))
    beside_x = jnp.where(mx > 0, 1, 0) + jnp.where(mx < gx - 1, 1, 0)
    beside_y = jnp.where(my > 0, 1, 0) + jnp.where(my < gy - 1, 1, 0)
    partners = (1 + beside_x) * (1 + beside_y) - 1

    pairs = [
        (feat, staged),
        (cell_hbm, cell),
        (nbr_hbm, nbr),
        (b1_hbm, b1),
        (w1, w1p.at[0:3, :, :, 0:128]),
        (w1, w1p.at[1:4, :, :, 128:256]),
        (w2, w2p.at[0:3, :, :, 0:128]),
        (w2, w2p.at[1:4, :, :, 128:256]),
        (b2_hbm, b2),
        (wc, wcv),
        (wl, wlv),
        (bc_hbm, bc),
    ]
    copies = [
        pltpu.make_async_copy(src, dst, local_sem.at[k])
        for k, (src, dst) in enumerate(pairs)
    ]
    for copy in copies[:6]:
        copy.start()

    for wp in (w1p, w2p):
        wp[3, :, :, 0:128] = jnp.zeros((3, 384, 128), BF16)
        wp[0, :, :, 128:256] = jnp.zeros((3, 384, 128), BF16)
    field[4] = jnp.zeros((4, 2, 8, 8, 128), F32)
    hidden[4] = jnp.zeros((4, 2, 8, 8, 128), F32)
    coarse_field[4] = jnp.zeros((4, 4, 8, 128), F32)
    for d in range(4):
        side_src[d, 8] = jnp.zeros((8, 8, 128), F32)
        cside_src[d, 8] = jnp.zeros((4, 8, 128), F32)
        edge_src[d, 16] = jnp.zeros((1, 8, 128), F32)
        cedge_src[d, 16] = jnp.zeros((1, 8, 128), F32)
    for z in (zin, zhid):
        z[:, :, 0] = jnp.zeros((2, 4, 32, 384), BF16)
        z[:, :, 9] = jnp.zeros((2, 4, 32, 384), BF16)
    zy[:, 0, 0] = jnp.zeros((2, 32, 384), BF16)
    zy[:, 1, 4] = jnp.zeros((2, 32, 384), BF16)

    copies[0].wait()
    for s in range(4):
        for x in range(8):
            field[s, x // 2, x % 2] = staged[s, x].astype(F32).reshape(8, 8, 128)

    def plane(source, s, x):
        if source is coarse_field:
            return source[s, x]
        return source[s, x // 2, x % 2]

    def across(source, s, y):
        if source is coarse_field:
            return source[s, :, y]
        return source[s, :, :, y].reshape(8, 8, 128)

    def column(source, s, x, y):
        if source is coarse_field:
            return source[s, x, y]
        return source[s, x // 2, x % 2, y]

    def exchange(number, source, last, sides, edges, rsides, redges):
        rows = 8 * (last + 1)
        for d, (ox, oy) in enumerate(SIDES):
            if number == 0 and oy == 0:
                continue
            for s in range(4):
                if oy == 0:
                    face = plane(source, s, edge_of(ox, last))
                else:
                    face = across(source, s, edge_of(oy, last))
                sides[d, s] = face.reshape(rows, 128).astype(BF16)
        for d, (ox, oy) in enumerate(EDGES):
            edges[d] = jnp.concatenate(
                [
                    column(source, s, edge_of(ox, last), edge_of(oy, last))
                    for s in range(4)
                ],
                axis=0,
            ).astype(BF16)
        described = {}
        for k in (4, 5, 6, 7, 2, 3, 0, 1):
            ox, oy = ALL[k]
            if k < 4:
                src, dst = sides.at[k], rsides.at[k]
                if number == 0 and oy == 0:
                    src = feat.at[:, edge_of(ox, last)]
            else:
                src, dst = edges.at[k - 4], redges.at[k - 4]
            described[ox, oy] = (
                pltpu.make_async_remote_copy(
                    src_ref=src,
                    dst_ref=dst,
                    send_sem=send_sem.at[number, k],
                    recv_sem=recv_sem.at[number, k],
                    device_id=device_at(-ox, -oy),
                    device_id_type=MESH,
                )
            )
        return described

    def start(described):
        for (ox, oy), copy in described.items():
            when_inside(-ox, -oy, copy.start)

    def arrive(described):
        for (ox, oy), copy in described.items():
            when_inside(ox, oy, copy.wait_recv)

    sent = exchange(
        0, field, 7, send_side.at[0], send_edge.at[0], recv_side.at[0], recv_edge.at[0]
    )
    pl.semaphore_wait(barrier, partners)
    start(sent)

    for k in (1, 2, 3):
        copies[k].wait()
    live = [jnp.where(cell[s] >= 0, 1.0, 0.0).astype(F32) for s in range(4)]

    def index(s, ox, oy, oz):
        if (ox, oy, oz) == (0, 0, 0):
            return s
        entry = nbr[s, NUMBER[ox, oy, oz]]
        safe = jnp.maximum(entry, 0)
        block = lax.shift_right_logical(safe, 2)
        slot = lax.bitwise_and(safe, 3)
        if (ox, oy) == (0, 0):
            return jnp.where(entry < 0, 4, slot)
        if ox == 0 or oy == 0:
            place = slot + jnp.where(block == 4, 0, 4)
            return jnp.where(entry < 0, 8, place)
        beside_x = (ox + 1) * 3 + 1
        beside_y = 3 + (oy + 1)
        place = slot + jnp.where(
            block == 4,
            0,
            jnp.where(block == beside_x, 4, jnp.where(block == beside_y, 8, 12)),
        )
        return jnp.where(entry < 0, 16, place)

    where = {
        (s, ox, oy, oz): index(s, ox, oy, oz)
        for s in range(4)
        for ox in (-1, 0, 1)
        for oy in (-1, 0, 1)
        for oz in (-1, 0, 1)
    }

    def shifted(low, own, high, step):
        row = lax.broadcasted_iota(jnp.int32, own.shape, own.ndim - 2)
        axis = own.ndim - 2
        down = pltpu.roll(jnp.where(row >= 8 - step, low, own), step, axis)
        up = pltpu.roll(jnp.where(row < step, high, own), 8 - step, axis)
        return down, own, up

    def pair(fetch, ox, oy, step):
        for half in (0, 1):
            parts = [
                shifted(*[fetch(where[s, ox, oy, oz]) for oz in (-1, 0, 1)], step)
                for s in (2 * half, 2 * half + 1)
            ]
            for kz in range(3):
                both = jnp.concatenate([parts[0][kz], parts[1][kz]], axis=-2)
                yield slice(16 * half, 16 * half + 16), slice(
                    128 * kz, 128 * kz + 128
                ), both.astype(BF16)

    def fine_centre(source, z):
        def body(m, carry):
            for h in (0, 1):
                for rows, lanes, value in pair(lambda q: source[q, m, h], 0, 0, 1):
                    z[h, m, 1:9, rows, lanes] = value
            return carry

        lax.fori_loop(0, 4, body, 0)

    def fine_rim():
        for d, (ox, oy) in enumerate(SIDES):
            for rows, lanes, value in pair(lambda q: side_src[d, q], ox, oy, 1):
                if oy == 0:
                    zx[d, 1:9, rows, lanes] = value
                else:
                    split = value.reshape(4, 2, 16, 128)
                    zy[d - 2, 1, 0:4, rows, lanes] = split[:, 0]
                    zy[d - 2, 0, 1:5, rows, lanes] = split[:, 1]
        for d, (ox, oy) in enumerate(EDGES):
            for rows, lanes, value in pair(lambda q: edge_src[d, q], ox, oy, 1):
                zx[0 if ox < 0 else 1, 0 if oy < 0 else 9, rows, lanes] = value[0]

    def own_sources(source, last, sides, edges):
        for d, (ox, oy) in enumerate(SIDES):
            for s in range(4):
                if oy == 0:
                    sides[d, s] = plane(source, s, edge_of(ox, last))
                else:
                    sides[d, s] = across(source, s, edge_of(oy, last))
        for d, (ox, oy) in enumerate(EDGES):
            for s in range(4):
                edges[d, s, 0] = column(
                    source, s, edge_of(ox, last), edge_of(oy, last)
                )

    def received_sources(last, sides, edges, rsides, redges):
        for d in range(4):
            for s in range(4):
                sides[d, 4 + s] = rsides[d, s].astype(F32).reshape(last + 1, 8, 128)
        for d, (ox, oy) in enumerate(EDGES):
            dx = SIDES.index((ox, 0))
            dy = SIDES.index((0, oy))
            far = redges[d].astype(F32)
            for s in range(4):
                edges[d, 4 + s, 0] = sides[dx, 4 + s, edge_of(oy, last)]
                edges[d, 8 + s, 0] = sides[dy, 4 + s, edge_of(ox, last)]
                edges[d, 12 + s, 0] = far[8 * s : 8 * s + 8]

    def centre_conv(z, wp, i):
        planes = [(1, i - 1), (0, i), (1, i), (0, i + 1)]
        used = [p for p in range(4) if 0 <= planes[p][1] < 4]
        lhs = jnp.concatenate(
            [
                z[planes[p][0], planes[p][1], ky : ky + 8].reshape(256, 384)
                for ky in range(3)
                for p in used
            ],
            axis=1,
        )
        rhs = jnp.concatenate([wp[p, ky] for ky in range(3) for p in used], axis=0)
        return jnp.dot(lhs, rhs, preferred_element_type=F32)

    def convolve(z, wp, finish):
        for i in range(4):
            acc = centre_conv(z, wp, i)
            for h in (0, 1):
                part = acc[:, 128 * h : 128 * h + 128].reshape(8, 32, 128)
                total[i, h] = part
                if 0 < 2 * i + h < 7:
                    inner = part[1:7].reshape(6, 4, 8, 128)
                    for s in range(4):
                        finish(s, (i, h, slice(1, 7)), inner[:, s])

    def add_rim(wp, finish):
        for d in (0, 1):
            y, ky = (0, 0) if d == 0 else (7, 2)
            lhs = jnp.concatenate(
                [
                    zy[d, p % 2, p // 2 : p // 2 + 4].reshape(128, 384)
                    for p in range(4)
                ],
                axis=1,
            )
            rhs = jnp.concatenate([wp[p, ky] for p in range(4)], axis=0)
            add = jnp.dot(lhs, rhs, preferred_element_type=F32)
            for h in (0, 1):
                part = add[:, 128 * h : 128 * h + 128].reshape(4, 32, 128)
                part = total[:, h, y] + part
                if h == 0:
                    total[0, h, y] = part[0]
                else:
                    total[3, h, y] = part[3]
                inner = part.reshape(4, 4, 8, 128)
                for s in range(4):
                    finish(s, (slice(0, 4), h, y), inner[:, s])
        for d in (0, 1):
            i, h, p = (0, 0, 0) if d == 0 else (3, 1, 3)
            lhs = jnp.concatenate(
                [zx[d, ky : ky + 8].reshape(256, 384) for ky in range(3)], axis=1
            )
            rhs = jnp.concatenate(
                [wp[p, ky][:, 128 * h : 128 * h + 128] for ky in range(3)], axis=0
            )
            add = jnp.dot(lhs, rhs, preferred_element_type=F32).reshape(8, 32, 128)
            part = (total[i, h] + add).reshape(8, 4, 8, 128)
            for s in range(4):
                finish(s, (i, h, slice(0, 8)), part[:, s])

    own_sources(field, 7, side_src, edge_src)
    fine_centre(field, zin)

    copies[4].wait()
    copies[5].wait()
    for copy in copies[6:]:
        copy.start()

    def to_hidden(s, at, value):
        value = jnp.maximum(value + b1[...].reshape(1, 1, 128), 0.0) * live[s]
        hidden[(s,) + at] = value.astype(BF16).astype(F32)

    convolve(zin, w1p, to_hidden)
    arrive(sent)
    received_sources(7, side_src, edge_src, recv_side.at[0], recv_edge.at[0])
    fine_rim()
    add_rim(w1p, to_hidden)
    sent_hidden = exchange(
        1, hidden, 7, send_side.at[1], send_edge.at[1], recv_side.at[1], recv_edge.at[1]
    )
    start(sent_hidden)
    own_sources(hidden, 7, side_src, edge_src)
    fine_centre(hidden, zhid)

    for k in (6, 7, 8):
        copies[k].wait()

    def to_fine(s, at, value):
        value = value + b2[...].reshape(1, 1, 128) + field[(s,) + at]
        out[(s,) + at] = value * live[s]

    convolve(zhid, w2p, to_fine)
    arrive(sent_hidden)
    received_sources(7, side_src, edge_src, recv_side.at[1], recv_edge.at[1])
    fine_rim()
    add_rim(w2p, to_fine)

    for s in range(4):
        for i in range(4):
            rows = (out[s, i, 0] + out[s, i, 1]).reshape(4, 2, 8, 128)
            rows = rows[:, 0] + rows[:, 1]
            even = lax.broadcasted_iota(jnp.int32, rows.shape, 1) % 2 == 0
            other = jnp.where(even, pltpu.roll(rows, 7, 1), pltpu.roll(rows, 1, 1))
            mean = (rows + other) * 0.125
            coarse_field[s, i] = mean.astype(BF16).astype(F32)
    sent_coarse = exchange(
        2, coarse_field, 3, csend_side, csend_edge, crecv_side, crecv_edge
    )
    start(sent_coarse)
    own_sources(coarse_field, 3, cside_src, cedge_src)
    for x in range(4):
        for rows, lanes, value in pair(lambda q: coarse_field[q, x], 0, 0, 2):
            zc[x + 1, 1:5, rows, lanes] = value
    for k in (9, 10, 11):
        copies[k].wait()
    arrive(sent_coarse)
    received_sources(3, cside_src, cedge_src, crecv_side, crecv_edge)
    for d, (ox, oy) in enumerate(SIDES):
        for rows, lanes, value in pair(lambda q: cside_src[d, q], ox, oy, 2):
            if oy == 0:
                zc[0 if ox < 0 else 5, 1:5, rows, lanes] = value
            else:
                zc[1:5, 0 if oy < 0 else 5, rows, lanes] = value
    for d, (ox, oy) in enumerate(EDGES):
        for rows, lanes, value in pair(lambda q: cedge_src[d, q], ox, oy, 2):
            zc[0 if ox < 0 else 5, 0 if oy < 0 else 5, rows, lanes] = value[0]

    lhs = jnp.concatenate(
        [
            zc[kx : kx + 4, ky : ky + 4].reshape(512, 384)
            for kx in range(3)
            for ky in range(3)
        ],
        axis=1,
    )
    acc = jnp.dot(lhs, wcv[...], preferred_element_type=F32)
    acc = jnp.maximum(acc + bc[...], 0.0).reshape(16, 4, 8, 256)
    acc = jnp.concatenate([(acc[:, s] * live[s])[:, None] for s in range(4)], axis=1)
    lifted = jnp.dot(
        acc.reshape(512, 256).astype(BF16), wlv[...], preferred_element_type=F32
    ).reshape(4, 4, 1, 4, 8, 128)
    for s in range(4):
        for x in range(4):
            raised = jnp.broadcast_to(lifted[x, :, :, s], (4, 2, 8, 128))
            raised = raised.reshape(8, 8, 128)
            for h in (0, 1):
                out[s, x, h] = (out[s, x, h] + raised) * live[s]
    for described in (sent, sent_hidden, sent_coarse):
        for (ox, oy), copy in described.items():
            when_inside(-ox, -oy, copy.wait_send)


def local(gx, gy, features, slot_cell, neighbours, w1, b1, w2, b2, wc, bc, wl):
    operands = [
        pltpu.with_memory_space_constraint(operand, pltpu.HBM)
        for operand in (
            slot_cell.reshape(4),
            neighbours.reshape(4, 26),
            features.reshape(4, 8, 64, 128),
            w1.reshape(3, 3, 384, 128),
            b1.reshape(1, 128),
            w2.reshape(3, 3, 384, 128),
            b2.reshape(1, 128),
            wc.reshape(3456, 256),
            bc.reshape(1, 256),
            wl,
        )
    ]
    result = pl.pallas_call(
        functools.partial(kernel, gx, gy),
        out_shape=jax.ShapeDtypeStruct((4, 4, 2, 8, 8, 128), F32),
        in_specs=[pl.BlockSpec(memory_space=pl.ANY)] * 10,
        out_specs=pl.BlockSpec(memory_space=pltpu.VMEM),
        scratch_shapes=[
            pltpu.SMEM((4,), jnp.int32),
            pltpu.SMEM((4, 26), jnp.int32),
            pltpu.VMEM((1, 128), F32),
            pltpu.VMEM((1, 128), F32),
            pltpu.VMEM((1, 256), F32),
            pltpu.VMEM((4, 8, 64, 128), BF16),
            pltpu.VMEM((5, 4, 2, 8, 8, 128), F32),
            pltpu.VMEM((5, 4, 2, 8, 8, 128), F32),
            pltpu.VMEM((5, 4, 4, 8, 128), F32),
            pltpu.VMEM((4, 9, 8, 8, 128), F32),
            pltpu.VMEM((4, 17, 1, 8, 128), F32),
            pltpu.VMEM((4, 9, 4, 8, 128), F32),
            pltpu.VMEM((4, 17, 1, 8, 128), F32),
            pltpu.VMEM((2, 4, 10, 32, 384), BF16),
            pltpu.VMEM((2, 4, 10, 32, 384), BF16),
            pltpu.VMEM((2, 10, 32, 384), BF16),
            pltpu.VMEM((2, 2, 5, 32, 384), BF16),
            pltpu.VMEM((6, 6, 32, 384), BF16),
            pltpu.VMEM((4, 3, 384, 256), BF16),
            pltpu.VMEM((4, 3, 384, 256), BF16),
            pltpu.VMEM((3456, 256), BF16),
            pltpu.VMEM((256, 128), BF16),
            pltpu.VMEM((4, 2, 8, 32, 128), F32),
            pltpu.VMEM((2, 4, 4, 64, 128), BF16),
            pltpu.VMEM((2, 4, 32, 128), BF16),
            pltpu.VMEM((2, 4, 4, 64, 128), BF16),
            pltpu.VMEM((2, 4, 32, 128), BF16),
            pltpu.VMEM((4, 4, 32, 128), BF16),
            pltpu.VMEM((4, 32, 128), BF16),
            pltpu.VMEM((4, 4, 32, 128), BF16),
            pltpu.VMEM((4, 32, 128), BF16),
            pltpu.SemaphoreType.DMA((12,)),
            pltpu.SemaphoreType.DMA((3, 8)),
            pltpu.SemaphoreType.DMA((3, 8)),
        ],
        compiler_params=pltpu.CompilerParams(
            collective_id=0, has_side_effects=True, vmem_limit_bytes=48 * 2**20
        ),
        cost_estimate=pl.CostEstimate(
            flops=8_000_000_000, bytes_accessed=8_000_000, transcendentals=0
        ),
        name="unet_window",
    )(*operands)
    return result.reshape(1, 1, 4, 512, 128)


def solution(mesh):
    placed = (
        P("gx", "gy", None, None, None),
        P("gx", "gy", None),
        P("gx", "gy", None, None),
    ) + (P(),) * 7
    return jax.shard_map(
        functools.partial(local, mesh.shape["gx"], mesh.shape["gy"]),
        mesh=mesh,
        in_specs=placed,
        out_specs=P("gx", "gy", None, None, None),
        check_vma=False,
    )
```

```python
import functools

import jax
import jax.numpy as jnp
from jax import lax
from jax.experimental import pallas as pl
from jax.experimental.pallas import tpu as pltpu
from jax.sharding import PartitionSpec as P

MESH = pl.DeviceIdType.MESH
F32 = jnp.float32
BF16 = jnp.bfloat16

OFFSETS = [
    (ox, oy, oz)
    for ox in (-1, 0, 1)
    for oy in (-1, 0, 1)
    for oz in (-1, 0, 1)
    if (ox, oy, oz) != (0, 0, 0)
]
NUMBER = {offset: k for k, offset in enumerate(OFFSETS)}
SIDES = [(-1, 0), (1, 0), (0, -1), (0, 1)]
EDGES = [(-1, -1), (-1, 1), (1, -1), (1, 1)]
ALL = SIDES + EDGES
FARTHEST = (4, 5, 6, 7, 2, 3, 0, 1)


def edge_of(step, last):
    return last if step < 0 else 0


def kernel(
    gx,
    gy,
    cell_hbm,
    nbr_hbm,
    feat,
    w1,
    b1_hbm,
    w2,
    b2_hbm,
    wc,
    bc_hbm,
    wl,
    out,
    cell,
    nbr,
    b1,
    b2,
    bc,
    staged,
    staged_rim,
    field,
    hidden,
    coarse_field,
    side_src,
    edge_src,
    cside_src,
    cedge_src,
    zin,
    zhid,
    zx,
    zy,
    zc,
    zcx,
    zcy,
    w1p,
    w2p,
    wcv,
    wlv,
    total,
    ctotal,
    send_side,
    send_edge,
    recv_side,
    recv_edge,
    csend_side,
    csend_edge,
    crecv_side,
    crecv_edge,
    local_sem,
    rim_sem,
    send_sem,
    recv_sem,
):
    mx = lax.axis_index("gx")
    my = lax.axis_index("gy")

    def device_at(ox, oy):
        return (lax.rem(mx + ox + gx, gx), lax.rem(my + oy + gy, gy))

    def inside(ox, oy):
        found = None
        for at, step, size in ((mx, ox, gx), (my, oy, gy)):
            if step != 0:
                here = at > 0 if step < 0 else at < size - 1
                found = here if found is None else jnp.logical_and(found, here)
        return found

    def when_inside(ox, oy, act):
        @pl.when(inside(ox, oy))
        def _():
            act()

    def signal_to(ox, oy):
        pl.semaphore_signal(
            barrier, inc=1, device_id=device_at(ox, oy), device_id_type=MESH
        )

    barrier = pltpu.get_barrier_semaphore()
    for k in FARTHEST:
        when_inside(*ALL[k], functools.partial(signal_to, *ALL[k]))
    beside_x = jnp.where(mx > 0, 1, 0) + jnp.where(mx < gx - 1, 1, 0)
    beside_y = jnp.where(my > 0, 1, 0) + jnp.where(my < gy - 1, 1, 0)
    partners = (1 + beside_x) * (1 + beside_y) - 1

    pairs = [
        (feat, staged),
        (cell_hbm, cell),
        (nbr_hbm, nbr),
        (b1_hbm, b1),
        (w1, w1p.at[0:3, :, :, 0:128]),
        (w1, w1p.at[1:4, :, :, 128:256]),
        (w2, w2p.at[0:3, :, :, 0:128]),
        (w2, w2p.at[1:4, :, :, 128:256]),
        (b2_hbm, b2),
        (wc, wcv),
        (wl, wlv),
        (bc_hbm, bc),
    ]
    copies = [
        pltpu.make_async_copy(src, dst, local_sem.at[k])
        for k, (src, dst) in enumerate(pairs)
    ]
    rims = [
        pltpu.make_async_copy(
            feat.at[:, :, 48 * d : 48 * d + 16], staged_rim.at[d], rim_sem.at[d]
        )
        for d in (0, 1)
    ]
    for copy in rims + copies[:6]:
        copy.start()

    for wp in (w1p, w2p):
        wp[3, :, :, 0:128] = jnp.zeros((3, 384, 128), BF16)
        wp[0, :, :, 128:256] = jnp.zeros((3, 384, 128), BF16)
    field[4] = jnp.zeros((4, 2, 8, 8, 128), F32)
    hidden[4] = jnp.zeros((4, 2, 8, 8, 128), F32)
    coarse_field[4] = jnp.zeros((4, 4, 8, 128), F32)
    for d in range(4):
        side_src[d, 8] = jnp.zeros((8, 8, 128), F32)
        cside_src[d, 8] = jnp.zeros((4, 8, 128), F32)
        edge_src[d, 16] = jnp.zeros((1, 8, 128), F32)
        cedge_src[d, 16] = jnp.zeros((1, 8, 128), F32)
    for z in (zin, zhid):
        z[:, :, 0] = jnp.zeros((2, 4, 32, 384), BF16)
        z[:, :, 9] = jnp.zeros((2, 4, 32, 384), BF16)
    for side in range(2):
        for end in (0, 9):
            zx[side, end] = jnp.zeros((32, 384), BF16)
        for end in (0, 5):
            zcx[side, end] = jnp.zeros((32, 384), BF16)
    for end in (0, 5):
        zc[end] = jnp.zeros((6, 32, 384), BF16)
        zc[:, end] = jnp.zeros((6, 32, 384), BF16)

    for copy in rims:
        copy.wait()

    def plane(source, s, x):
        if source is coarse_field:
            return source[s, x]
        return source[s, x // 2, x % 2]

    def across(source, s, y):
        if source is coarse_field:
            return source[s, :, y]
        if source is field:
            d = y // 7
            return staged_rim[d, s].astype(F32)[:, 8 * d : 8 * d + 8]
        return source[s, :, :, y].reshape(8, 8, 128)

    def column(source, s, x, y):
        if source is coarse_field:
            return source[s, x, y]
        if source is field:
            d = y // 7
            return staged_rim[d, s, x].astype(F32)[8 * d : 8 * d + 8]
        return source[s, x // 2, x % 2, y]

    def exchange(number, source, last, sides, edges, rsides, redges):
        rows = 8 * (last + 1)
        for d, (ox, oy) in enumerate(SIDES):
            if number == 0 and oy == 0:
                continue
            for s in range(4):
                if oy == 0:
                    face = plane(source, s, edge_of(ox, last))
                else:
                    face = across(source, s, edge_of(oy, last))
                sides[d, s] = face.reshape(rows, 128).astype(BF16)
        for d, (ox, oy) in enumerate(EDGES):
            edges[d] = jnp.concatenate(
                [
                    column(source, s, edge_of(ox, last), edge_of(oy, last))
                    for s in range(4)
                ],
                axis=0,
            ).astype(BF16)
        described = {}
        for k in FARTHEST:
            ox, oy = ALL[k]
            if k < 4:
                src, dst = sides.at[k], rsides.at[k]
                if number == 0 and oy == 0:
                    src = feat.at[:, edge_of(ox, last)]
            else:
                src, dst = edges.at[k - 4], redges.at[k - 4]
            described[ox, oy] = (
                pltpu.make_async_remote_copy(
                    src_ref=src,
                    dst_ref=dst,
                    send_sem=send_sem.at[number, k],
                    recv_sem=recv_sem.at[number, k],
                    device_id=device_at(-ox, -oy),
                    device_id_type=MESH,
                )
            )
        return described

    def start(described):
        for (ox, oy), copy in described.items():
            when_inside(-ox, -oy, copy.start)

    def arrive(described, directions):
        for ox, oy in directions:
            when_inside(ox, oy, described[ox, oy].wait_recv)

    sent = exchange(
        0, field, 7, send_side.at[0], send_edge.at[0], recv_side.at[0], recv_edge.at[0]
    )
    pl.semaphore_wait(barrier, partners)
    start(sent)

    copies[0].wait()
    for s in range(4):
        for x in range(8):
            field[s, x // 2, x % 2] = staged[s, x].astype(F32).reshape(8, 8, 128)

    for k in (1, 2, 3):
        copies[k].wait()
    live = [jnp.where(cell[s] >= 0, 1.0, 0.0).astype(F32) for s in range(4)]

    def index(s, ox, oy, oz):
        if (ox, oy, oz) == (0, 0, 0):
            return s
        entry = nbr[s, NUMBER[ox, oy, oz]]
        safe = jnp.maximum(entry, 0)
        block = lax.shift_right_logical(safe, 2)
        slot = lax.bitwise_and(safe, 3)
        if (ox, oy) == (0, 0):
            return jnp.where(entry < 0, 4, slot)
        if ox == 0 or oy == 0:
            place = slot + jnp.where(block == 4, 0, 4)
            return jnp.where(entry < 0, 8, place)
        beside_x = (ox + 1) * 3 + 1
        beside_y = 3 + (oy + 1)
        place = slot + jnp.where(
            block == 4,
            0,
            jnp.where(block == beside_x, 4, jnp.where(block == beside_y, 8, 12)),
        )
        return jnp.where(entry < 0, 16, place)

    where = {
        (s, ox, oy, oz): index(s, ox, oy, oz)
        for s in range(4)
        for ox in (-1, 0, 1)
        for oy in (-1, 0, 1)
        for oz in (-1, 0, 1)
    }

    def shifted(low, own, high, step):
        row = lax.broadcasted_iota(jnp.int32, own.shape, own.ndim - 2)
        axis = own.ndim - 2
        down = pltpu.roll(jnp.where(row >= 8 - step, low, own), step, axis)
        up = pltpu.roll(jnp.where(row < step, high, own), 8 - step, axis)
        return down, own, up

    def pair(fetch, ox, oy, step):
        for half in (0, 1):
            parts = [
                shifted(*[fetch(where[s, ox, oy, oz]) for oz in (-1, 0, 1)], step)
                for s in (2 * half, 2 * half + 1)
            ]
            for kz in range(3):
                both = jnp.concatenate([parts[0][kz], parts[1][kz]], axis=-2)
                yield slice(16 * half, 16 * half + 16), slice(
                    128 * kz, 128 * kz + 128
                ), both.astype(BF16)

    def fine_centre(source, z):
        def body(m, carry):
            for h in (0, 1):
                for rows, lanes, value in pair(lambda q: source[q, m, h], 0, 0, 1):
                    z[h, m, 1:9, rows, lanes] = value
            return carry

        lax.fori_loop(0, 4, body, 0)

    def x_rim(number, sides, low, high):
        for d in (0, 1):
            for rows, lanes, value in pair(lambda q: sides[d, q], *SIDES[d], number):
                low[d, 1 : high + 1, rows, lanes] = value

    def fine_y_rim():
        for d in (0, 1):
            for rows, lanes, value in pair(
                lambda q: side_src[d + 2, q], *SIDES[d + 2], 1
            ):
                split = value.reshape(4, 2, 16, 128)
                zy[d, 1, 0:4, rows, lanes] = split[:, 0]
                zy[d, 0, 1:5, rows, lanes] = split[:, 1]
        for k, (ox, oy) in enumerate(EDGES):
            at = (0, 0) if ox < 0 else (1, 4)
            for rows, lanes, value in pair(lambda q: edge_src[k, q], ox, oy, 1):
                zy[(0 if oy < 0 else 1,) + at + (rows, lanes)] = value[0]

    def own_sources(source, last, sides, edges):
        for d, (ox, oy) in enumerate(SIDES):
            for s in range(4):
                if oy == 0:
                    sides[d, s] = plane(source, s, edge_of(ox, last))
                else:
                    sides[d, s] = across(source, s, edge_of(oy, last))
        for d, (ox, oy) in enumerate(EDGES):
            for s in range(4):
                edges[d, s, 0] = column(
                    source, s, edge_of(ox, last), edge_of(oy, last)
                )

    def received_sides(which, last, sides, rsides):
        for d in which:
            for s in range(4):
                sides[d, 4 + s] = rsides[d, s].astype(F32).reshape(last + 1, 8, 128)

    def received_edges(last, sides, edges, redges):
        for d, (ox, oy) in enumerate(EDGES):
            dx = SIDES.index((ox, 0))
            dy = SIDES.index((0, oy))
            far = redges[d].astype(F32)
            for s in range(4):
                edges[d, 4 + s, 0] = sides[dx, 4 + s, edge_of(oy, last)]
                edges[d, 8 + s, 0] = sides[dy, 4 + s, edge_of(ox, last)]
                edges[d, 12 + s, 0] = far[8 * s : 8 * s + 8]

    def centre_conv(z, wp, i):
        planes = [(1, i - 1), (0, i), (1, i), (0, i + 1)]
        used = [p for p in range(4) if 0 <= planes[p][1] < 4]
        lhs = jnp.concatenate(
            [
                z[planes[p][0], planes[p][1], ky : ky + 8].reshape(256, 384)
                for ky in range(3)
                for p in used
            ],
            axis=1,
        )
        rhs = jnp.concatenate([wp[p, ky] for ky in range(3) for p in used], axis=0)
        return jnp.dot(lhs, rhs, preferred_element_type=F32)

    def convolve(z, wp, finish):
        for i in range(4):
            acc = centre_conv(z, wp, i)
            for h in (0, 1):
                part = acc[:, 128 * h : 128 * h + 128].reshape(8, 32, 128)
                total[i, h] = part
                if 0 < 2 * i + h < 7:
                    inner = part[1:7].reshape(6, 4, 8, 128)
                    for s in range(4):
                        finish(s, (i, h, slice(1, 7)), inner[:, s])

    def add_x(number, described, wp, finish):
        arrive(described, SIDES[:2])
        received_sides((0, 1), 7, side_src, recv_side.at[number])
        x_rim(1, side_src, zx, 8)
        for d in (0, 1):
            i, h, p = (0, 0, 0) if d == 0 else (3, 1, 3)
            lhs = jnp.concatenate(
                [zx[d, ky : ky + 8].reshape(256, 384) for ky in range(3)], axis=1
            )
            rhs = jnp.concatenate(
                [wp[p, ky][:, 128 * h : 128 * h + 128] for ky in range(3)], axis=0
            )
            add = jnp.dot(lhs, rhs, preferred_element_type=F32).reshape(8, 32, 128)
            part = total[i, h] + add
            for y in (0, 7):
                total[i, h, y] = part[y]
            inner = part[1:7].reshape(6, 4, 8, 128)
            for s in range(4):
                finish(s, (i, h, slice(1, 7)), inner[:, s])

    def add_y(number, described, wp, finish):
        arrive(described, EDGES + SIDES[2:])
        received_sides((2, 3), 7, side_src, recv_side.at[number])
        received_edges(7, side_src, edge_src, recv_edge.at[number])
        fine_y_rim()
        for d in (0, 1):
            y, ky = (0, 0) if d == 0 else (7, 2)
            lhs = jnp.concatenate(
                [
                    zy[d, p % 2, p // 2 : p // 2 + 4].reshape(128, 384)
                    for p in range(4)
                ],
                axis=1,
            )
            rhs = jnp.concatenate([wp[p, ky] for p in range(4)], axis=0)
            add = jnp.dot(lhs, rhs, preferred_element_type=F32)
            for h in (0, 1):
                part = add[:, 128 * h : 128 * h + 128].reshape(4, 32, 128)
                part = (total[:, h, y] + part).reshape(4, 4, 8, 128)
                for s in range(4):
                    finish(s, (slice(0, 4), h, y), part[:, s])

    own_sources(field, 7, side_src, edge_src)
    fine_centre(field, zin)

    copies[4].wait()
    copies[5].wait()
    for copy in copies[6:]:
        copy.start()

    def to_hidden(s, at, value):
        value = jnp.maximum(value + b1[...].reshape(1, 1, 128), 0.0) * live[s]
        hidden[(s,) + at] = value.astype(BF16).astype(F32)

    convolve(zin, w1p, to_hidden)
    add_x(0, sent, w1p, to_hidden)
    add_y(0, sent, w1p, to_hidden)
    sent_hidden = exchange(
        1, hidden, 7, send_side.at[1], send_edge.at[1], recv_side.at[1], recv_edge.at[1]
    )
    start(sent_hidden)
    own_sources(hidden, 7, side_src, edge_src)
    fine_centre(hidden, zhid)

    for k in (6, 7, 8):
        copies[k].wait()

    def to_fine(s, at, value):
        value = value + b2[...].reshape(1, 1, 128) + field[(s,) + at]
        out[(s,) + at] = value * live[s]

    def pooled(value):
        even = lax.broadcasted_iota(jnp.int32, value.shape, 1) % 2 == 0
        other = jnp.where(even, pltpu.roll(value, 7, 1), pltpu.roll(value, 1, 1))
        return ((value + other) * 0.125).astype(BF16).astype(F32)

    def pool(ys):
        for s in range(4):
            for y in ys:
                value = out[s, :, 0, 2 * y] + out[s, :, 1, 2 * y]
                value = value + out[s, :, 0, 2 * y + 1] + out[s, :, 1, 2 * y + 1]
                coarse_field[s, :, y] = pooled(value)

    convolve(zhid, w2p, to_fine)
    add_x(1, sent_hidden, w2p, to_fine)
    pool((1, 2))
    add_y(1, sent_hidden, w2p, to_fine)
    pool((0, 3))
    sent_coarse = exchange(
        2, coarse_field, 3, csend_side, csend_edge, crecv_side, crecv_edge
    )
    start(sent_coarse)

    own_sources(coarse_field, 3, cside_src, cedge_src)
    for x in range(4):
        for rows, lanes, value in pair(lambda q: coarse_field[q, x], 0, 0, 2):
            zc[x + 1, 1:5, rows, lanes] = value
    for k in (9, 10, 11):
        copies[k].wait()
    lhs = jnp.concatenate(
        [
            zc[kx : kx + 4, ky : ky + 4].reshape(512, 384)
            for kx in range(3)
            for ky in range(3)
        ],
        axis=1,
    )
    acc = jnp.dot(lhs, wcv[...], preferred_element_type=F32)
    ctotal[...] = acc.reshape(4, 4, 32, 256)

    def join(ys):
        acc = jnp.concatenate([ctotal[:, y] for y in ys], axis=0)
        acc = jnp.maximum(acc.reshape(-1, 256) + bc[...], 0.0)
        acc = acc.reshape(4 * len(ys), 4, 8, 256)
        acc = jnp.concatenate(
            [(acc[:, s] * live[s])[:, None] for s in range(4)], axis=1
        )
        lifted = jnp.dot(
            acc.reshape(-1, 256).astype(BF16), wlv[...], preferred_element_type=F32
        ).reshape(len(ys), 4, 4, 8, 128)
        for k, y in enumerate(ys):
            for s in range(4):
                raised = lifted[k, :, s]
                for h in (0, 1):
                    for f in (0, 1):
                        at = (s, slice(0, 4), h, 2 * y + f)
                        out[at] = (out[at] + raised) * live[s]

    arrive(sent_coarse, SIDES[:2])
    received_sides((0, 1), 3, cside_src, crecv_side)
    x_rim(2, cside_src, zcx, 4)
    for d in (0, 1):
        lhs = jnp.concatenate(
            [zcx[d, ky : ky + 4].reshape(128, 384) for ky in range(3)], axis=1
        )
        rhs = wcv[2304 * d : 2304 * d + 1152]
        add = jnp.dot(lhs, rhs, preferred_element_type=F32)
        ctotal[3 * d] = ctotal[3 * d] + add.reshape(4, 32, 256)
    join((1, 2))
    arrive(sent_coarse, EDGES + SIDES[2:])
    received_sides((2, 3), 3, cside_src, crecv_side)
    received_edges(3, cside_src, cedge_src, crecv_edge)
    for d in (0, 1):
        for rows, lanes, value in pair(
            lambda q: cside_src[d + 2, q], *SIDES[d + 2], 2
        ):
            zcy[d, 1:5, rows, lanes] = value
    for k, (ox, oy) in enumerate(EDGES):
        for rows, lanes, value in pair(lambda q: cedge_src[k, q], ox, oy, 2):
            zcy[0 if oy < 0 else 1, 0 if ox < 0 else 5, rows, lanes] = value[0]
    for d in (0, 1):
        lhs = jnp.concatenate(
            [zcy[d, kx : kx + 4].reshape(128, 384) for kx in range(3)], axis=1
        )
        rhs = jnp.concatenate(
            [
                wcv[1152 * kx + 768 * d : 1152 * kx + 768 * d + 384]
                for kx in range(3)
            ],
            axis=0,
        )
        add = jnp.dot(lhs, rhs, preferred_element_type=F32)
        ctotal[:, 3 * d] = ctotal[:, 3 * d] + add.reshape(4, 32, 256)
    join((0, 3))
    for described in (sent, sent_hidden, sent_coarse):
        for (ox, oy), copy in described.items():
            when_inside(-ox, -oy, copy.wait_send)


def local(gx, gy, features, slot_cell, neighbours, w1, b1, w2, b2, wc, bc, wl):
    operands = [
        pltpu.with_memory_space_constraint(operand, pltpu.HBM)
        for operand in (
            slot_cell.reshape(4),
            neighbours.reshape(4, 26),
            features.reshape(4, 8, 64, 128),
            w1.reshape(3, 3, 384, 128),
            b1.reshape(1, 128),
            w2.reshape(3, 3, 384, 128),
            b2.reshape(1, 128),
            wc.reshape(3456, 256),
            bc.reshape(1, 256),
            wl,
        )
    ]
    result = pl.pallas_call(
        functools.partial(kernel, gx, gy),
        out_shape=jax.ShapeDtypeStruct((4, 4, 2, 8, 8, 128), F32),
        in_specs=[pl.BlockSpec(memory_space=pl.ANY)] * 10,
        out_specs=pl.BlockSpec(memory_space=pltpu.VMEM),
        scratch_shapes=[
            pltpu.SMEM((4,), jnp.int32),
            pltpu.SMEM((4, 26), jnp.int32),
            pltpu.VMEM((1, 128), F32),
            pltpu.VMEM((1, 128), F32),
            pltpu.VMEM((1, 256), F32),
            pltpu.VMEM((4, 8, 64, 128), BF16),
            pltpu.VMEM((2, 4, 8, 16, 128), BF16),
            pltpu.VMEM((5, 4, 2, 8, 8, 128), F32),
            pltpu.VMEM((5, 4, 2, 8, 8, 128), F32),
            pltpu.VMEM((5, 4, 4, 8, 128), F32),
            pltpu.VMEM((4, 9, 8, 8, 128), F32),
            pltpu.VMEM((4, 17, 1, 8, 128), F32),
            pltpu.VMEM((4, 9, 4, 8, 128), F32),
            pltpu.VMEM((4, 17, 1, 8, 128), F32),
            pltpu.VMEM((2, 4, 10, 32, 384), BF16),
            pltpu.VMEM((2, 4, 10, 32, 384), BF16),
            pltpu.VMEM((2, 10, 32, 384), BF16),
            pltpu.VMEM((2, 2, 5, 32, 384), BF16),
            pltpu.VMEM((6, 6, 32, 384), BF16),
            pltpu.VMEM((2, 6, 32, 384), BF16),
            pltpu.VMEM((2, 6, 32, 384), BF16),
            pltpu.VMEM((4, 3, 384, 256), BF16),
            pltpu.VMEM((4, 3, 384, 256), BF16),
            pltpu.VMEM((3456, 256), BF16),
            pltpu.VMEM((256, 128), BF16),
            pltpu.VMEM((4, 2, 8, 32, 128), F32),
            pltpu.VMEM((4, 4, 32, 256), F32),
            pltpu.VMEM((2, 4, 4, 64, 128), BF16),
            pltpu.VMEM((2, 4, 32, 128), BF16),
            pltpu.VMEM((2, 4, 4, 64, 128), BF16),
            pltpu.VMEM((2, 4, 32, 128), BF16),
            pltpu.VMEM((4, 4, 32, 128), BF16),
            pltpu.VMEM((4, 32, 128), BF16),
            pltpu.VMEM((4, 4, 32, 128), BF16),
            pltpu.VMEM((4, 32, 128), BF16),
            pltpu.SemaphoreType.DMA((12,)),
            pltpu.SemaphoreType.DMA((2,)),
            pltpu.SemaphoreType.DMA((3, 8)),
            pltpu.SemaphoreType.DMA((3, 8)),
        ],
        compiler_params=pltpu.CompilerParams(
            collective_id=0, has_side_effects=True, vmem_limit_bytes=48 * 2**20
        ),
        cost_estimate=pl.CostEstimate(
            flops=8_000_000_000, bytes_accessed=8_000_000, transcendentals=0
        ),
        name="unet_window",
    )(*operands)
    return result.reshape(1, 1, 4, 512, 128)


def solution(mesh):
    placed = (
        P("gx", "gy", None, None, None),
        P("gx", "gy", None),
        P("gx", "gy", None, None),
    ) + (P(),) * 7
    return jax.shard_map(
        functools.partial(local, mesh.shape["gx"], mesh.shape["gy"]),
        mesh=mesh,
        in_specs=placed,
        out_specs=P("gx", "gy", None, None, None),
        check_vma=False,
    )
```

```python
import functools

import jax
import jax.numpy as jnp
from jax import lax
from jax.experimental import pallas as pl
from jax.experimental.pallas import tpu as pltpu
from jax.sharding import PartitionSpec as P

MESH = pl.DeviceIdType.MESH
F32 = jnp.float32
BF16 = jnp.bfloat16

OFFSETS = [
    (ox, oy, oz)
    for ox in (-1, 0, 1)
    for oy in (-1, 0, 1)
    for oz in (-1, 0, 1)
    if (ox, oy, oz) != (0, 0, 0)
]
NUMBER = {offset: k for k, offset in enumerate(OFFSETS)}
SIDES = [(-1, 0), (1, 0), (0, -1), (0, 1)]
EDGES = [(-1, -1), (-1, 1), (1, -1), (1, 1)]
ALL = SIDES + EDGES
FARTHEST = (4, 5, 6, 7, 2, 3, 0, 1)


def edge_of(step, last):
    return last if step < 0 else 0


def kernel(
    gx,
    gy,
    cell_hbm,
    nbr_hbm,
    feat,
    w1,
    b1_hbm,
    w2,
    b2_hbm,
    wc,
    bc_hbm,
    wl,
    out,
    cell,
    nbr,
    b1,
    b2,
    bc,
    staged,
    staged_rim,
    field,
    hidden,
    coarse_field,
    edge_src,
    cedge_src,
    zin,
    zhid,
    zx,
    zy,
    zc,
    zcx,
    zcy,
    w1p,
    w2p,
    wcv,
    wlv,
    total,
    ctotal,
    send_edge,
    recv_edge,
    csend_edge,
    crecv_edge,
    local_sem,
    rim_sem,
    send_sem,
    recv_sem,
    *side_refs,
):
    sides = [side_refs[4 * number : 4 * number + 4] for number in range(3)]
    mx = lax.axis_index("gx")
    my = lax.axis_index("gy")

    def device_at(ox, oy):
        return (lax.rem(mx + ox + gx, gx), lax.rem(my + oy + gy, gy))

    def inside(ox, oy):
        found = None
        for at, step, size in ((mx, ox, gx), (my, oy, gy)):
            if step != 0:
                here = at > 0 if step < 0 else at < size - 1
                found = here if found is None else jnp.logical_and(found, here)
        return found

    def when_inside(ox, oy, act):
        @pl.when(inside(ox, oy))
        def _():
            act()

    def signal_to(ox, oy):
        pl.semaphore_signal(
            barrier, inc=1, device_id=device_at(ox, oy), device_id_type=MESH
        )

    barrier = pltpu.get_barrier_semaphore()
    for k in FARTHEST:
        when_inside(*ALL[k], functools.partial(signal_to, *ALL[k]))
    beside_x = jnp.where(mx > 0, 1, 0) + jnp.where(mx < gx - 1, 1, 0)
    beside_y = jnp.where(my > 0, 1, 0) + jnp.where(my < gy - 1, 1, 0)
    partners = (1 + beside_x) * (1 + beside_y) - 1

    pairs = [
        (feat, staged),
        (cell_hbm, cell),
        (nbr_hbm, nbr),
        (b1_hbm, b1),
        (w1, w1p.at[0:3, :, :, 0:128]),
        (w1, w1p.at[1:4, :, :, 128:256]),
        (w2, w2p.at[0:3, :, :, 0:128]),
        (w2, w2p.at[1:4, :, :, 128:256]),
        (b2_hbm, b2),
        (wc, wcv),
        (wl, wlv),
        (bc_hbm, bc),
    ]
    copies = [
        pltpu.make_async_copy(src, dst, local_sem.at[k])
        for k, (src, dst) in enumerate(pairs)
    ]
    rims = [
        pltpu.make_async_copy(
            feat.at[:, :, 48 * d : 48 * d + 16], staged_rim.at[d], rim_sem.at[d]
        )
        for d in (0, 1)
    ]
    for copy in rims + copies[:6]:
        copy.start()

    for wp in (w1p, w2p):
        wp[3, :, :, 0:128] = jnp.zeros((3, 384, 128), BF16)
        wp[0, :, :, 128:256] = jnp.zeros((3, 384, 128), BF16)
    field[4] = jnp.zeros((4, 2, 8, 8, 128), F32)
    hidden[4] = jnp.zeros((4, 2, 8, 8, 128), F32)
    coarse_field[4] = jnp.zeros((4, 4, 8, 128), F32)
    for d in range(4):
        for number, rows in ((0, 64), (1, 64), (2, 32)):
            sides[number][d][8] = jnp.zeros((rows, 128), BF16)
        edge_src[d, 16] = jnp.zeros((1, 8, 128), F32)
        cedge_src[d, 16] = jnp.zeros((1, 8, 128), F32)
    for z in (zin, zhid):
        z[:, :, 0] = jnp.zeros((2, 4, 32, 384), BF16)
        z[:, :, 9] = jnp.zeros((2, 4, 32, 384), BF16)
    for side in range(2):
        for end in (0, 9):
            zx[side, end] = jnp.zeros((32, 384), BF16)
        for end in (0, 5):
            zcx[side, end] = jnp.zeros((32, 384), BF16)
    for end in (0, 5):
        zc[end] = jnp.zeros((6, 32, 384), BF16)
        zc[:, end] = jnp.zeros((6, 32, 384), BF16)

    for copy in rims:
        copy.wait()

    def plane(source, s, x):
        if source is coarse_field:
            return source[s, x]
        return source[s, x // 2, x % 2]

    def across(source, s, y):
        if source is coarse_field:
            return source[s, :, y]
        if source is field:
            d = y // 7
            return staged_rim[d, s].astype(F32)[:, 8 * d : 8 * d + 8]
        return source[s, :, :, y].reshape(8, 8, 128)

    def column(source, s, x, y):
        if source is coarse_field:
            return source[s, x, y]
        if source is field:
            d = y // 7
            return staged_rim[d, s, x].astype(F32)[8 * d : 8 * d + 8]
        return source[s, x // 2, x % 2, y]

    def pack_side(number, source, last, d):
        ox, oy = SIDES[d]
        for s in range(4):
            if oy == 0:
                face = plane(source, s, edge_of(ox, last))
            else:
                face = across(source, s, edge_of(oy, last))
            sides[number][d][s] = face.reshape(8 * (last + 1), 128).astype(BF16)

    def pack_edges(source, last, edges):
        for d, (ox, oy) in enumerate(EDGES):
            edges[d] = jnp.concatenate(
                [
                    column(source, s, edge_of(ox, last), edge_of(oy, last))
                    for s in range(4)
                ],
                axis=0,
            ).astype(BF16)

    def describe(number, edges, redges):
        described = {}
        for k in FARTHEST:
            ox, oy = ALL[k]
            if k < 4:
                src = sides[number][k].at[0:4]
                dst = sides[number][k].at[4:8]
                if number == 0 and oy == 0:
                    src = feat.at[:, edge_of(ox, 7)]
            else:
                src, dst = edges.at[k - 4], redges.at[k - 4]
            described[ox, oy] = pltpu.make_async_remote_copy(
                src_ref=src,
                dst_ref=dst,
                send_sem=send_sem.at[number, k],
                recv_sem=recv_sem.at[number, k],
                device_id=device_at(-ox, -oy),
                device_id_type=MESH,
            )
        return described

    def start(described, directions):
        for ox, oy in directions:
            when_inside(-ox, -oy, described[ox, oy].start)

    def exchange(number, source, last, edges, redges):
        described = describe(number, edges, redges)
        pack_edges(source, last, edges)
        for d in (2, 3):
            pack_side(number, source, last, d)
        start(described, EDGES + SIDES[2:])
        for d in (0, 1):
            pack_side(number, source, last, d)
        start(described, SIDES[:2])
        return described

    def arrive(described, directions):
        for ox, oy in directions:
            when_inside(ox, oy, described[ox, oy].wait_recv)

    sent = describe(0, send_edge.at[0], recv_edge.at[0])
    pack_edges(field, 7, send_edge.at[0])
    for d in (2, 3):
        pack_side(0, field, 7, d)
    pl.semaphore_wait(barrier, partners)
    start(sent, EDGES + SIDES[2:] + SIDES[:2])
    copies[0].wait()
    for s in range(4):
        for x in range(8):
            field[s, x // 2, x % 2] = staged[s, x].astype(F32).reshape(8, 8, 128)
        for d in (0, 1):
            sides[0][d][s] = staged[s, edge_of(SIDES[d][0], 7)]

    for k in (1, 2, 3):
        copies[k].wait()
    live = [jnp.where(cell[s] >= 0, 1.0, 0.0).astype(F32) for s in range(4)]

    def index(s, ox, oy, oz):
        if (ox, oy, oz) == (0, 0, 0):
            return s
        entry = nbr[s, NUMBER[ox, oy, oz]]
        safe = jnp.maximum(entry, 0)
        block = lax.shift_right_logical(safe, 2)
        slot = lax.bitwise_and(safe, 3)
        if (ox, oy) == (0, 0):
            return jnp.where(entry < 0, 4, slot)
        if ox == 0 or oy == 0:
            place = slot + jnp.where(block == 4, 0, 4)
            return jnp.where(entry < 0, 8, place)
        beside_x = (ox + 1) * 3 + 1
        beside_y = 3 + (oy + 1)
        place = slot + jnp.where(
            block == 4,
            0,
            jnp.where(block == beside_x, 4, jnp.where(block == beside_y, 8, 12)),
        )
        return jnp.where(entry < 0, 16, place)

    where = {
        (s, ox, oy, oz): index(s, ox, oy, oz)
        for s in range(4)
        for ox in (-1, 0, 1)
        for oy in (-1, 0, 1)
        for oz in (-1, 0, 1)
    }

    def shifted(low, own, high, step):
        row = lax.broadcasted_iota(jnp.int32, own.shape, own.ndim - 2)
        axis = own.ndim - 2
        down = pltpu.roll(jnp.where(row >= 8 - step, low, own), step, axis)
        up = pltpu.roll(jnp.where(row < step, high, own), 8 - step, axis)
        return down, own, up

    def pair(fetch, ox, oy, step):
        for half in (0, 1):
            parts = [
                shifted(*[fetch(where[s, ox, oy, oz]) for oz in (-1, 0, 1)], step)
                for s in (2 * half, 2 * half + 1)
            ]
            for kz in range(3):
                both = jnp.concatenate([parts[0][kz], parts[1][kz]], axis=-2)
                yield slice(16 * half, 16 * half + 16), slice(
                    128 * kz, 128 * kz + 128
                ), both.astype(BF16)

    def fine_centre(source, z):
        def body(m, carry):
            for h in (0, 1):
                for rows, lanes, value in pair(lambda q: source[q, m, h], 0, 0, 1):
                    z[h, m, 1:9, rows, lanes] = value
            return carry

        lax.fori_loop(0, 4, body, 0)

    def face(number, d):
        def fetch(q):
            value = sides[number][d][q].astype(F32)
            return value.reshape(value.shape[0] // 8, 8, 128)

        return fetch

    def own_edges(source, last, edges):
        for d, (ox, oy) in enumerate(EDGES):
            for s in range(4):
                edges[d, s, 0] = column(
                    source, s, edge_of(ox, last), edge_of(oy, last)
                )

    def end_of(number, d, s, step):
        ref = sides[number][d]
        if step < 0:
            rows = ref.shape[1]
            return ref[4 + s, rows - 16 : rows].astype(F32)[8:16]
        return ref[4 + s, 0:16].astype(F32)[0:8]

    def edges_beside_x(number, edges):
        for k, (ox, oy) in enumerate(EDGES):
            for s in range(4):
                edges[k, 4 + s, 0] = end_of(number, SIDES.index((ox, 0)), s, oy)

    def edges_beside_y(number, edges, redges):
        for k, (ox, oy) in enumerate(EDGES):
            far = redges[k].astype(F32)
            for s in range(4):
                edges[k, 8 + s, 0] = end_of(number, SIDES.index((0, oy)), s, ox)
                edges[k, 12 + s, 0] = far[8 * s : 8 * s + 8]

    def y_rim(number, step, last, edges, rim):
        for d in (0, 1):
            for rows, lanes, value in pair(
                face(number, d + 2), *SIDES[d + 2], step
            ):
                rim[d, 1 : last + 2, rows, lanes] = value
        for k, (ox, oy) in enumerate(EDGES):
            x = 0 if ox < 0 else last + 2
            for rows, lanes, value in pair(lambda q: edges[k, q], ox, oy, step):
                rim[0 if oy < 0 else 1, x, rows, lanes] = value[0]

    def x_rim(number, step, last, rim):
        for d in (0, 1):
            for rows, lanes, value in pair(face(number, d), *SIDES[d], step):
                rim[d, 1 : last + 2, rows, lanes] = value

    def centre_conv(z, wp, i):
        planes = [(1, i - 1), (0, i), (1, i), (0, i + 1)]
        used = [p for p in range(4) if 0 <= planes[p][1] < 4]
        lhs = jnp.concatenate(
            [
                z[planes[p][0], planes[p][1], ky : ky + 8].reshape(256, 384)
                for ky in range(3)
                for p in used
            ],
            axis=1,
        )
        rhs = jnp.concatenate([wp[p, ky] for ky in range(3) for p in used], axis=0)
        return jnp.dot(lhs, rhs, preferred_element_type=F32)

    def convolve(z, wp, finish):
        for i in range(4):
            acc = centre_conv(z, wp, i)
            for h in (0, 1):
                part = acc[:, 128 * h : 128 * h + 128].reshape(8, 32, 128)
                total[i, h] = part
                if 0 < 2 * i + h < 7:
                    inner = part[1:7].reshape(6, 4, 8, 128)
                    for s in range(4):
                        finish(s, (i, h, slice(1, 7)), inner[:, s])

    def add_x(number, described, wp, finish):
        arrive(described, SIDES[:2])
        x_rim(number, 1, 7, zx)
        edges_beside_x(number, edge_src)
        for d in (0, 1):
            i, h, p = (0, 0, 0) if d == 0 else (3, 1, 3)
            lhs = jnp.concatenate(
                [zx[d, ky : ky + 8].reshape(256, 384) for ky in range(3)], axis=1
            )
            rhs = jnp.concatenate(
                [wp[p, ky][:, 128 * h : 128 * h + 128] for ky in range(3)], axis=0
            )
            add = jnp.dot(lhs, rhs, preferred_element_type=F32).reshape(8, 32, 128)
            part = total[i, h] + add
            for y in (0, 7):
                total[i, h, y] = part[y]
            inner = part[1:7].reshape(6, 4, 8, 128)
            for s in range(4):
                finish(s, (i, h, slice(1, 7)), inner[:, s])

    def add_y(number, described, wp, finish):
        arrive(described, EDGES + SIDES[2:])
        edges_beside_y(number, edge_src, recv_edge.at[number])
        y_rim(number, 1, 7, edge_src, zy)
        for d in (0, 1):
            y, ky = (0, 0) if d == 0 else (7, 2)
            lhs = jnp.concatenate(
                [zy[d, kx : kx + 8].reshape(256, 384) for kx in range(3)], axis=1
            )
            rhs = jnp.concatenate([wp[kx, ky][:, 0:128] for kx in range(3)], axis=0)
            add = jnp.dot(lhs, rhs, preferred_element_type=F32)
            part = total[:, :, y] + add.reshape(4, 2, 32, 128)
            part = part.reshape(4, 2, 4, 8, 128)
            for s in range(4):
                finish(s, (slice(0, 4), slice(0, 2), y), part[:, :, s])

    own_edges(field, 7, edge_src)
    fine_centre(field, zin)

    copies[4].wait()
    copies[5].wait()
    for copy in copies[6:]:
        copy.start()

    def to_hidden(s, at, value):
        value = jnp.maximum(value + b1[...].reshape(1, 1, 128), 0.0) * live[s]
        hidden[(s,) + at] = value.astype(BF16).astype(F32)

    convolve(zin, w1p, to_hidden)
    add_x(0, sent, w1p, to_hidden)
    add_y(0, sent, w1p, to_hidden)
    sent_hidden = exchange(1, hidden, 7, send_edge.at[1], recv_edge.at[1])
    own_edges(hidden, 7, edge_src)
    fine_centre(hidden, zhid)

    for k in (6, 7, 8):
        copies[k].wait()

    def to_fine(s, at, value):
        value = value + b2[...].reshape(1, 1, 128) + field[(s,) + at]
        out[(s,) + at] = value * live[s]

    def pooled(value):
        even = lax.broadcasted_iota(jnp.int32, value.shape, 1) % 2 == 0
        other = jnp.where(even, pltpu.roll(value, 7, 1), pltpu.roll(value, 1, 1))
        return ((value + other) * 0.125).astype(BF16).astype(F32)

    def pool(ys):
        for s in range(4):
            for y in ys:
                value = out[s, :, 0, 2 * y] + out[s, :, 1, 2 * y]
                value = value + out[s, :, 0, 2 * y + 1] + out[s, :, 1, 2 * y + 1]
                coarse_field[s, :, y] = pooled(value)

    convolve(zhid, w2p, to_fine)
    add_x(1, sent_hidden, w2p, to_fine)
    pool((1, 2))
    add_y(1, sent_hidden, w2p, to_fine)
    pool((0, 3))
    sent_coarse = exchange(2, coarse_field, 3, csend_edge, crecv_edge)

    own_edges(coarse_field, 3, cedge_src)
    for x in range(4):
        for rows, lanes, value in pair(lambda q: coarse_field[q, x], 0, 0, 2):
            zc[x + 1, 1:5, rows, lanes] = value
    for k in (9, 10, 11):
        copies[k].wait()
    lhs = jnp.concatenate(
        [
            zc[kx : kx + 4, ky : ky + 4].reshape(512, 384)
            for kx in range(3)
            for ky in range(3)
        ],
        axis=1,
    )
    acc = jnp.dot(lhs, wcv[...], preferred_element_type=F32)
    ctotal[...] = acc.reshape(4, 4, 32, 256)

    def join(ys):
        acc = jnp.concatenate([ctotal[:, y] for y in ys], axis=0)
        acc = jnp.maximum(acc.reshape(-1, 256) + bc[...], 0.0)
        acc = acc.reshape(4 * len(ys), 4, 8, 256)
        acc = jnp.concatenate(
            [(acc[:, s] * live[s])[:, None] for s in range(4)], axis=1
        )
        lifted = jnp.dot(
            acc.reshape(-1, 256).astype(BF16), wlv[...], preferred_element_type=F32
        ).reshape(len(ys), 4, 4, 8, 128)
        for k, y in enumerate(ys):
            for s in range(4):
                raised = lifted[k, :, s]
                for h in (0, 1):
                    for f in (0, 1):
                        at = (s, slice(0, 4), h, 2 * y + f)
                        out[at] = (out[at] + raised) * live[s]

    arrive(sent_coarse, SIDES[:2])
    x_rim(2, 2, 3, zcx)
    edges_beside_x(2, cedge_src)
    for d in (0, 1):
        lhs = jnp.concatenate(
            [zcx[d, ky : ky + 4].reshape(128, 384) for ky in range(3)], axis=1
        )
        rhs = wcv[2304 * d : 2304 * d + 1152]
        add = jnp.dot(lhs, rhs, preferred_element_type=F32)
        ctotal[3 * d] = ctotal[3 * d] + add.reshape(4, 32, 256)
    join((1, 2))
    arrive(sent_coarse, EDGES + SIDES[2:])
    edges_beside_y(2, cedge_src, crecv_edge)
    y_rim(2, 2, 3, cedge_src, zcy)
    for d in (0, 1):
        lhs = jnp.concatenate(
            [zcy[d, kx : kx + 4].reshape(128, 384) for kx in range(3)], axis=1
        )
        rhs = jnp.concatenate(
            [
                wcv[1152 * kx + 768 * d : 1152 * kx + 768 * d + 384]
                for kx in range(3)
            ],
            axis=0,
        )
        add = jnp.dot(lhs, rhs, preferred_element_type=F32)
        ctotal[:, 3 * d] = ctotal[:, 3 * d] + add.reshape(4, 32, 256)
    join((0, 3))
    for described in (sent, sent_hidden, sent_coarse):
        for (ox, oy), copy in described.items():
            when_inside(-ox, -oy, copy.wait_send)


def local(gx, gy, features, slot_cell, neighbours, w1, b1, w2, b2, wc, bc, wl):
    operands = [
        pltpu.with_memory_space_constraint(operand, pltpu.HBM)
        for operand in (
            slot_cell.reshape(4),
            neighbours.reshape(4, 26),
            features.reshape(4, 8, 64, 128),
            w1.reshape(3, 3, 384, 128),
            b1.reshape(1, 128),
            w2.reshape(3, 3, 384, 128),
            b2.reshape(1, 128),
            wc.reshape(3456, 256),
            bc.reshape(1, 256),
            wl,
        )
    ]
    result = pl.pallas_call(
        functools.partial(kernel, gx, gy),
        out_shape=jax.ShapeDtypeStruct((4, 4, 2, 8, 8, 128), F32),
        in_specs=[pl.BlockSpec(memory_space=pl.ANY)] * 10,
        out_specs=pl.BlockSpec(memory_space=pltpu.VMEM),
        scratch_shapes=[
            pltpu.SMEM((4,), jnp.int32),
            pltpu.SMEM((4, 26), jnp.int32),
            pltpu.VMEM((1, 128), F32),
            pltpu.VMEM((1, 128), F32),
            pltpu.VMEM((1, 256), F32),
            pltpu.VMEM((4, 8, 64, 128), BF16),
            pltpu.VMEM((2, 4, 8, 16, 128), BF16),
            pltpu.VMEM((5, 4, 2, 8, 8, 128), F32),
            pltpu.VMEM((5, 4, 2, 8, 8, 128), F32),
            pltpu.VMEM((5, 4, 4, 8, 128), F32),
            pltpu.VMEM((4, 17, 1, 8, 128), F32),
            pltpu.VMEM((4, 17, 1, 8, 128), F32),
            pltpu.VMEM((2, 4, 10, 32, 384), BF16),
            pltpu.VMEM((2, 4, 10, 32, 384), BF16),
            pltpu.VMEM((2, 10, 32, 384), BF16),
            pltpu.VMEM((2, 10, 32, 384), BF16),
            pltpu.VMEM((6, 6, 32, 384), BF16),
            pltpu.VMEM((2, 6, 32, 384), BF16),
            pltpu.VMEM((2, 6, 32, 384), BF16),
            pltpu.VMEM((4, 3, 384, 256), BF16),
            pltpu.VMEM((4, 3, 384, 256), BF16),
            pltpu.VMEM((3456, 256), BF16),
            pltpu.VMEM((256, 128), BF16),
            pltpu.VMEM((4, 2, 8, 32, 128), F32),
            pltpu.VMEM((4, 4, 32, 256), F32),
            pltpu.VMEM((2, 4, 32, 128), BF16),
            pltpu.VMEM((2, 4, 32, 128), BF16),
            pltpu.VMEM((4, 32, 128), BF16),
            pltpu.VMEM((4, 32, 128), BF16),
            pltpu.SemaphoreType.DMA((12,)),
            pltpu.SemaphoreType.DMA((2,)),
            pltpu.SemaphoreType.DMA((3, 8)),
            pltpu.SemaphoreType.DMA((3, 8)),
        ]
        + [pltpu.VMEM((9, 64, 128), BF16)] * 8
        + [pltpu.VMEM((9, 32, 128), BF16)] * 4,
        compiler_params=pltpu.CompilerParams(
            collective_id=0, has_side_effects=True, vmem_limit_bytes=48 * 2**20
        ),
        cost_estimate=pl.CostEstimate(
            flops=8_000_000_000, bytes_accessed=8_000_000, transcendentals=0
        ),
        name="unet_window",
    )(*operands)
    return result.reshape(1, 1, 4, 512, 128)


def solution(mesh):
    placed = (
        P("gx", "gy", None, None, None),
        P("gx", "gy", None),
        P("gx", "gy", None, None),
    ) + (P(),) * 7
    return jax.shard_map(
        functools.partial(local, mesh.shape["gx"], mesh.shape["gy"]),
        mesh=mesh,
        in_specs=placed,
        out_specs=P("gx", "gy", None, None, None),
        check_vma=False,
    )
```

```python
import functools

import jax
import jax.numpy as jnp
from jax import lax
from jax.experimental import pallas as pl
from jax.experimental.pallas import tpu as pltpu
from jax.sharding import PartitionSpec as P

MESH = pl.DeviceIdType.MESH
F32 = jnp.float32
BF16 = jnp.bfloat16

OFFSETS = [
    (ox, oy, oz)
    for ox in (-1, 0, 1)
    for oy in (-1, 0, 1)
    for oz in (-1, 0, 1)
    if (ox, oy, oz) != (0, 0, 0)
]
NUMBER = {offset: k for k, offset in enumerate(OFFSETS)}
SIDES = [(-1, 0), (1, 0), (0, -1), (0, 1)]
EDGES = [(-1, -1), (-1, 1), (1, -1), (1, 1)]
ALL = SIDES + EDGES
FARTHEST = (4, 5, 6, 7, 2, 3, 0, 1)


def edges_on(oy):
    return [(k, edge) for k, edge in enumerate(EDGES) if edge[1] == oy]


def edge_of(step, last):
    return last if step < 0 else 0


def kernel(
    gx,
    gy,
    cell_hbm,
    nbr_hbm,
    feat,
    w1,
    b1_hbm,
    w2,
    b2_hbm,
    wc,
    bc_hbm,
    wl,
    out,
    cell,
    nbr,
    b1,
    b2,
    bc,
    staged,
    staged_rim,
    field,
    hidden,
    coarse_field,
    edge_src,
    cedge_src,
    zin,
    zhid,
    zx,
    zy,
    zc,
    zcx,
    zcy,
    w1p,
    w2p,
    wcv,
    wlv,
    total,
    ctotal,
    send_edge,
    recv_edge,
    csend_edge,
    crecv_edge,
    local_sem,
    rim_sem,
    send_sem,
    recv_sem,
    *side_refs,
):
    sides = [side_refs[4 * number : 4 * number + 4] for number in range(3)]
    mx = lax.axis_index("gx")
    my = lax.axis_index("gy")

    def device_at(ox, oy):
        return (lax.rem(mx + ox + gx, gx), lax.rem(my + oy + gy, gy))

    def inside(ox, oy):
        found = None
        for at, step, size in ((mx, ox, gx), (my, oy, gy)):
            if step != 0:
                here = at > 0 if step < 0 else at < size - 1
                found = here if found is None else jnp.logical_and(found, here)
        return found

    def when_inside(ox, oy, act):
        @pl.when(inside(ox, oy))
        def _():
            act()

    def signal_to(ox, oy):
        pl.semaphore_signal(
            barrier, inc=1, device_id=device_at(ox, oy), device_id_type=MESH
        )

    barrier = pltpu.get_barrier_semaphore()
    for k in FARTHEST:
        when_inside(*ALL[k], functools.partial(signal_to, *ALL[k]))
    beside_x = jnp.where(mx > 0, 1, 0) + jnp.where(mx < gx - 1, 1, 0)
    beside_y = jnp.where(my > 0, 1, 0) + jnp.where(my < gy - 1, 1, 0)
    partners = (1 + beside_x) * (1 + beside_y) - 1

    pairs = [
        (feat, staged),
        (cell_hbm, cell),
        (nbr_hbm, nbr),
        (b1_hbm, b1),
        (w1, w1p.at[0:3, :, :, 0:128]),
        (w1, w1p.at[1:4, :, :, 128:256]),
        (w2, w2p.at[0:3, :, :, 0:128]),
        (w2, w2p.at[1:4, :, :, 128:256]),
        (b2_hbm, b2),
        (wc, wcv),
        (wl, wlv),
        (bc_hbm, bc),
    ]
    copies = [
        pltpu.make_async_copy(src, dst, local_sem.at[k])
        for k, (src, dst) in enumerate(pairs)
    ]
    rims = [
        pltpu.make_async_copy(
            feat.at[:, :, 48 * d : 48 * d + 16], staged_rim.at[d], rim_sem.at[d]
        )
        for d in (0, 1)
    ]
    for copy in rims + copies[:6]:
        copy.start()

    for wp in (w1p, w2p):
        wp[3, :, :, 0:128] = jnp.zeros((3, 384, 128), BF16)
        wp[0, :, :, 128:256] = jnp.zeros((3, 384, 128), BF16)
    field[4] = jnp.zeros((4, 2, 8, 8, 128), F32)
    hidden[4] = jnp.zeros((4, 2, 8, 8, 128), F32)
    coarse_field[4] = jnp.zeros((4, 4, 8, 128), F32)
    for d in range(4):
        for number, rows in ((0, 64), (1, 64), (2, 32)):
            sides[number][d][8] = jnp.zeros((rows, 128), BF16)
        edge_src[d, 16] = jnp.zeros((1, 8, 128), F32)
        cedge_src[d, 16] = jnp.zeros((1, 8, 128), F32)
    for z in (zin, zhid):
        z[:, :, 0] = jnp.zeros((2, 4, 32, 384), BF16)
        z[:, :, 9] = jnp.zeros((2, 4, 32, 384), BF16)
    for side in range(2):
        for end in (0, 9):
            zx[side, end] = jnp.zeros((32, 384), BF16)
        for end in (0, 5):
            zcx[side, end] = jnp.zeros((32, 384), BF16)
    for end in (0, 5):
        zc[end] = jnp.zeros((6, 32, 384), BF16)
        zc[:, end] = jnp.zeros((6, 32, 384), BF16)

    for copy in rims:
        copy.wait()

    def plane(source, s, x):
        if source is coarse_field:
            return source[s, x]
        return source[s, x // 2, x % 2]

    def across(source, s, y):
        if source is coarse_field:
            return source[s, :, y]
        if source is field:
            d = y // 7
            return staged_rim[d, s].astype(F32)[:, 8 * d : 8 * d + 8]
        return source[s, :, :, y].reshape(8, 8, 128)

    def column(source, s, x, y):
        if source is coarse_field:
            return source[s, x, y]
        if source is field:
            d = y // 7
            return staged_rim[d, s, x].astype(F32)[8 * d : 8 * d + 8]
        return source[s, x // 2, x % 2, y]

    def pack_side(number, source, last, d):
        ox, oy = SIDES[d]
        for s in range(4):
            if oy == 0:
                face = plane(source, s, edge_of(ox, last))
            else:
                face = across(source, s, edge_of(oy, last))
            sides[number][d][s] = face.reshape(8 * (last + 1), 128).astype(BF16)

    def pack_edges(source, last, edges, oy):
        for d, (ox, oy) in edges_on(oy):
            edges[d] = jnp.concatenate(
                [
                    column(source, s, edge_of(ox, last), edge_of(oy, last))
                    for s in range(4)
                ],
                axis=0,
            ).astype(BF16)

    def describe(number, edges, redges):
        described = {}
        for k in FARTHEST:
            ox, oy = ALL[k]
            if k < 4:
                src = sides[number][k].at[0:4]
                dst = sides[number][k].at[4:8]
                if number == 0 and oy == 0:
                    src = feat.at[:, edge_of(ox, 7)]
            else:
                src, dst = edges.at[k - 4], redges.at[k - 4]
            described[ox, oy] = pltpu.make_async_remote_copy(
                src_ref=src,
                dst_ref=dst,
                send_sem=send_sem.at[number, k],
                recv_sem=recv_sem.at[number, k],
                device_id=device_at(-ox, -oy),
                device_id_type=MESH,
            )
        return described

    def start(described, directions):
        for ox, oy in directions:
            when_inside(-ox, -oy, described[ox, oy].start)

    def leave_y(number, described, source, last, edges, d):
        oy = 1 - 2 * d
        pack_edges(source, last, edges, oy)
        pack_side(number, source, last, 3 - d)
        start(described, [edge for _, edge in edges_on(oy)] + [(0, oy)])

    def leave_x(number, described, source, last):
        for d in (0, 1):
            pack_side(number, source, last, d)
        start(described, SIDES[:2])

    def arrive(described, directions):
        for ox, oy in directions:
            when_inside(ox, oy, described[ox, oy].wait_recv)

    sent = describe(0, send_edge.at[0], recv_edge.at[0])
    for oy in (-1, 1):
        pack_edges(field, 7, send_edge.at[0], oy)
    for d in (2, 3):
        pack_side(0, field, 7, d)
    pl.semaphore_wait(barrier, partners)
    start(sent, EDGES + SIDES[2:] + SIDES[:2])
    copies[0].wait()
    for s in range(4):
        for x in range(8):
            field[s, x // 2, x % 2] = staged[s, x].astype(F32).reshape(8, 8, 128)
        for d in (0, 1):
            sides[0][d][s] = staged[s, edge_of(SIDES[d][0], 7)]

    for k in (1, 2, 3):
        copies[k].wait()
    live = [jnp.where(cell[s] >= 0, 1.0, 0.0).astype(F32) for s in range(4)]

    def index(s, ox, oy, oz):
        if (ox, oy, oz) == (0, 0, 0):
            return s
        entry = nbr[s, NUMBER[ox, oy, oz]]
        safe = jnp.maximum(entry, 0)
        block = lax.shift_right_logical(safe, 2)
        slot = lax.bitwise_and(safe, 3)
        if (ox, oy) == (0, 0):
            return jnp.where(entry < 0, 4, slot)
        if ox == 0 or oy == 0:
            place = slot + jnp.where(block == 4, 0, 4)
            return jnp.where(entry < 0, 8, place)
        beside_x = (ox + 1) * 3 + 1
        beside_y = 3 + (oy + 1)
        place = slot + jnp.where(
            block == 4,
            0,
            jnp.where(block == beside_x, 4, jnp.where(block == beside_y, 8, 12)),
        )
        return jnp.where(entry < 0, 16, place)

    where = {
        (s, ox, oy, oz): index(s, ox, oy, oz)
        for s in range(4)
        for ox in (-1, 0, 1)
        for oy in (-1, 0, 1)
        for oz in (-1, 0, 1)
    }

    def shifted(low, own, high, step):
        row = lax.broadcasted_iota(jnp.int32, own.shape, own.ndim - 2)
        axis = own.ndim - 2
        down = pltpu.roll(jnp.where(row >= 8 - step, low, own), step, axis)
        up = pltpu.roll(jnp.where(row < step, high, own), 8 - step, axis)
        return down, own, up

    def pair(fetch, ox, oy, step):
        for half in (0, 1):
            parts = [
                shifted(*[fetch(where[s, ox, oy, oz]) for oz in (-1, 0, 1)], step)
                for s in (2 * half, 2 * half + 1)
            ]
            for kz in range(3):
                both = jnp.concatenate([parts[0][kz], parts[1][kz]], axis=-2)
                yield slice(16 * half, 16 * half + 16), slice(
                    128 * kz, 128 * kz + 128
                ), both.astype(BF16)

    def fine_centre(source, z):
        def body(m, carry):
            for h in (0, 1):
                for rows, lanes, value in pair(lambda q: source[q, m, h], 0, 0, 1):
                    z[h, m, 1:9, rows, lanes] = value
            return carry

        lax.fori_loop(0, 4, body, 0)

    def face(number, d):
        def fetch(q):
            value = sides[number][d][q].astype(F32)
            return value.reshape(value.shape[0] // 8, 8, 128)

        return fetch

    def own_edges(source, last, edges):
        for d, (ox, oy) in enumerate(EDGES):
            for s in range(4):
                edges[d, s, 0] = column(
                    source, s, edge_of(ox, last), edge_of(oy, last)
                )

    def end_of(number, d, s, step):
        ref = sides[number][d]
        if step < 0:
            rows = ref.shape[1]
            return ref[4 + s, rows - 16 : rows].astype(F32)[8:16]
        return ref[4 + s, 0:16].astype(F32)[0:8]

    def edges_beside_x(number, edges):
        for k, (ox, oy) in enumerate(EDGES):
            for s in range(4):
                edges[k, 4 + s, 0] = end_of(number, SIDES.index((ox, 0)), s, oy)

    def edges_beside_y(number, edges, redges, d):
        for k, (ox, oy) in edges_on(2 * d - 1):
            far = redges[k].astype(F32)
            for s in range(4):
                edges[k, 8 + s, 0] = end_of(number, d + 2, s, ox)
                edges[k, 12 + s, 0] = far[8 * s : 8 * s + 8]

    def y_rim(number, step, last, edges, rim, d):
        for rows, lanes, value in pair(face(number, d + 2), *SIDES[d + 2], step):
            rim[d, 1 : last + 2, rows, lanes] = value
        for k, (ox, oy) in edges_on(2 * d - 1):
            x = 0 if ox < 0 else last + 2
            for rows, lanes, value in pair(lambda q: edges[k, q], ox, oy, step):
                rim[d, x, rows, lanes] = value[0]

    def arrive_y(described, d):
        arrive(described, [edge for _, edge in edges_on(2 * d - 1)] + [SIDES[d + 2]])

    def by_turns(step):
        far_low = lax.rem(my, 4) == 0

        @pl.when(far_low)
        def _():
            step(1)

        step(0)

        @pl.when(jnp.logical_not(far_low))
        def _():
            step(1)

    def x_rim(number, step, last, rim):
        for d in (0, 1):
            for rows, lanes, value in pair(face(number, d), *SIDES[d], step):
                rim[d, 1 : last + 2, rows, lanes] = value

    def centre_conv(z, wp, i):
        planes = [(1, i - 1), (0, i), (1, i), (0, i + 1)]
        used = [p for p in range(4) if 0 <= planes[p][1] < 4]
        lhs = jnp.concatenate(
            [
                z[planes[p][0], planes[p][1], ky : ky + 8].reshape(256, 384)
                for ky in range(3)
                for p in used
            ],
            axis=1,
        )
        rhs = jnp.concatenate([wp[p, ky] for ky in range(3) for p in used], axis=0)
        return jnp.dot(lhs, rhs, preferred_element_type=F32)

    def convolve(z, wp, finish):
        for i in range(4):
            acc = centre_conv(z, wp, i)
            for h in (0, 1):
                part = acc[:, 128 * h : 128 * h + 128].reshape(8, 32, 128)
                total[i, h] = part
                if 0 < 2 * i + h < 7:
                    inner = part[1:7].reshape(6, 4, 8, 128)
                    for s in range(4):
                        finish(s, (i, h, slice(1, 7)), inner[:, s])

    def add_x(number, described, wp, finish):
        arrive(described, SIDES[:2])
        x_rim(number, 1, 7, zx)
        edges_beside_x(number, edge_src)
        for d in (0, 1):
            i, h, p = (0, 0, 0) if d == 0 else (3, 1, 3)
            lhs = jnp.concatenate(
                [zx[d, ky : ky + 8].reshape(256, 384) for ky in range(3)], axis=1
            )
            rhs = jnp.concatenate(
                [wp[p, ky][:, 128 * h : 128 * h + 128] for ky in range(3)], axis=0
            )
            add = jnp.dot(lhs, rhs, preferred_element_type=F32).reshape(8, 32, 128)
            part = total[i, h] + add
            for y in (0, 7):
                total[i, h, y] = part[y]
            inner = part[1:7].reshape(6, 4, 8, 128)
            for s in range(4):
                finish(s, (i, h, slice(1, 7)), inner[:, s])

    def add_y(number, described, wp, finish, after):
        def step(d):
            arrive_y(described, d)
            edges_beside_y(number, edge_src, recv_edge.at[number], d)
            y_rim(number, 1, 7, edge_src, zy, d)
            y, ky = (0, 0) if d == 0 else (7, 2)
            lhs = jnp.concatenate(
                [zy[d, kx : kx + 8].reshape(256, 384) for kx in range(3)], axis=1
            )
            rhs = jnp.concatenate([wp[kx, ky][:, 0:128] for kx in range(3)], axis=0)
            add = jnp.dot(lhs, rhs, preferred_element_type=F32)
            part = total[:, :, y] + add.reshape(4, 2, 32, 128)
            part = part.reshape(4, 2, 4, 8, 128)
            for s in range(4):
                finish(s, (slice(0, 4), slice(0, 2), y), part[:, :, s])
            after(d)

        by_turns(step)

    own_edges(field, 7, edge_src)
    fine_centre(field, zin)

    copies[4].wait()
    copies[5].wait()
    for copy in copies[6:]:
        copy.start()

    def to_hidden(s, at, value):
        value = jnp.maximum(value + b1[...].reshape(1, 1, 128), 0.0) * live[s]
        hidden[(s,) + at] = value.astype(BF16).astype(F32)

    convolve(zin, w1p, to_hidden)
    add_x(0, sent, w1p, to_hidden)
    sent_hidden = describe(1, send_edge.at[1], recv_edge.at[1])
    add_y(
        0,
        sent,
        w1p,
        to_hidden,
        lambda d: leave_y(1, sent_hidden, hidden, 7, send_edge.at[1], d),
    )
    leave_x(1, sent_hidden, hidden, 7)
    own_edges(hidden, 7, edge_src)
    fine_centre(hidden, zhid)

    for k in (6, 7, 8):
        copies[k].wait()

    def to_fine(s, at, value):
        value = value + b2[...].reshape(1, 1, 128) + field[(s,) + at]
        out[(s,) + at] = value * live[s]

    def pooled(value):
        even = lax.broadcasted_iota(jnp.int32, value.shape, 1) % 2 == 0
        other = jnp.where(even, pltpu.roll(value, 7, 1), pltpu.roll(value, 1, 1))
        return ((value + other) * 0.125).astype(BF16).astype(F32)

    def pool(ys):
        for s in range(4):
            for y in ys:
                value = out[s, :, 0, 2 * y] + out[s, :, 1, 2 * y]
                value = value + out[s, :, 0, 2 * y + 1] + out[s, :, 1, 2 * y + 1]
                coarse_field[s, :, y] = pooled(value)

    convolve(zhid, w2p, to_fine)
    add_x(1, sent_hidden, w2p, to_fine)
    pool((1, 2))
    sent_coarse = describe(2, csend_edge, crecv_edge)

    def to_coarse(d):
        pool((3 * d,))
        leave_y(2, sent_coarse, coarse_field, 3, csend_edge, d)

    add_y(1, sent_hidden, w2p, to_fine, to_coarse)
    leave_x(2, sent_coarse, coarse_field, 3)

    own_edges(coarse_field, 3, cedge_src)
    for x in range(4):
        for rows, lanes, value in pair(lambda q: coarse_field[q, x], 0, 0, 2):
            zc[x + 1, 1:5, rows, lanes] = value
    for k in (9, 10, 11):
        copies[k].wait()
    lhs = jnp.concatenate(
        [
            zc[kx : kx + 4, ky : ky + 4].reshape(512, 384)
            for kx in range(3)
            for ky in range(3)
        ],
        axis=1,
    )
    acc = jnp.dot(lhs, wcv[...], preferred_element_type=F32)
    ctotal[...] = acc.reshape(4, 4, 32, 256)

    def join(ys):
        acc = jnp.concatenate([ctotal[:, y] for y in ys], axis=0)
        acc = jnp.maximum(acc.reshape(-1, 256) + bc[...], 0.0)
        acc = acc.reshape(4 * len(ys), 4, 8, 256)
        acc = jnp.concatenate(
            [(acc[:, s] * live[s])[:, None] for s in range(4)], axis=1
        )
        lifted = jnp.dot(
            acc.reshape(-1, 256).astype(BF16), wlv[...], preferred_element_type=F32
        ).reshape(len(ys), 4, 4, 8, 128)
        for k, y in enumerate(ys):
            for s in range(4):
                raised = lifted[k, :, s]
                for h in (0, 1):
                    for f in (0, 1):
                        at = (s, slice(0, 4), h, 2 * y + f)
                        out[at] = (out[at] + raised) * live[s]

    arrive(sent_coarse, SIDES[:2])
    x_rim(2, 2, 3, zcx)
    edges_beside_x(2, cedge_src)
    for d in (0, 1):
        lhs = jnp.concatenate(
            [zcx[d, ky : ky + 4].reshape(128, 384) for ky in range(3)], axis=1
        )
        rhs = wcv[2304 * d : 2304 * d + 1152]
        add = jnp.dot(lhs, rhs, preferred_element_type=F32)
        ctotal[3 * d] = ctotal[3 * d] + add.reshape(4, 32, 256)
    join((1, 2))

    def coarse_y(d):
        arrive_y(sent_coarse, d)
        edges_beside_y(2, cedge_src, crecv_edge, d)
        y_rim(2, 2, 3, cedge_src, zcy, d)
        lhs = jnp.concatenate(
            [zcy[d, kx : kx + 4].reshape(128, 384) for kx in range(3)], axis=1
        )
        rhs = jnp.concatenate(
            [
                wcv[1152 * kx + 768 * d : 1152 * kx + 768 * d + 384]
                for kx in range(3)
            ],
            axis=0,
        )
        add = jnp.dot(lhs, rhs, preferred_element_type=F32)
        ctotal[:, 3 * d] = ctotal[:, 3 * d] + add.reshape(4, 32, 256)
        join((3 * d,))

    by_turns(coarse_y)
    for described in (sent, sent_hidden, sent_coarse):
        for (ox, oy), copy in described.items():
            when_inside(-ox, -oy, copy.wait_send)


def local(gx, gy, features, slot_cell, neighbours, w1, b1, w2, b2, wc, bc, wl):
    operands = [
        pltpu.with_memory_space_constraint(operand, pltpu.HBM)
        for operand in (
            slot_cell.reshape(4),
            neighbours.reshape(4, 26),
            features.reshape(4, 8, 64, 128),
            w1.reshape(3, 3, 384, 128),
            b1.reshape(1, 128),
            w2.reshape(3, 3, 384, 128),
            b2.reshape(1, 128),
            wc.reshape(3456, 256),
            bc.reshape(1, 256),
            wl,
        )
    ]
    result = pl.pallas_call(
        functools.partial(kernel, gx, gy),
        out_shape=jax.ShapeDtypeStruct((4, 4, 2, 8, 8, 128), F32),
        in_specs=[pl.BlockSpec(memory_space=pl.ANY)] * 10,
        out_specs=pl.BlockSpec(memory_space=pltpu.VMEM),
        scratch_shapes=[
            pltpu.SMEM((4,), jnp.int32),
            pltpu.SMEM((4, 26), jnp.int32),
            pltpu.VMEM((1, 128), F32),
            pltpu.VMEM((1, 128), F32),
            pltpu.VMEM((1, 256), F32),
            pltpu.VMEM((4, 8, 64, 128), BF16),
            pltpu.VMEM((2, 4, 8, 16, 128), BF16),
            pltpu.VMEM((5, 4, 2, 8, 8, 128), F32),
            pltpu.VMEM((5, 4, 2, 8, 8, 128), F32),
            pltpu.VMEM((5, 4, 4, 8, 128), F32),
            pltpu.VMEM((4, 17, 1, 8, 128), F32),
            pltpu.VMEM((4, 17, 1, 8, 128), F32),
            pltpu.VMEM((2, 4, 10, 32, 384), BF16),
            pltpu.VMEM((2, 4, 10, 32, 384), BF16),
            pltpu.VMEM((2, 10, 32, 384), BF16),
            pltpu.VMEM((2, 10, 32, 384), BF16),
            pltpu.VMEM((6, 6, 32, 384), BF16),
            pltpu.VMEM((2, 6, 32, 384), BF16),
            pltpu.VMEM((2, 6, 32, 384), BF16),
            pltpu.VMEM((4, 3, 384, 256), BF16),
            pltpu.VMEM((4, 3, 384, 256), BF16),
            pltpu.VMEM((3456, 256), BF16),
            pltpu.VMEM((256, 128), BF16),
            pltpu.VMEM((4, 2, 8, 32, 128), F32),
            pltpu.VMEM((4, 4, 32, 256), F32),
            pltpu.VMEM((2, 4, 32, 128), BF16),
            pltpu.VMEM((2, 4, 32, 128), BF16),
            pltpu.VMEM((4, 32, 128), BF16),
            pltpu.VMEM((4, 32, 128), BF16),
            pltpu.SemaphoreType.DMA((12,)),
            pltpu.SemaphoreType.DMA((2,)),
            pltpu.SemaphoreType.DMA((3, 8)),
            pltpu.SemaphoreType.DMA((3, 8)),
        ]
        + [pltpu.VMEM((9, 64, 128), BF16)] * 8
        + [pltpu.VMEM((9, 32, 128), BF16)] * 4,
        compiler_params=pltpu.CompilerParams(
            collective_id=0, has_side_effects=True, vmem_limit_bytes=48 * 2**20
        ),
        cost_estimate=pl.CostEstimate(
            flops=8_000_000_000, bytes_accessed=8_000_000, transcendentals=0
        ),
        name="unet_window",
    )(*operands)
    return result.reshape(1, 1, 4, 512, 128)


def solution(mesh):
    placed = (
        P("gx", "gy", None, None, None),
        P("gx", "gy", None),
        P("gx", "gy", None, None),
    ) + (P(),) * 7
    return jax.shard_map(
        functools.partial(local, mesh.shape["gx"], mesh.shape["gy"]),
        mesh=mesh,
        in_specs=placed,
        out_specs=P("gx", "gy", None, None, None),
        check_vma=False,
    )
```

```python
import functools

import jax
import jax.numpy as jnp
from jax import lax
from jax.experimental import pallas as pl
from jax.experimental.pallas import tpu as pltpu
from jax.sharding import PartitionSpec as P

MESH = pl.DeviceIdType.MESH
F32 = jnp.float32
BF16 = jnp.bfloat16

OFFSETS = [
    (ox, oy, oz)
    for ox in (-1, 0, 1)
    for oy in (-1, 0, 1)
    for oz in (-1, 0, 1)
    if (ox, oy, oz) != (0, 0, 0)
]
NUMBER = {offset: k for k, offset in enumerate(OFFSETS)}
SIDES = [(-1, 0), (1, 0), (0, -1), (0, 1)]
EDGES = [(-1, -1), (-1, 1), (1, -1), (1, 1)]
ALL = SIDES + EDGES
FARTHEST = (4, 5, 6, 7, 2, 3, 0, 1)


def edges_on(oy):
    return [(k, edge) for k, edge in enumerate(EDGES) if edge[1] == oy]


def edge_of(step, last):
    return last if step < 0 else 0


def kernel(
    gx,
    gy,
    cell_hbm,
    nbr_hbm,
    feat,
    w1,
    b1_hbm,
    w2,
    b2_hbm,
    wc,
    bc_hbm,
    wl,
    out,
    cell,
    nbr,
    b1,
    b2,
    bc,
    staged,
    staged_rim,
    field,
    hidden,
    coarse_field,
    edge_src,
    cedge_src,
    zin,
    zhid,
    zx,
    zy,
    zc,
    zcx,
    zcy,
    w1p,
    w2p,
    wcv,
    wlv,
    total,
    ctotal,
    send_edge,
    recv_edge,
    csend_edge,
    crecv_edge,
    local_sem,
    rim_sem,
    send_sem,
    recv_sem,
    *side_refs,
):
    sides = [side_refs[4 * number : 4 * number + 4] for number in range(3)]
    mx = lax.axis_index("gx")
    my = lax.axis_index("gy")

    def device_at(ox, oy):
        return (lax.rem(mx + ox + gx, gx), lax.rem(my + oy + gy, gy))

    def inside(ox, oy):
        found = None
        for at, step, size in ((mx, ox, gx), (my, oy, gy)):
            if step != 0:
                here = at > 0 if step < 0 else at < size - 1
                found = here if found is None else jnp.logical_and(found, here)
        return found

    def when_inside(ox, oy, act):
        @pl.when(inside(ox, oy))
        def _():
            act()

    def signal_to(ox, oy):
        pl.semaphore_signal(
            barrier, inc=1, device_id=device_at(ox, oy), device_id_type=MESH
        )

    barrier = pltpu.get_barrier_semaphore()
    for k in FARTHEST:
        when_inside(*ALL[k], functools.partial(signal_to, *ALL[k]))
    beside_x = jnp.where(mx > 0, 1, 0) + jnp.where(mx < gx - 1, 1, 0)
    beside_y = jnp.where(my > 0, 1, 0) + jnp.where(my < gy - 1, 1, 0)
    partners = (1 + beside_x) * (1 + beside_y) - 1

    pairs = [
        (feat, staged),
        (cell_hbm, cell),
        (nbr_hbm, nbr),
        (b1_hbm, b1),
        (w1, w1p.at[0:3, :, :, 0:128]),
        (w1, w1p.at[1:4, :, :, 128:256]),
        (w2, w2p.at[0:3, :, :, 0:128]),
        (w2, w2p.at[1:4, :, :, 128:256]),
        (b2_hbm, b2),
        (wc, wcv),
        (wl, wlv),
        (bc_hbm, bc),
    ]
    copies = [
        pltpu.make_async_copy(src, dst, local_sem.at[k])
        for k, (src, dst) in enumerate(pairs)
    ]
    rims = [
        pltpu.make_async_copy(
            feat.at[:, :, 48 * d : 48 * d + 16], staged_rim.at[d], rim_sem.at[d]
        )
        for d in (0, 1)
    ]
    for copy in rims + copies[:6]:
        copy.start()

    for wp in (w1p, w2p):
        wp[3, :, :, 0:128] = jnp.zeros((3, 384, 128), BF16)
        wp[0, :, :, 128:256] = jnp.zeros((3, 384, 128), BF16)
    field[4] = jnp.zeros((4, 2, 8, 8, 128), F32)
    hidden[4] = jnp.zeros((4, 2, 8, 8, 128), F32)
    coarse_field[4] = jnp.zeros((4, 4, 8, 128), F32)
    for d in range(4):
        for number, rows in ((0, 64), (1, 64), (2, 32)):
            sides[number][d][8] = jnp.zeros((rows, 128), BF16)
        edge_src[d, 16] = jnp.zeros((1, 8, 128), F32)
        cedge_src[d, 16] = jnp.zeros((1, 8, 128), F32)
    for z in (zin, zhid):
        z[:, :, 0] = jnp.zeros((2, 4, 32, 384), BF16)
        z[:, :, 9] = jnp.zeros((2, 4, 32, 384), BF16)
    for side in range(2):
        for end in (0, 9):
            zx[side, end] = jnp.zeros((32, 384), BF16)
        for end in (0, 5):
            zcx[side, end] = jnp.zeros((32, 384), BF16)
    for end in (0, 5):
        zc[end] = jnp.zeros((6, 32, 384), BF16)
        zc[:, end] = jnp.zeros((6, 32, 384), BF16)

    for copy in rims:
        copy.wait()

    def plane(source, s, x):
        if source is coarse_field:
            return source[s, x]
        return source[s, x // 2, x % 2]

    def across(source, s, y):
        if source is coarse_field:
            return source[s, :, y]
        if source is field:
            d = y // 7
            return staged_rim[d, s].astype(F32)[:, 8 * d : 8 * d + 8]
        return source[s, :, :, y].reshape(8, 8, 128)

    def column(source, s, x, y):
        if source is coarse_field:
            return source[s, x, y]
        if source is field:
            d = y // 7
            return staged_rim[d, s, x].astype(F32)[8 * d : 8 * d + 8]
        return source[s, x // 2, x % 2, y]

    def pack_side(number, source, last, d):
        ox, oy = SIDES[d]
        for s in range(4):
            if oy == 0:
                face = plane(source, s, edge_of(ox, last))
            else:
                face = across(source, s, edge_of(oy, last))
            sides[number][d][s] = face.reshape(8 * (last + 1), 128).astype(BF16)

    def pack_edges(source, last, edges, oy):
        for d, (ox, oy) in edges_on(oy):
            edges[d] = jnp.concatenate(
                [
                    column(source, s, edge_of(ox, last), edge_of(oy, last))
                    for s in range(4)
                ],
                axis=0,
            ).astype(BF16)

    def describe(number, edges, redges):
        described = {}
        for k in FARTHEST:
            ox, oy = ALL[k]
            if k < 4:
                src = sides[number][k].at[0:4]
                dst = sides[number][k].at[4:8]
                if number == 0 and oy == 0:
                    src = feat.at[:, edge_of(ox, 7)]
            else:
                src, dst = edges.at[k - 4], redges.at[k - 4]
            described[ox, oy] = pltpu.make_async_remote_copy(
                src_ref=src,
                dst_ref=dst,
                send_sem=send_sem.at[number, k],
                recv_sem=recv_sem.at[number, k],
                device_id=device_at(-ox, -oy),
                device_id_type=MESH,
            )
        return described

    def start(described, directions):
        for ox, oy in directions:
            when_inside(-ox, -oy, described[ox, oy].start)

    def leave_y(number, described, source, last, edges, d):
        oy = 1 - 2 * d
        pack_side(number, source, last, 3 - d)
        start(described, [(0, oy)])
        pack_edges(source, last, edges, oy)
        start(described, [edge for _, edge in edges_on(oy)])

    def leave_x(number, described, source, last):
        for d in (0, 1):
            pack_side(number, source, last, d)
        start(described, SIDES[:2])

    def arrive(described, directions):
        for ox, oy in directions:
            when_inside(ox, oy, described[ox, oy].wait_recv)

    sent = describe(0, send_edge.at[0], recv_edge.at[0])
    for oy in (-1, 1):
        pack_edges(field, 7, send_edge.at[0], oy)
    for d in (2, 3):
        pack_side(0, field, 7, d)
    copies[0].wait()
    for s in range(4):
        for x in range(8):
            field[s, x // 2, x % 2] = staged[s, x].astype(F32).reshape(8, 8, 128)
        for d in (0, 1):
            sides[0][d][s] = staged[s, edge_of(SIDES[d][0], 7)]

    for k in (1, 2, 3):
        copies[k].wait()
    live = [jnp.where(cell[s] >= 0, 1.0, 0.0).astype(F32) for s in range(4)]

    def index(s, ox, oy, oz):
        if (ox, oy, oz) == (0, 0, 0):
            return s
        entry = nbr[s, NUMBER[ox, oy, oz]]
        safe = jnp.maximum(entry, 0)
        block = lax.shift_right_logical(safe, 2)
        slot = lax.bitwise_and(safe, 3)
        if (ox, oy) == (0, 0):
            return jnp.where(entry < 0, 4, slot)
        if ox == 0 or oy == 0:
            place = slot + jnp.where(block == 4, 0, 4)
            return jnp.where(entry < 0, 8, place)
        beside_x = (ox + 1) * 3 + 1
        beside_y = 3 + (oy + 1)
        place = slot + jnp.where(
            block == 4,
            0,
            jnp.where(block == beside_x, 4, jnp.where(block == beside_y, 8, 12)),
        )
        return jnp.where(entry < 0, 16, place)

    where = {
        (s, ox, oy, oz): index(s, ox, oy, oz)
        for s in range(4)
        for ox in (-1, 0, 1)
        for oy in (-1, 0, 1)
        for oz in (-1, 0, 1)
    }

    def shifted(low, own, high, step):
        row = lax.broadcasted_iota(jnp.int32, own.shape, own.ndim - 2)
        axis = own.ndim - 2
        down = pltpu.roll(jnp.where(row >= 8 - step, low, own), step, axis)
        up = pltpu.roll(jnp.where(row < step, high, own), 8 - step, axis)
        return down, own, up

    def pair(fetch, ox, oy, step):
        for half in (0, 1):
            parts = [
                shifted(*[fetch(where[s, ox, oy, oz]) for oz in (-1, 0, 1)], step)
                for s in (2 * half, 2 * half + 1)
            ]
            for kz in range(3):
                both = jnp.concatenate([parts[0][kz], parts[1][kz]], axis=-2)
                yield slice(16 * half, 16 * half + 16), slice(
                    128 * kz, 128 * kz + 128
                ), both.astype(BF16)

    def fine_centre(source, z):
        def body(m, carry):
            for h in (0, 1):
                for rows, lanes, value in pair(lambda q: source[q, m, h], 0, 0, 1):
                    z[h, m, 1:9, rows, lanes] = value
            return carry

        lax.fori_loop(0, 4, body, 0)

    def face(number, d):
        def fetch(q):
            value = sides[number][d][q].astype(F32)
            return value.reshape(value.shape[0] // 8, 8, 128)

        return fetch

    def own_edges(source, last, edges):
        for d, (ox, oy) in enumerate(EDGES):
            for s in range(4):
                edges[d, s, 0] = column(
                    source, s, edge_of(ox, last), edge_of(oy, last)
                )

    def end_of(number, d, s, step):
        ref = sides[number][d]
        if step < 0:
            rows = ref.shape[1]
            return ref[4 + s, rows - 16 : rows].astype(F32)[8:16]
        return ref[4 + s, 0:16].astype(F32)[0:8]

    def edges_beside_x(number, edges):
        for k, (ox, oy) in enumerate(EDGES):
            for s in range(4):
                edges[k, 4 + s, 0] = end_of(number, SIDES.index((ox, 0)), s, oy)

    def edges_beside_y(number, edges, redges, d):
        for k, (ox, oy) in edges_on(2 * d - 1):
            far = redges[k].astype(F32)
            for s in range(4):
                edges[k, 8 + s, 0] = end_of(number, d + 2, s, ox)
                edges[k, 12 + s, 0] = far[8 * s : 8 * s + 8]

    def y_rim(number, step, last, edges, rim, d):
        for rows, lanes, value in pair(face(number, d + 2), *SIDES[d + 2], step):
            rim[d, 1 : last + 2, rows, lanes] = value
        for k, (ox, oy) in edges_on(2 * d - 1):
            x = 0 if ox < 0 else last + 2
            for rows, lanes, value in pair(lambda q: edges[k, q], ox, oy, step):
                rim[d, x, rows, lanes] = value[0]

    def arrive_y(described, d):
        arrive(described, [edge for _, edge in edges_on(2 * d - 1)] + [SIDES[d + 2]])

    def by_turns(step):
        far_low = lax.rem(my, 4) == 0

        @pl.when(far_low)
        def _():
            step(1)

        step(0)

        @pl.when(jnp.logical_not(far_low))
        def _():
            step(1)

    def x_rim(number, step, last, rim):
        for d in (0, 1):
            for rows, lanes, value in pair(face(number, d), *SIDES[d], step):
                rim[d, 1 : last + 2, rows, lanes] = value

    def centre_conv(z, wp, i):
        planes = [(1, i - 1), (0, i), (1, i), (0, i + 1)]
        used = [p for p in range(4) if 0 <= planes[p][1] < 4]
        lhs = jnp.concatenate(
            [
                z[planes[p][0], planes[p][1], ky : ky + 8].reshape(256, 384)
                for ky in range(3)
                for p in used
            ],
            axis=1,
        )
        rhs = jnp.concatenate([wp[p, ky] for ky in range(3) for p in used], axis=0)
        return jnp.dot(lhs, rhs, preferred_element_type=F32)

    def convolve(z, wp, finish):
        for i in range(4):
            acc = centre_conv(z, wp, i)
            for h in (0, 1):
                part = acc[:, 128 * h : 128 * h + 128].reshape(8, 32, 128)
                total[i, h] = part
                if 0 < 2 * i + h < 7:
                    inner = part[1:7].reshape(6, 4, 8, 128)
                    for s in range(4):
                        finish(s, (i, h, slice(1, 7)), inner[:, s])

    def add_x(number, described, wp, finish):
        arrive(described, SIDES[:2])
        x_rim(number, 1, 7, zx)
        edges_beside_x(number, edge_src)
        for d in (0, 1):
            i, h, p = (0, 0, 0) if d == 0 else (3, 1, 3)
            lhs = jnp.concatenate(
                [zx[d, ky : ky + 8].reshape(256, 384) for ky in range(3)], axis=1
            )
            rhs = jnp.concatenate(
                [wp[p, ky][:, 128 * h : 128 * h + 128] for ky in range(3)], axis=0
            )
            add = jnp.dot(lhs, rhs, preferred_element_type=F32).reshape(8, 32, 128)
            part = total[i, h] + add
            for y in (0, 7):
                total[i, h, y] = part[y]
            inner = part[1:7].reshape(6, 4, 8, 128)
            for s in range(4):
                finish(s, (i, h, slice(1, 7)), inner[:, s])

    def add_y(number, described, wp, finish, after):
        def step(d):
            arrive_y(described, d)
            edges_beside_y(number, edge_src, recv_edge.at[number], d)
            y_rim(number, 1, 7, edge_src, zy, d)
            y, ky = (0, 0) if d == 0 else (7, 2)
            lhs = jnp.concatenate(
                [zy[d, kx : kx + 8].reshape(256, 384) for kx in range(3)], axis=1
            )
            rhs = jnp.concatenate([wp[kx, ky][:, 0:128] for kx in range(3)], axis=0)
            add = jnp.dot(lhs, rhs, preferred_element_type=F32)
            part = total[:, :, y] + add.reshape(4, 2, 32, 128)
            part = part.reshape(4, 2, 4, 8, 128)
            for s in range(4):
                finish(s, (slice(0, 4), slice(0, 2), y), part[:, :, s])
            after(d)

        by_turns(step)

    own_edges(field, 7, edge_src)
    fine_centre(field, zin)
    pl.semaphore_wait(barrier, partners)
    start(sent, EDGES + SIDES[2:] + SIDES[:2])

    copies[4].wait()
    copies[5].wait()
    for copy in copies[6:]:
        copy.start()

    def to_hidden(s, at, value):
        value = jnp.maximum(value + b1[...].reshape(1, 1, 128), 0.0) * live[s]
        hidden[(s,) + at] = value.astype(BF16).astype(F32)

    convolve(zin, w1p, to_hidden)
    add_x(0, sent, w1p, to_hidden)
    sent_hidden = describe(1, send_edge.at[1], recv_edge.at[1])
    add_y(
        0,
        sent,
        w1p,
        to_hidden,
        lambda d: leave_y(1, sent_hidden, hidden, 7, send_edge.at[1], d),
    )
    leave_x(1, sent_hidden, hidden, 7)
    own_edges(hidden, 7, edge_src)
    fine_centre(hidden, zhid)

    for k in (6, 7, 8):
        copies[k].wait()

    def to_fine(s, at, value):
        value = value + b2[...].reshape(1, 1, 128) + field[(s,) + at]
        out[(s,) + at] = value * live[s]

    def pooled(value):
        even = lax.broadcasted_iota(jnp.int32, value.shape, 1) % 2 == 0
        other = jnp.where(even, pltpu.roll(value, 7, 1), pltpu.roll(value, 1, 1))
        return ((value + other) * 0.125).astype(BF16).astype(F32)

    def pool(ys):
        for s in range(4):
            for y in ys:
                value = out[s, :, 0, 2 * y] + out[s, :, 1, 2 * y]
                value = value + out[s, :, 0, 2 * y + 1] + out[s, :, 1, 2 * y + 1]
                coarse_field[s, :, y] = pooled(value)

    convolve(zhid, w2p, to_fine)
    add_x(1, sent_hidden, w2p, to_fine)
    pool((1, 2))
    sent_coarse = describe(2, csend_edge, crecv_edge)

    def to_coarse(d):
        pool((3 * d,))
        leave_y(2, sent_coarse, coarse_field, 3, csend_edge, d)

    add_y(1, sent_hidden, w2p, to_fine, to_coarse)
    leave_x(2, sent_coarse, coarse_field, 3)

    own_edges(coarse_field, 3, cedge_src)
    for x in range(4):
        for rows, lanes, value in pair(lambda q: coarse_field[q, x], 0, 0, 2):
            zc[x + 1, 1:5, rows, lanes] = value
    for k in (9, 10, 11):
        copies[k].wait()
    lhs = jnp.concatenate(
        [
            zc[kx : kx + 4, ky : ky + 4].reshape(512, 384)
            for kx in range(3)
            for ky in range(3)
        ],
        axis=1,
    )
    acc = jnp.dot(lhs, wcv[...], preferred_element_type=F32)
    ctotal[...] = acc.reshape(4, 4, 32, 256)

    def join(ys):
        acc = jnp.concatenate([ctotal[:, y] for y in ys], axis=0)
        acc = jnp.maximum(acc.reshape(-1, 256) + bc[...], 0.0)
        acc = acc.reshape(4 * len(ys), 4, 8, 256)
        acc = jnp.concatenate(
            [(acc[:, s] * live[s])[:, None] for s in range(4)], axis=1
        )
        lifted = jnp.dot(
            acc.reshape(-1, 256).astype(BF16), wlv[...], preferred_element_type=F32
        ).reshape(len(ys), 4, 4, 8, 128)
        for k, y in enumerate(ys):
            for s in range(4):
                raised = lifted[k, :, s]
                for h in (0, 1):
                    for f in (0, 1):
                        at = (s, slice(0, 4), h, 2 * y + f)
                        out[at] = (out[at] + raised) * live[s]

    arrive(sent_coarse, SIDES[:2])
    x_rim(2, 2, 3, zcx)
    edges_beside_x(2, cedge_src)
    for d in (0, 1):
        lhs = jnp.concatenate(
            [zcx[d, ky : ky + 4].reshape(128, 384) for ky in range(3)], axis=1
        )
        rhs = wcv[2304 * d : 2304 * d + 1152]
        add = jnp.dot(lhs, rhs, preferred_element_type=F32)
        ctotal[3 * d] = ctotal[3 * d] + add.reshape(4, 32, 256)
    join((1, 2))

    def coarse_y(d):
        arrive_y(sent_coarse, d)
        edges_beside_y(2, cedge_src, crecv_edge, d)
        y_rim(2, 2, 3, cedge_src, zcy, d)
        lhs = jnp.concatenate(
            [zcy[d, kx : kx + 4].reshape(128, 384) for kx in range(3)], axis=1
        )
        rhs = jnp.concatenate(
            [
                wcv[1152 * kx + 768 * d : 1152 * kx + 768 * d + 384]
                for kx in range(3)
            ],
            axis=0,
        )
        add = jnp.dot(lhs, rhs, preferred_element_type=F32)
        ctotal[:, 3 * d] = ctotal[:, 3 * d] + add.reshape(4, 32, 256)
        join((3 * d,))

    by_turns(coarse_y)
    for described in (sent, sent_hidden, sent_coarse):
        for (ox, oy), copy in described.items():
            when_inside(-ox, -oy, copy.wait_send)


def local(gx, gy, features, slot_cell, neighbours, w1, b1, w2, b2, wc, bc, wl):
    operands = [
        pltpu.with_memory_space_constraint(operand, pltpu.HBM)
        for operand in (
            slot_cell.reshape(4),
            neighbours.reshape(4, 26),
            features.reshape(4, 8, 64, 128),
            w1.reshape(3, 3, 384, 128),
            b1.reshape(1, 128),
            w2.reshape(3, 3, 384, 128),
            b2.reshape(1, 128),
            wc.reshape(3456, 256),
            bc.reshape(1, 256),
            wl,
        )
    ]
    result = pl.pallas_call(
        functools.partial(kernel, gx, gy),
        out_shape=jax.ShapeDtypeStruct((4, 4, 2, 8, 8, 128), F32),
        in_specs=[pl.BlockSpec(memory_space=pl.ANY)] * 10,
        out_specs=pl.BlockSpec(memory_space=pltpu.VMEM),
        scratch_shapes=[
            pltpu.SMEM((4,), jnp.int32),
            pltpu.SMEM((4, 26), jnp.int32),
            pltpu.VMEM((1, 128), F32),
            pltpu.VMEM((1, 128), F32),
            pltpu.VMEM((1, 256), F32),
            pltpu.VMEM((4, 8, 64, 128), BF16),
            pltpu.VMEM((2, 4, 8, 16, 128), BF16),
            pltpu.VMEM((5, 4, 2, 8, 8, 128), F32),
            pltpu.VMEM((5, 4, 2, 8, 8, 128), F32),
            pltpu.VMEM((5, 4, 4, 8, 128), F32),
            pltpu.VMEM((4, 17, 1, 8, 128), F32),
            pltpu.VMEM((4, 17, 1, 8, 128), F32),
            pltpu.VMEM((2, 4, 10, 32, 384), BF16),
            pltpu.VMEM((2, 4, 10, 32, 384), BF16),
            pltpu.VMEM((2, 10, 32, 384), BF16),
            pltpu.VMEM((2, 10, 32, 384), BF16),
            pltpu.VMEM((6, 6, 32, 384), BF16),
            pltpu.VMEM((2, 6, 32, 384), BF16),
            pltpu.VMEM((2, 6, 32, 384), BF16),
            pltpu.VMEM((4, 3, 384, 256), BF16),
            pltpu.VMEM((4, 3, 384, 256), BF16),
            pltpu.VMEM((3456, 256), BF16),
            pltpu.VMEM((256, 128), BF16),
            pltpu.VMEM((4, 2, 8, 32, 128), F32),
            pltpu.VMEM((4, 4, 32, 256), F32),
            pltpu.VMEM((2, 4, 32, 128), BF16),
            pltpu.VMEM((2, 4, 32, 128), BF16),
            pltpu.VMEM((4, 32, 128), BF16),
            pltpu.VMEM((4, 32, 128), BF16),
            pltpu.SemaphoreType.DMA((12,)),
            pltpu.SemaphoreType.DMA((2,)),
            pltpu.SemaphoreType.DMA((3, 8)),
            pltpu.SemaphoreType.DMA((3, 8)),
        ]
        + [pltpu.VMEM((9, 64, 128), BF16)] * 8
        + [pltpu.VMEM((9, 32, 128), BF16)] * 4,
        compiler_params=pltpu.CompilerParams(
            collective_id=0, has_side_effects=True, vmem_limit_bytes=48 * 2**20
        ),
        cost_estimate=pl.CostEstimate(
            flops=8_000_000_000, bytes_accessed=8_000_000, transcendentals=0
        ),
        name="unet_window",
    )(*operands)
    return result.reshape(1, 1, 4, 512, 128)


def solution(mesh):
    placed = (
        P("gx", "gy", None, None, None),
        P("gx", "gy", None),
        P("gx", "gy", None, None),
    ) + (P(),) * 7
    return jax.shard_map(
        functools.partial(local, mesh.shape["gx"], mesh.shape["gy"]),
        mesh=mesh,
        in_specs=placed,
        out_specs=P("gx", "gy", None, None, None),
        check_vma=False,
    )
```

```python
import functools

import jax
import jax.numpy as jnp
from jax import lax
from jax.experimental import pallas as pl
from jax.experimental.pallas import tpu as pltpu
from jax.sharding import PartitionSpec as P

MESH = pl.DeviceIdType.MESH
F32 = jnp.float32
BF16 = jnp.bfloat16

OFFSETS = [
    (ox, oy, oz)
    for ox in (-1, 0, 1)
    for oy in (-1, 0, 1)
    for oz in (-1, 0, 1)
    if (ox, oy, oz) != (0, 0, 0)
]
NUMBER = {offset: k for k, offset in enumerate(OFFSETS)}
SIDES = [(-1, 0), (1, 0), (0, -1), (0, 1)]
EDGES = [(-1, -1), (-1, 1), (1, -1), (1, 1)]
ALL = SIDES + EDGES
FARTHEST = (4, 5, 6, 7, 2, 3, 0, 1)


def edges_on(oy):
    return [(k, edge) for k, edge in enumerate(EDGES) if edge[1] == oy]


def edge_of(step, last):
    return last if step < 0 else 0


def kernel(
    gx,
    gy,
    cell_hbm,
    nbr_hbm,
    feat,
    w1,
    b1_hbm,
    w2,
    b2_hbm,
    wc,
    bc_hbm,
    wl,
    out,
    cell,
    nbr,
    b1,
    b2,
    bc,
    staged,
    staged_rim,
    field,
    hidden,
    coarse_field,
    edge_src,
    cedge_src,
    zin,
    zhid,
    zx,
    zy,
    zc,
    zcx,
    zcy,
    w1p,
    w2p,
    wcv,
    wlv,
    total,
    ctotal,
    send_edge,
    recv_edge,
    csend_edge,
    crecv_edge,
    local_sem,
    rim_sem,
    send_sem,
    recv_sem,
    *side_refs,
):
    sides = [side_refs[4 * number : 4 * number + 4] for number in range(3)]
    mx = lax.axis_index("gx")
    my = lax.axis_index("gy")

    def device_at(ox, oy):
        return (lax.rem(mx + ox + gx, gx), lax.rem(my + oy + gy, gy))

    def inside(ox, oy):
        found = None
        for at, step, size in ((mx, ox, gx), (my, oy, gy)):
            if step != 0:
                here = at > 0 if step < 0 else at < size - 1
                found = here if found is None else jnp.logical_and(found, here)
        return found

    def when_inside(ox, oy, act):
        @pl.when(inside(ox, oy))
        def _():
            act()

    def signal_to(ox, oy):
        pl.semaphore_signal(
            barrier, inc=1, device_id=device_at(ox, oy), device_id_type=MESH
        )

    barrier = pltpu.get_barrier_semaphore()
    for k in FARTHEST:
        when_inside(*ALL[k], functools.partial(signal_to, *ALL[k]))
    beside_x = jnp.where(mx > 0, 1, 0) + jnp.where(mx < gx - 1, 1, 0)
    beside_y = jnp.where(my > 0, 1, 0) + jnp.where(my < gy - 1, 1, 0)
    partners = (1 + beside_x) * (1 + beside_y) - 1

    pairs = [
        (feat, staged),
        (cell_hbm, cell),
        (nbr_hbm, nbr),
        (b1_hbm, b1),
        (w1, w1p.at[0:3, :, :, 0:128]),
        (w1, w1p.at[1:4, :, :, 128:256]),
        (w2, w2p.at[0:3, :, :, 0:128]),
        (w2, w2p.at[1:4, :, :, 128:256]),
        (b2_hbm, b2),
        (wc, wcv),
        (wl, wlv),
        (bc_hbm, bc),
    ]
    copies = [
        pltpu.make_async_copy(src, dst, local_sem.at[k])
        for k, (src, dst) in enumerate(pairs)
    ]
    rims = [
        pltpu.make_async_copy(
            feat.at[:, :, 48 * d : 48 * d + 16], staged_rim.at[d], rim_sem.at[d]
        )
        for d in (0, 1)
    ]
    for copy in rims + copies[:6]:
        copy.start()

    def clear_weights(wp):
        wp[3, :, :, 0:128] = jnp.zeros((3, 384, 128), BF16)
        wp[0, :, :, 128:256] = jnp.zeros((3, 384, 128), BF16)

    def clear_ends(z):
        z[:, :, 0] = jnp.zeros((2, 4, 32, 384), BF16)
        z[:, :, 9] = jnp.zeros((2, 4, 32, 384), BF16)

    clear_weights(w1p)
    clear_ends(zin)
    field[4] = jnp.zeros((4, 2, 8, 8, 128), F32)
    for d in range(4):
        sides[0][d][8] = jnp.zeros((64, 128), BF16)
        edge_src[d, 16] = jnp.zeros((1, 8, 128), F32)

    def clear_later():
        clear_weights(w2p)
        clear_ends(zhid)
        hidden[4] = jnp.zeros((4, 2, 8, 8, 128), F32)
        coarse_field[4] = jnp.zeros((4, 4, 8, 128), F32)
        for d in range(4):
            for number, rows in ((1, 64), (2, 32)):
                sides[number][d][8] = jnp.zeros((rows, 128), BF16)
            cedge_src[d, 16] = jnp.zeros((1, 8, 128), F32)
        for side in range(2):
            for end in (0, 9):
                zx[side, end] = jnp.zeros((32, 384), BF16)
            for end in (0, 5):
                zcx[side, end] = jnp.zeros((32, 384), BF16)
        for end in (0, 5):
            zc[end] = jnp.zeros((6, 32, 384), BF16)
            zc[:, end] = jnp.zeros((6, 32, 384), BF16)

    for copy in rims:
        copy.wait()

    def plane(source, s, x):
        if source is coarse_field:
            return source[s, x]
        return source[s, x // 2, x % 2]

    def across(source, s, y):
        if source is coarse_field:
            return source[s, :, y]
        if source is field:
            d = y // 7
            return staged_rim[d, s].astype(F32)[:, 8 * d : 8 * d + 8]
        return source[s, :, :, y].reshape(8, 8, 128)

    def column(source, s, x, y):
        if source is coarse_field:
            return source[s, x, y]
        if source is field:
            d = y // 7
            return staged_rim[d, s, x].astype(F32)[8 * d : 8 * d + 8]
        return source[s, x // 2, x % 2, y]

    def pack_side(number, source, last, d):
        ox, oy = SIDES[d]
        for s in range(4):
            if oy == 0:
                face = plane(source, s, edge_of(ox, last))
            else:
                face = across(source, s, edge_of(oy, last))
            sides[number][d][s] = face.reshape(8 * (last + 1), 128).astype(BF16)

    def pack_edges(source, last, edges, oy):
        for d, (ox, oy) in edges_on(oy):
            edges[d] = jnp.concatenate(
                [
                    column(source, s, edge_of(ox, last), edge_of(oy, last))
                    for s in range(4)
                ],
                axis=0,
            ).astype(BF16)

    def describe(number, edges, redges):
        described = {}
        for k in FARTHEST:
            ox, oy = ALL[k]
            if k < 4:
                src = sides[number][k].at[0:4]
                dst = sides[number][k].at[4:8]
                if number == 0 and oy == 0:
                    src = feat.at[:, edge_of(ox, 7)]
            else:
                src, dst = edges.at[k - 4], redges.at[k - 4]
            described[ox, oy] = pltpu.make_async_remote_copy(
                src_ref=src,
                dst_ref=dst,
                send_sem=send_sem.at[number, k],
                recv_sem=recv_sem.at[number, k],
                device_id=device_at(-ox, -oy),
                device_id_type=MESH,
            )
        return described

    def start(described, directions):
        for ox, oy in directions:
            when_inside(-ox, -oy, described[ox, oy].start)

    def leave_y(number, described, source, last, edges, d):
        oy = 1 - 2 * d
        pack_edges(source, last, edges, oy)
        pack_side(number, source, last, 3 - d)
        start(described, [edge for _, edge in edges_on(oy)] + [(0, oy)])

    def leave_x(number, described, source, last):
        for d in (0, 1):
            pack_side(number, source, last, d)
        start(described, SIDES[:2])

    def arrive(described, directions):
        for ox, oy in directions:
            when_inside(ox, oy, described[ox, oy].wait_recv)

    sent = describe(0, send_edge.at[0], recv_edge.at[0])
    for oy in (-1, 1):
        pack_edges(field, 7, send_edge.at[0], oy)
    for d in (2, 3):
        pack_side(0, field, 7, d)
    pl.semaphore_wait(barrier, partners)
    start(sent, EDGES + SIDES[2:] + SIDES[:2])
    copies[0].wait()
    for s in range(4):
        for x in range(8):
            field[s, x // 2, x % 2] = staged[s, x].astype(F32).reshape(8, 8, 128)
        for d in (0, 1):
            sides[0][d][s] = staged[s, edge_of(SIDES[d][0], 7)]

    for k in (1, 2, 3):
        copies[k].wait()
    live = [jnp.where(cell[s] >= 0, 1.0, 0.0).astype(F32) for s in range(4)]

    def index(s, ox, oy, oz):
        if (ox, oy, oz) == (0, 0, 0):
            return s
        entry = nbr[s, NUMBER[ox, oy, oz]]
        safe = jnp.maximum(entry, 0)
        block = lax.shift_right_logical(safe, 2)
        slot = lax.bitwise_and(safe, 3)
        if (ox, oy) == (0, 0):
            return jnp.where(entry < 0, 4, slot)
        if ox == 0 or oy == 0:
            place = slot + jnp.where(block == 4, 0, 4)
            return jnp.where(entry < 0, 8, place)
        beside_x = (ox + 1) * 3 + 1
        beside_y = 3 + (oy + 1)
        place = slot + jnp.where(
            block == 4,
            0,
            jnp.where(block == beside_x, 4, jnp.where(block == beside_y, 8, 12)),
        )
        return jnp.where(entry < 0, 16, place)

    where = {
        (s, 0, 0, oz): index(s, 0, 0, oz) for s in range(4) for oz in (-1, 0, 1)
    }

    def index_rims():
        for s in range(4):
            for ox, oy in ALL:
                for oz in (-1, 0, 1):
                    where[s, ox, oy, oz] = index(s, ox, oy, oz)

    def shifted(low, own, high, step):
        row = lax.broadcasted_iota(jnp.int32, own.shape, own.ndim - 2)
        axis = own.ndim - 2
        down = pltpu.roll(jnp.where(row >= 8 - step, low, own), step, axis)
        up = pltpu.roll(jnp.where(row < step, high, own), 8 - step, axis)
        return down, own, up

    def pair(fetch, ox, oy, step):
        for half in (0, 1):
            parts = [
                shifted(*[fetch(where[s, ox, oy, oz]) for oz in (-1, 0, 1)], step)
                for s in (2 * half, 2 * half + 1)
            ]
            for kz in range(3):
                both = jnp.concatenate([parts[0][kz], parts[1][kz]], axis=-2)
                yield slice(16 * half, 16 * half + 16), slice(
                    128 * kz, 128 * kz + 128
                ), both.astype(BF16)

    def fine_centre(source, z):
        for m in range(4):
            for h in (0, 1):
                for rows, lanes, value in pair(lambda q: source[q, m, h], 0, 0, 1):
                    z[h, m, 1:9, rows, lanes] = value

    def face(number, d):
        def fetch(q):
            value = sides[number][d][q].astype(F32)
            return value.reshape(value.shape[0] // 8, 8, 128)

        return fetch

    def own_edges(source, last, edges):
        for d, (ox, oy) in enumerate(EDGES):
            for s in range(4):
                edges[d, s, 0] = column(
                    source, s, edge_of(ox, last), edge_of(oy, last)
                )

    def end_of(number, d, s, step):
        ref = sides[number][d]
        if step < 0:
            rows = ref.shape[1]
            return ref[4 + s, rows - 16 : rows].astype(F32)[8:16]
        return ref[4 + s, 0:16].astype(F32)[0:8]

    def edges_beside_x(number, edges):
        for k, (ox, oy) in enumerate(EDGES):
            for s in range(4):
                edges[k, 4 + s, 0] = end_of(number, SIDES.index((ox, 0)), s, oy)

    def edges_beside_y(number, edges, redges, d):
        for k, (ox, oy) in edges_on(2 * d - 1):
            far = redges[k].astype(F32)
            for s in range(4):
                edges[k, 8 + s, 0] = end_of(number, d + 2, s, ox)
                edges[k, 12 + s, 0] = far[8 * s : 8 * s + 8]

    def y_rim(number, step, last, edges, rim, d):
        for rows, lanes, value in pair(face(number, d + 2), *SIDES[d + 2], step):
            rim[d, 1 : last + 2, rows, lanes] = value
        for k, (ox, oy) in edges_on(2 * d - 1):
            x = 0 if ox < 0 else last + 2
            for rows, lanes, value in pair(lambda q: edges[k, q], ox, oy, step):
                rim[d, x, rows, lanes] = value[0]

    def arrive_y(described, d):
        arrive(described, [edge for _, edge in edges_on(2 * d - 1)] + [SIDES[d + 2]])

    def by_turns(step):
        far_low = lax.rem(my, 4) == 0

        @pl.when(far_low)
        def _():
            step(1)

        step(0)

        @pl.when(jnp.logical_not(far_low))
        def _():
            step(1)

    def x_rim(number, step, last, rim):
        for d in (0, 1):
            for rows, lanes, value in pair(face(number, d), *SIDES[d], step):
                rim[d, 1 : last + 2, rows, lanes] = value

    def centre_conv(z, wp, i):
        planes = [(1, i - 1), (0, i), (1, i), (0, i + 1)]
        used = [p for p in range(4) if 0 <= planes[p][1] < 4]
        lhs = jnp.concatenate(
            [
                z[planes[p][0], planes[p][1], ky : ky + 8].reshape(256, 384)
                for ky in range(3)
                for p in used
            ],
            axis=1,
        )
        rhs = jnp.concatenate([wp[p, ky] for ky in range(3) for p in used], axis=0)
        return jnp.dot(lhs, rhs, preferred_element_type=F32)

    def convolve(z, wp, finish):
        for i in range(4):
            acc = centre_conv(z, wp, i)
            for h in (0, 1):
                part = acc[:, 128 * h : 128 * h + 128].reshape(8, 32, 128)
                total[i, h] = part
                if 0 < 2 * i + h < 7:
                    inner = part[1:7].reshape(6, 4, 8, 128)
                    for s in range(4):
                        finish(s, (i, h, slice(1, 7)), inner[:, s])

    def add_x(number, described, wp, finish):
        arrive(described, SIDES[:2])
        x_rim(number, 1, 7, zx)
        edges_beside_x(number, edge_src)
        for d in (0, 1):
            i, h, p = (0, 0, 0) if d == 0 else (3, 1, 3)
            lhs = jnp.concatenate(
                [zx[d, ky : ky + 8].reshape(256, 384) for ky in range(3)], axis=1
            )
            rhs = jnp.concatenate(
                [wp[p, ky][:, 128 * h : 128 * h + 128] for ky in range(3)], axis=0
            )
            add = jnp.dot(lhs, rhs, preferred_element_type=F32).reshape(8, 32, 128)
            part = total[i, h] + add
            for y in (0, 7):
                total[i, h, y] = part[y]
            inner = part[1:7].reshape(6, 4, 8, 128)
            for s in range(4):
                finish(s, (i, h, slice(1, 7)), inner[:, s])

    def add_y(number, described, wp, finish, after):
        def step(d):
            arrive_y(described, d)
            edges_beside_y(number, edge_src, recv_edge.at[number], d)
            y_rim(number, 1, 7, edge_src, zy, d)
            y, ky = (0, 0) if d == 0 else (7, 2)
            lhs = jnp.concatenate(
                [zy[d, kx : kx + 8].reshape(256, 384) for kx in range(3)], axis=1
            )
            rhs = jnp.concatenate([wp[kx, ky][:, 0:128] for kx in range(3)], axis=0)
            add = jnp.dot(lhs, rhs, preferred_element_type=F32)
            part = total[:, :, y] + add.reshape(4, 2, 32, 128)
            part = part.reshape(4, 2, 4, 8, 128)
            for s in range(4):
                finish(s, (slice(0, 4), slice(0, 2), y), part[:, :, s])
            after(d)

        by_turns(step)

    copies[4].wait()
    copies[5].wait()
    for copy in copies[6:]:
        copy.start()
    fine_centre(field, zin)
    own_edges(field, 7, edge_src)
    index_rims()
    clear_later()

    def to_hidden(s, at, value):
        value = jnp.maximum(value + b1[...].reshape(1, 1, 128), 0.0) * live[s]
        hidden[(s,) + at] = value.astype(BF16).astype(F32)

    convolve(zin, w1p, to_hidden)
    add_x(0, sent, w1p, to_hidden)
    sent_hidden = describe(1, send_edge.at[1], recv_edge.at[1])
    add_y(
        0,
        sent,
        w1p,
        to_hidden,
        lambda d: leave_y(1, sent_hidden, hidden, 7, send_edge.at[1], d),
    )
    leave_x(1, sent_hidden, hidden, 7)
    for k in (6, 7, 8):
        copies[k].wait()
    own_edges(hidden, 7, edge_src)
    fine_centre(hidden, zhid)

    def to_fine(s, at, value):
        value = value + b2[...].reshape(1, 1, 128) + field[(s,) + at]
        out[(s,) + at] = value * live[s]

    def pooled(value):
        even = lax.broadcasted_iota(jnp.int32, value.shape, 1) % 2 == 0
        other = jnp.where(even, pltpu.roll(value, 7, 1), pltpu.roll(value, 1, 1))
        return ((value + other) * 0.125).astype(BF16).astype(F32)

    def pool(ys):
        for s in range(4):
            for y in ys:
                value = out[s, :, 0, 2 * y] + out[s, :, 1, 2 * y]
                value = value + out[s, :, 0, 2 * y + 1] + out[s, :, 1, 2 * y + 1]
                coarse_field[s, :, y] = pooled(value)

    convolve(zhid, w2p, to_fine)
    add_x(1, sent_hidden, w2p, to_fine)
    pool((1, 2))
    sent_coarse = describe(2, csend_edge, crecv_edge)

    def to_coarse(d):
        pool((3 * d,))
        leave_y(2, sent_coarse, coarse_field, 3, csend_edge, d)

    add_y(1, sent_hidden, w2p, to_fine, to_coarse)
    leave_x(2, sent_coarse, coarse_field, 3)

    own_edges(coarse_field, 3, cedge_src)
    for x in range(4):
        for rows, lanes, value in pair(lambda q: coarse_field[q, x], 0, 0, 2):
            zc[x + 1, 1:5, rows, lanes] = value
    for k in (9, 10, 11):
        copies[k].wait()
    lhs = jnp.concatenate(
        [
            zc[kx : kx + 4, ky : ky + 4].reshape(512, 384)
            for kx in range(3)
            for ky in range(3)
        ],
        axis=1,
    )
    acc = jnp.dot(lhs, wcv[...], preferred_element_type=F32)
    ctotal[...] = acc.reshape(4, 4, 32, 256)

    def join(ys):
        acc = jnp.concatenate([ctotal[:, y] for y in ys], axis=0)
        acc = jnp.maximum(acc.reshape(-1, 256) + bc[...], 0.0)
        acc = acc.reshape(4 * len(ys), 4, 8, 256)
        acc = jnp.concatenate(
            [(acc[:, s] * live[s])[:, None] for s in range(4)], axis=1
        )
        lifted = jnp.dot(
            acc.reshape(-1, 256).astype(BF16), wlv[...], preferred_element_type=F32
        ).reshape(len(ys), 4, 4, 8, 128)
        for k, y in enumerate(ys):
            for s in range(4):
                raised = lifted[k, :, s]
                for h in (0, 1):
                    for f in (0, 1):
                        at = (s, slice(0, 4), h, 2 * y + f)
                        out[at] = (out[at] + raised) * live[s]

    arrive(sent_coarse, SIDES[:2])
    x_rim(2, 2, 3, zcx)
    edges_beside_x(2, cedge_src)
    for d in (0, 1):
        lhs = jnp.concatenate(
            [zcx[d, ky : ky + 4].reshape(128, 384) for ky in range(3)], axis=1
        )
        rhs = wcv[2304 * d : 2304 * d + 1152]
        add = jnp.dot(lhs, rhs, preferred_element_type=F32)
        ctotal[3 * d] = ctotal[3 * d] + add.reshape(4, 32, 256)
    join((1, 2))

    def coarse_y(d):
        arrive_y(sent_coarse, d)
        edges_beside_y(2, cedge_src, crecv_edge, d)
        y_rim(2, 2, 3, cedge_src, zcy, d)
        lhs = jnp.concatenate(
            [zcy[d, kx : kx + 4].reshape(128, 384) for kx in range(3)], axis=1
        )
        rhs = jnp.concatenate(
            [
                wcv[1152 * kx + 768 * d : 1152 * kx + 768 * d + 384]
                for kx in range(3)
            ],
            axis=0,
        )
        add = jnp.dot(lhs, rhs, preferred_element_type=F32)
        ctotal[:, 3 * d] = ctotal[:, 3 * d] + add.reshape(4, 32, 256)
        join((3 * d,))

    by_turns(coarse_y)
    for described in (sent, sent_hidden, sent_coarse):
        for (ox, oy), copy in described.items():
            when_inside(-ox, -oy, copy.wait_send)


def local(gx, gy, features, slot_cell, neighbours, w1, b1, w2, b2, wc, bc, wl):
    operands = [
        pltpu.with_memory_space_constraint(operand, pltpu.HBM)
        for operand in (
            slot_cell.reshape(4),
            neighbours.reshape(4, 26),
            features.reshape(4, 8, 64, 128),
            w1.reshape(3, 3, 384, 128),
            b1.reshape(1, 128),
            w2.reshape(3, 3, 384, 128),
            b2.reshape(1, 128),
            wc.reshape(3456, 256),
            bc.reshape(1, 256),
            wl,
        )
    ]
    result = pl.pallas_call(
        functools.partial(kernel, gx, gy),
        out_shape=jax.ShapeDtypeStruct((4, 4, 2, 8, 8, 128), F32),
        in_specs=[pl.BlockSpec(memory_space=pl.ANY)] * 10,
        out_specs=pl.BlockSpec(memory_space=pltpu.VMEM),
        scratch_shapes=[
            pltpu.SMEM((4,), jnp.int32),
            pltpu.SMEM((4, 26), jnp.int32),
            pltpu.VMEM((1, 128), F32),
            pltpu.VMEM((1, 128), F32),
            pltpu.VMEM((1, 256), F32),
            pltpu.VMEM((4, 8, 64, 128), BF16),
            pltpu.VMEM((2, 4, 8, 16, 128), BF16),
            pltpu.VMEM((5, 4, 2, 8, 8, 128), F32),
            pltpu.VMEM((5, 4, 2, 8, 8, 128), F32),
            pltpu.VMEM((5, 4, 4, 8, 128), F32),
            pltpu.VMEM((4, 17, 1, 8, 128), F32),
            pltpu.VMEM((4, 17, 1, 8, 128), F32),
            pltpu.VMEM((2, 4, 10, 32, 384), BF16),
            pltpu.VMEM((2, 4, 10, 32, 384), BF16),
            pltpu.VMEM((2, 10, 32, 384), BF16),
            pltpu.VMEM((2, 10, 32, 384), BF16),
            pltpu.VMEM((6, 6, 32, 384), BF16),
            pltpu.VMEM((2, 6, 32, 384), BF16),
            pltpu.VMEM((2, 6, 32, 384), BF16),
            pltpu.VMEM((4, 3, 384, 256), BF16),
            pltpu.VMEM((4, 3, 384, 256), BF16),
            pltpu.VMEM((3456, 256), BF16),
            pltpu.VMEM((256, 128), BF16),
            pltpu.VMEM((4, 2, 8, 32, 128), F32),
            pltpu.VMEM((4, 4, 32, 256), F32),
            pltpu.VMEM((2, 4, 32, 128), BF16),
            pltpu.VMEM((2, 4, 32, 128), BF16),
            pltpu.VMEM((4, 32, 128), BF16),
            pltpu.VMEM((4, 32, 128), BF16),
            pltpu.SemaphoreType.DMA((12,)),
            pltpu.SemaphoreType.DMA((2,)),
            pltpu.SemaphoreType.DMA((3, 8)),
            pltpu.SemaphoreType.DMA((3, 8)),
        ]
        + [pltpu.VMEM((9, 64, 128), BF16)] * 8
        + [pltpu.VMEM((9, 32, 128), BF16)] * 4,
        compiler_params=pltpu.CompilerParams(
            collective_id=0, has_side_effects=True, vmem_limit_bytes=48 * 2**20
        ),
        cost_estimate=pl.CostEstimate(
            flops=8_000_000_000, bytes_accessed=8_000_000, transcendentals=0
        ),
        name="unet_window",
    )(*operands)
    return result.reshape(1, 1, 4, 512, 128)


def solution(mesh):
    placed = (
        P("gx", "gy", None, None, None),
        P("gx", "gy", None),
        P("gx", "gy", None, None),
    ) + (P(),) * 7
    return jax.shard_map(
        functools.partial(local, mesh.shape["gx"], mesh.shape["gy"]),
        mesh=mesh,
        in_specs=placed,
        out_specs=P("gx", "gy", None, None, None),
        check_vma=False,
    )
```

```python
import functools

import jax
import jax.numpy as jnp
from jax import lax
from jax.experimental import pallas as pl
from jax.experimental.pallas import tpu as pltpu
from jax.sharding import PartitionSpec as P

MESH = pl.DeviceIdType.MESH
F32 = jnp.float32
BF16 = jnp.bfloat16

OFFSETS = [
    (ox, oy, oz)
    for ox in (-1, 0, 1)
    for oy in (-1, 0, 1)
    for oz in (-1, 0, 1)
    if (ox, oy, oz) != (0, 0, 0)
]
NUMBER = {offset: k for k, offset in enumerate(OFFSETS)}
SIDES = [(-1, 0), (1, 0), (0, -1), (0, 1)]
EDGES = [(-1, -1), (-1, 1), (1, -1), (1, 1)]
ALL = SIDES + EDGES
FARTHEST = (4, 5, 6, 7, 2, 3, 0, 1)


def edges_on(oy):
    return [(k, edge) for k, edge in enumerate(EDGES) if edge[1] == oy]


def edge_of(step, last):
    return last if step < 0 else 0


def kernel(
    gx,
    gy,
    cell_hbm,
    nbr_hbm,
    feat,
    w1,
    b1_hbm,
    w2,
    b2_hbm,
    wc,
    bc_hbm,
    wl,
    out,
    cell,
    nbr,
    b1,
    b2,
    bc,
    staged,
    staged_rim,
    field,
    hidden,
    coarse_field,
    edge_src,
    cedge_src,
    zin,
    zhid,
    zx,
    zy,
    zc,
    zcx,
    zcy,
    w1p,
    w2p,
    wcv,
    wlv,
    total,
    ctotal,
    send_edge,
    recv_edge,
    csend_edge,
    crecv_edge,
    local_sem,
    rim_sem,
    send_sem,
    recv_sem,
    *side_refs,
):
    sides = [side_refs[4 * number : 4 * number + 4] for number in range(3)]
    mx = lax.axis_index("gx")
    my = lax.axis_index("gy")

    def device_at(ox, oy):
        return (lax.rem(mx + ox + gx, gx), lax.rem(my + oy + gy, gy))

    def inside(ox, oy):
        found = None
        for at, step, size in ((mx, ox, gx), (my, oy, gy)):
            if step != 0:
                here = at > 0 if step < 0 else at < size - 1
                found = here if found is None else jnp.logical_and(found, here)
        return found

    def when_inside(ox, oy, act):
        @pl.when(inside(ox, oy))
        def _():
            act()

    def signal_to(ox, oy):
        pl.semaphore_signal(
            barrier, inc=1, device_id=device_at(ox, oy), device_id_type=MESH
        )

    barrier = pltpu.get_barrier_semaphore()
    for k in FARTHEST:
        when_inside(*ALL[k], functools.partial(signal_to, *ALL[k]))
    beside_x = jnp.where(mx > 0, 1, 0) + jnp.where(mx < gx - 1, 1, 0)
    beside_y = jnp.where(my > 0, 1, 0) + jnp.where(my < gy - 1, 1, 0)
    partners = (1 + beside_x) * (1 + beside_y) - 1

    pairs = [
        (feat, staged),
        (cell_hbm, cell),
        (nbr_hbm, nbr),
        (b1_hbm, b1),
        (w1, w1p.at[0:3, :, :, 0:128]),
        (w1, w1p.at[1:4, :, :, 128:256]),
        (w2, w2p.at[0:3, :, :, 0:128]),
        (w2, w2p.at[1:4, :, :, 128:256]),
        (b2_hbm, b2),
        (wc, wcv),
        (wl, wlv),
        (bc_hbm, bc),
    ]
    copies = [
        pltpu.make_async_copy(src, dst, local_sem.at[k])
        for k, (src, dst) in enumerate(pairs)
    ]
    rims = [
        pltpu.make_async_copy(
            feat.at[:, :, 48 * d : 48 * d + 16], staged_rim.at[d], rim_sem.at[d]
        )
        for d in (0, 1)
    ]
    for copy in rims + copies[:4]:
        copy.start()

    def clear_weights(wp):
        wp[3, :, :, 0:128] = jnp.zeros((3, 384, 128), BF16)
        wp[0, :, :, 128:256] = jnp.zeros((3, 384, 128), BF16)

    def clear_ends(z):
        z[:, :, 0] = jnp.zeros((2, 4, 32, 384), BF16)
        z[:, :, 9] = jnp.zeros((2, 4, 32, 384), BF16)

    clear_weights(w1p)
    clear_ends(zin)
    field[4] = jnp.zeros((4, 2, 8, 8, 128), F32)
    for d in range(4):
        sides[0][d][8] = jnp.zeros((64, 128), BF16)
        edge_src[d, 16] = jnp.zeros((1, 8, 128), F32)

    def clear_later():
        clear_weights(w2p)
        clear_ends(zhid)
        hidden[4] = jnp.zeros((4, 2, 8, 8, 128), F32)
        coarse_field[4] = jnp.zeros((4, 4, 8, 128), F32)
        for d in range(4):
            for number, rows in ((1, 64), (2, 32)):
                sides[number][d][8] = jnp.zeros((rows, 128), BF16)
            cedge_src[d, 16] = jnp.zeros((1, 8, 128), F32)
        for side in range(2):
            for end in (0, 9):
                zx[side, end] = jnp.zeros((32, 384), BF16)
            for end in (0, 5):
                zcx[side, end] = jnp.zeros((32, 384), BF16)
        for end in (0, 5):
            zc[end] = jnp.zeros((6, 32, 384), BF16)
            zc[:, end] = jnp.zeros((6, 32, 384), BF16)

    for copy in rims:
        copy.wait()
    for copy in copies[4:6]:
        copy.start()

    def plane(source, s, x):
        if source is coarse_field:
            return source[s, x]
        return source[s, x // 2, x % 2]

    def across(source, s, y):
        if source is coarse_field:
            return source[s, :, y]
        if source is field:
            d = y // 7
            return staged_rim[d, s].astype(F32)[:, 8 * d : 8 * d + 8]
        return source[s, :, :, y].reshape(8, 8, 128)

    def column(source, s, x, y):
        if source is coarse_field:
            return source[s, x, y]
        if source is field:
            d = y // 7
            return staged_rim[d, s, x].astype(F32)[8 * d : 8 * d + 8]
        return source[s, x // 2, x % 2, y]

    def pack_side(number, source, last, d):
        ox, oy = SIDES[d]
        for s in range(4):
            if oy == 0:
                face = plane(source, s, edge_of(ox, last))
            else:
                face = across(source, s, edge_of(oy, last))
            sides[number][d][s] = face.reshape(8 * (last + 1), 128).astype(BF16)

    def pack_edges(source, last, edges, oy):
        for d, (ox, oy) in edges_on(oy):
            edges[d] = jnp.concatenate(
                [
                    column(source, s, edge_of(ox, last), edge_of(oy, last))
                    for s in range(4)
                ],
                axis=0,
            ).astype(BF16)

    def describe(number, edges, redges):
        described = {}
        for k in FARTHEST:
            ox, oy = ALL[k]
            if k < 4:
                src = sides[number][k].at[0:4]
                dst = sides[number][k].at[4:8]
                if number == 0 and oy == 0:
                    src = feat.at[:, edge_of(ox, 7)]
            else:
                src, dst = edges.at[k - 4], redges.at[k - 4]
            described[ox, oy] = pltpu.make_async_remote_copy(
                src_ref=src,
                dst_ref=dst,
                send_sem=send_sem.at[number, k],
                recv_sem=recv_sem.at[number, k],
                device_id=device_at(-ox, -oy),
                device_id_type=MESH,
            )
        return described

    def start(described, directions):
        for ox, oy in directions:
            when_inside(-ox, -oy, described[ox, oy].start)

    def left(described):
        for (ox, oy), copy in described.items():
            when_inside(-ox, -oy, copy.wait_send)

    def leave_y(number, described, source, last, edges, d):
        oy = 1 - 2 * d
        pack_edges(source, last, edges, oy)
        pack_side(number, source, last, 3 - d)
        start(described, [edge for _, edge in edges_on(oy)] + [(0, oy)])

    def leave_x(number, described, source, last):
        for d in (0, 1):
            pack_side(number, source, last, d)
        start(described, SIDES[:2])

    def arrive(described, directions):
        for ox, oy in directions:
            when_inside(ox, oy, described[ox, oy].wait_recv)

    sent = describe(0, send_edge.at[0], recv_edge.at[0])
    for oy in (-1, 1):
        pack_edges(field, 7, send_edge.at[0], oy)
    for d in (2, 3):
        pack_side(0, field, 7, d)
    pl.semaphore_wait(barrier, partners)
    start(sent, EDGES + SIDES[2:] + SIDES[:2])
    copies[0].wait()
    for s in range(4):
        for x in range(8):
            field[s, x // 2, x % 2] = staged[s, x].astype(F32).reshape(8, 8, 128)
        for d in (0, 1):
            sides[0][d][s] = staged[s, edge_of(SIDES[d][0], 7)]

    for k in (1, 2, 3):
        copies[k].wait()
    live = [jnp.where(cell[s] >= 0, 1.0, 0.0).astype(F32) for s in range(4)]

    def index(s, ox, oy, oz):
        if (ox, oy, oz) == (0, 0, 0):
            return s
        entry = nbr[s, NUMBER[ox, oy, oz]]
        safe = jnp.maximum(entry, 0)
        block = lax.shift_right_logical(safe, 2)
        slot = lax.bitwise_and(safe, 3)
        if (ox, oy) == (0, 0):
            return jnp.where(entry < 0, 4, slot)
        if ox == 0 or oy == 0:
            place = slot + jnp.where(block == 4, 0, 4)
            return jnp.where(entry < 0, 8, place)
        beside_x = (ox + 1) * 3 + 1
        beside_y = 3 + (oy + 1)
        place = slot + jnp.where(
            block == 4,
            0,
            jnp.where(block == beside_x, 4, jnp.where(block == beside_y, 8, 12)),
        )
        return jnp.where(entry < 0, 16, place)

    where = {
        (s, 0, 0, oz): index(s, 0, 0, oz) for s in range(4) for oz in (-1, 0, 1)
    }

    def index_rims():
        for s in range(4):
            for ox, oy in ALL:
                for oz in (-1, 0, 1):
                    where[s, ox, oy, oz] = index(s, ox, oy, oz)

    def shifted(low, own, high, step):
        row = lax.broadcasted_iota(jnp.int32, own.shape, own.ndim - 2)
        axis = own.ndim - 2
        down = pltpu.roll(jnp.where(row >= 8 - step, low, own), step, axis)
        up = pltpu.roll(jnp.where(row < step, high, own), 8 - step, axis)
        return down, own, up

    def pair(fetch, ox, oy, step):
        for half in (0, 1):
            parts = [
                shifted(*[fetch(where[s, ox, oy, oz]) for oz in (-1, 0, 1)], step)
                for s in (2 * half, 2 * half + 1)
            ]
            for kz in range(3):
                both = jnp.concatenate([parts[0][kz], parts[1][kz]], axis=-2)
                yield slice(16 * half, 16 * half + 16), slice(
                    128 * kz, 128 * kz + 128
                ), both.astype(BF16)

    def fine_centre(source, z):
        for m in range(4):
            for h in (0, 1):
                for rows, lanes, value in pair(lambda q: source[q, m, h], 0, 0, 1):
                    z[h, m, 1:9, rows, lanes] = value

    def face(number, d):
        def fetch(q):
            value = sides[number][d][q].astype(F32)
            return value.reshape(value.shape[0] // 8, 8, 128)

        return fetch

    def own_edges(source, last, edges):
        for d, (ox, oy) in enumerate(EDGES):
            for s in range(4):
                edges[d, s, 0] = column(
                    source, s, edge_of(ox, last), edge_of(oy, last)
                )

    def end_of(number, d, s, step):
        ref = sides[number][d]
        if step < 0:
            rows = ref.shape[1]
            return ref[4 + s, rows - 16 : rows].astype(F32)[8:16]
        return ref[4 + s, 0:16].astype(F32)[0:8]

    def edges_beside_x(number, edges):
        for k, (ox, oy) in enumerate(EDGES):
            for s in range(4):
                edges[k, 4 + s, 0] = end_of(number, SIDES.index((ox, 0)), s, oy)

    def edges_beside_y(number, edges, redges, d):
        for k, (ox, oy) in edges_on(2 * d - 1):
            far = redges[k].astype(F32)
            for s in range(4):
                edges[k, 8 + s, 0] = end_of(number, d + 2, s, ox)
                edges[k, 12 + s, 0] = far[8 * s : 8 * s + 8]

    def y_rim(number, step, last, edges, rim, d):
        for rows, lanes, value in pair(face(number, d + 2), *SIDES[d + 2], step):
            rim[d, 1 : last + 2, rows, lanes] = value
        for k, (ox, oy) in edges_on(2 * d - 1):
            x = 0 if ox < 0 else last + 2
            for rows, lanes, value in pair(lambda q: edges[k, q], ox, oy, step):
                rim[d, x, rows, lanes] = value[0]

    def arrive_y(described, d):
        arrive(described, [edge for _, edge in edges_on(2 * d - 1)] + [SIDES[d + 2]])

    def by_turns(step):
        far_low = lax.rem(my, 4) == 0

        @pl.when(far_low)
        def _():
            step(1)

        step(0)

        @pl.when(jnp.logical_not(far_low))
        def _():
            step(1)

    def x_rim(number, step, last, rim):
        for d in (0, 1):
            for rows, lanes, value in pair(face(number, d), *SIDES[d], step):
                rim[d, 1 : last + 2, rows, lanes] = value

    def centre_conv(z, wp, i):
        planes = [(1, i - 1), (0, i), (1, i), (0, i + 1)]
        used = [p for p in range(4) if 0 <= planes[p][1] < 4]
        lhs = jnp.concatenate(
            [
                z[planes[p][0], planes[p][1], ky : ky + 8].reshape(256, 384)
                for ky in range(3)
                for p in used
            ],
            axis=1,
        )
        rhs = jnp.concatenate([wp[p, ky] for ky in range(3) for p in used], axis=0)
        return jnp.dot(lhs, rhs, preferred_element_type=F32)

    def convolve(z, wp, finish):
        for i in range(4):
            acc = centre_conv(z, wp, i)
            for h in (0, 1):
                part = acc[:, 128 * h : 128 * h + 128].reshape(8, 32, 128)
                total[i, h] = part
                if 0 < 2 * i + h < 7:
                    inner = part[1:7].reshape(6, 4, 8, 128)
                    for s in range(4):
                        finish(s, (i, h, slice(1, 7)), inner[:, s])

    def add_x(number, described, wp, finish):
        arrive(described, SIDES[:2])
        x_rim(number, 1, 7, zx)
        edges_beside_x(number, edge_src)
        for d in (0, 1):
            i, h, p = (0, 0, 0) if d == 0 else (3, 1, 3)
            lhs = jnp.concatenate(
                [zx[d, ky : ky + 8].reshape(256, 384) for ky in range(3)], axis=1
            )
            rhs = jnp.concatenate(
                [wp[p, ky][:, 128 * h : 128 * h + 128] for ky in range(3)], axis=0
            )
            add = jnp.dot(lhs, rhs, preferred_element_type=F32).reshape(8, 32, 128)
            part = total[i, h] + add
            for y in (0, 7):
                total[i, h, y] = part[y]
            inner = part[1:7].reshape(6, 4, 8, 128)
            for s in range(4):
                finish(s, (i, h, slice(1, 7)), inner[:, s])

    def add_y(number, described, wp, finish, after):
        def step(d):
            arrive_y(described, d)
            edges_beside_y(number, edge_src, recv_edge.at[number], d)
            y_rim(number, 1, 7, edge_src, zy, d)
            y, ky = (0, 0) if d == 0 else (7, 2)
            lhs = jnp.concatenate(
                [zy[d, kx : kx + 8].reshape(256, 384) for kx in range(3)], axis=1
            )
            rhs = jnp.concatenate([wp[kx, ky][:, 0:128] for kx in range(3)], axis=0)
            add = jnp.dot(lhs, rhs, preferred_element_type=F32)
            part = total[:, :, y] + add.reshape(4, 2, 32, 128)
            part = part.reshape(4, 2, 4, 8, 128)
            for s in range(4):
                finish(s, (slice(0, 4), slice(0, 2), y), part[:, :, s])
            after(d)

        by_turns(step)

    copies[4].wait()
    copies[5].wait()
    for copy in copies[6:]:
        copy.start()
    fine_centre(field, zin)
    own_edges(field, 7, edge_src)
    index_rims()
    clear_later()

    def to_hidden(s, at, value):
        value = jnp.maximum(value + b1[...].reshape(1, 1, 128), 0.0) * live[s]
        hidden[(s,) + at] = value.astype(BF16).astype(F32)

    convolve(zin, w1p, to_hidden)
    add_x(0, sent, w1p, to_hidden)
    sent_hidden = describe(1, send_edge.at[1], recv_edge.at[1])
    add_y(
        0,
        sent,
        w1p,
        to_hidden,
        lambda d: leave_y(1, sent_hidden, hidden, 7, send_edge.at[1], d),
    )
    leave_x(1, sent_hidden, hidden, 7)
    for k in (6, 7, 8):
        copies[k].wait()
    own_edges(hidden, 7, edge_src)
    fine_centre(hidden, zhid)

    def to_fine(s, at, value):
        value = value + b2[...].reshape(1, 1, 128) + field[(s,) + at]
        out[(s,) + at] = value * live[s]

    def pooled(value):
        even = lax.broadcasted_iota(jnp.int32, value.shape, 1) % 2 == 0
        other = jnp.where(even, pltpu.roll(value, 7, 1), pltpu.roll(value, 1, 1))
        return ((value + other) * 0.125).astype(BF16).astype(F32)

    def pool(ys):
        for s in range(4):
            for y in ys:
                value = out[s, :, 0, 2 * y] + out[s, :, 1, 2 * y]
                value = value + out[s, :, 0, 2 * y + 1] + out[s, :, 1, 2 * y + 1]
                coarse_field[s, :, y] = pooled(value)

    convolve(zhid, w2p, to_fine)
    add_x(1, sent_hidden, w2p, to_fine)
    pool((1, 2))
    sent_coarse = describe(2, csend_edge, crecv_edge)

    def to_coarse(d):
        pool((3 * d,))
        leave_y(2, sent_coarse, coarse_field, 3, csend_edge, d)

    add_y(1, sent_hidden, w2p, to_fine, to_coarse)
    leave_x(2, sent_coarse, coarse_field, 3)

    own_edges(coarse_field, 3, cedge_src)
    for x in range(4):
        for rows, lanes, value in pair(lambda q: coarse_field[q, x], 0, 0, 2):
            zc[x + 1, 1:5, rows, lanes] = value
    for k in (9, 10, 11):
        copies[k].wait()
    lhs = jnp.concatenate(
        [
            zc[kx : kx + 4, ky : ky + 4].reshape(512, 384)
            for kx in range(3)
            for ky in range(3)
        ],
        axis=1,
    )
    acc = jnp.dot(lhs, wcv[...], preferred_element_type=F32)
    ctotal[...] = acc.reshape(4, 4, 32, 256)

    def join(ys):
        acc = jnp.concatenate([ctotal[:, y] for y in ys], axis=0)
        acc = jnp.maximum(acc.reshape(-1, 256) + bc[...], 0.0)
        acc = acc.reshape(4 * len(ys), 4, 8, 256)
        acc = jnp.concatenate(
            [(acc[:, s] * live[s])[:, None] for s in range(4)], axis=1
        )
        lifted = jnp.dot(
            acc.reshape(-1, 256).astype(BF16), wlv[...], preferred_element_type=F32
        ).reshape(len(ys), 4, 4, 8, 128)
        for k, y in enumerate(ys):
            for s in range(4):
                raised = lifted[k, :, s]
                for h in (0, 1):
                    for f in (0, 1):
                        at = (s, slice(0, 4), h, 2 * y + f)
                        out[at] = (out[at] + raised) * live[s]

    left(sent)
    left(sent_hidden)

    arrive(sent_coarse, SIDES[:2])
    x_rim(2, 2, 3, zcx)
    edges_beside_x(2, cedge_src)
    for d in (0, 1):
        lhs = jnp.concatenate(
            [zcx[d, ky : ky + 4].reshape(128, 384) for ky in range(3)], axis=1
        )
        rhs = wcv[2304 * d : 2304 * d + 1152]
        add = jnp.dot(lhs, rhs, preferred_element_type=F32)
        ctotal[3 * d] = ctotal[3 * d] + add.reshape(4, 32, 256)
    join((1, 2))
    left(sent_coarse)

    def coarse_y(d):
        arrive_y(sent_coarse, d)
        edges_beside_y(2, cedge_src, crecv_edge, d)
        y_rim(2, 2, 3, cedge_src, zcy, d)
        lhs = jnp.concatenate(
            [zcy[d, kx : kx + 4].reshape(128, 384) for kx in range(3)], axis=1
        )
        rhs = jnp.concatenate(
            [
                wcv[1152 * kx + 768 * d : 1152 * kx + 768 * d + 384]
                for kx in range(3)
            ],
            axis=0,
        )
        add = jnp.dot(lhs, rhs, preferred_element_type=F32)
        ctotal[:, 3 * d] = ctotal[:, 3 * d] + add.reshape(4, 32, 256)
        join((3 * d,))

    by_turns(coarse_y)


def local(gx, gy, features, slot_cell, neighbours, w1, b1, w2, b2, wc, bc, wl):
    operands = [
        pltpu.with_memory_space_constraint(operand, pltpu.HBM)
        for operand in (
            slot_cell.reshape(4),
            neighbours.reshape(4, 26),
            features.reshape(4, 8, 64, 128),
            w1.reshape(3, 3, 384, 128),
            b1.reshape(1, 128),
            w2.reshape(3, 3, 384, 128),
            b2.reshape(1, 128),
            wc.reshape(3456, 256),
            bc.reshape(1, 256),
            wl,
        )
    ]
    result = pl.pallas_call(
        functools.partial(kernel, gx, gy),
        out_shape=jax.ShapeDtypeStruct((4, 4, 2, 8, 8, 128), F32),
        in_specs=[pl.BlockSpec(memory_space=pl.ANY)] * 10,
        out_specs=pl.BlockSpec(memory_space=pltpu.VMEM),
        scratch_shapes=[
            pltpu.SMEM((4,), jnp.int32),
            pltpu.SMEM((4, 26), jnp.int32),
            pltpu.VMEM((1, 128), F32),
            pltpu.VMEM((1, 128), F32),
            pltpu.VMEM((1, 256), F32),
            pltpu.VMEM((4, 8, 64, 128), BF16),
            pltpu.VMEM((2, 4, 8, 16, 128), BF16),
            pltpu.VMEM((5, 4, 2, 8, 8, 128), F32),
            pltpu.VMEM((5, 4, 2, 8, 8, 128), F32),
            pltpu.VMEM((5, 4, 4, 8, 128), F32),
            pltpu.VMEM((4, 17, 1, 8, 128), F32),
            pltpu.VMEM((4, 17, 1, 8, 128), F32),
            pltpu.VMEM((2, 4, 10, 32, 384), BF16),
            pltpu.VMEM((2, 4, 10, 32, 384), BF16),
            pltpu.VMEM((2, 10, 32, 384), BF16),
            pltpu.VMEM((2, 10, 32, 384), BF16),
            pltpu.VMEM((6, 6, 32, 384), BF16),
            pltpu.VMEM((2, 6, 32, 384), BF16),
            pltpu.VMEM((2, 6, 32, 384), BF16),
            pltpu.VMEM((4, 3, 384, 256), BF16),
            pltpu.VMEM((4, 3, 384, 256), BF16),
            pltpu.VMEM((3456, 256), BF16),
            pltpu.VMEM((256, 128), BF16),
            pltpu.VMEM((4, 2, 8, 32, 128), F32),
            pltpu.VMEM((4, 4, 32, 256), F32),
            pltpu.VMEM((2, 4, 32, 128), BF16),
            pltpu.VMEM((2, 4, 32, 128), BF16),
            pltpu.VMEM((4, 32, 128), BF16),
            pltpu.VMEM((4, 32, 128), BF16),
            pltpu.SemaphoreType.DMA((12,)),
            pltpu.SemaphoreType.DMA((2,)),
            pltpu.SemaphoreType.DMA((3, 8)),
            pltpu.SemaphoreType.DMA((3, 8)),
        ]
        + [pltpu.VMEM((9, 64, 128), BF16)] * 8
        + [pltpu.VMEM((9, 32, 128), BF16)] * 4,
        compiler_params=pltpu.CompilerParams(
            collective_id=0, has_side_effects=True, vmem_limit_bytes=48 * 2**20
        ),
        cost_estimate=pl.CostEstimate(
            flops=8_000_000_000, bytes_accessed=8_000_000, transcendentals=0
        ),
        name="unet_window",
    )(*operands)
    return result.reshape(1, 1, 4, 512, 128)


def solution(mesh):
    placed = (
        P("gx", "gy", None, None, None),
        P("gx", "gy", None),
        P("gx", "gy", None, None),
    ) + (P(),) * 7
    return jax.shard_map(
        functools.partial(local, mesh.shape["gx"], mesh.shape["gy"]),
        mesh=mesh,
        in_specs=placed,
        out_specs=P("gx", "gy", None, None, None),
        check_vma=False,
    )
```

```python
import functools

import jax
import jax.numpy as jnp
from jax import lax
from jax.experimental import pallas as pl
from jax.experimental.pallas import tpu as pltpu
from jax.sharding import PartitionSpec as P

MESH = pl.DeviceIdType.MESH
F32 = jnp.float32
BF16 = jnp.bfloat16

OFFSETS = [
    (ox, oy, oz)
    for ox in (-1, 0, 1)
    for oy in (-1, 0, 1)
    for oz in (-1, 0, 1)
    if (ox, oy, oz) != (0, 0, 0)
]
NUMBER = {offset: k for k, offset in enumerate(OFFSETS)}
SIDES = [(-1, 0), (1, 0), (0, -1), (0, 1)]
EDGES = [(-1, -1), (-1, 1), (1, -1), (1, 1)]
ALL = SIDES + EDGES
FARTHEST = (4, 5, 6, 7, 2, 3, 0, 1)


def edges_on(oy):
    return [(k, edge) for k, edge in enumerate(EDGES) if edge[1] == oy]


def edge_of(step, last):
    return last if step < 0 else 0


def kernel(
    gx,
    gy,
    cell_hbm,
    nbr_hbm,
    feat,
    w1,
    b1_hbm,
    w2,
    b2_hbm,
    wc,
    bc_hbm,
    wl,
    out,
    cell,
    nbr,
    b1,
    b2,
    bc,
    staged,
    staged_rim,
    field,
    hidden,
    coarse_field,
    edge_src,
    cedge_src,
    zin,
    zhid,
    zx,
    zy,
    zc,
    zcx,
    zcy,
    w1p,
    w2p,
    wcv,
    wlv,
    total,
    ctotal,
    send_edge,
    recv_edge,
    csend_edge,
    crecv_edge,
    local_sem,
    rim_sem,
    send_sem,
    recv_sem,
    *side_refs,
):
    sides = [side_refs[4 * number : 4 * number + 4] for number in range(3)]
    mx = lax.axis_index("gx")
    my = lax.axis_index("gy")

    def device_at(ox, oy):
        return (lax.rem(mx + ox + gx, gx), lax.rem(my + oy + gy, gy))

    def inside(ox, oy):
        found = None
        for at, step, size in ((mx, ox, gx), (my, oy, gy)):
            if step != 0:
                here = at > 0 if step < 0 else at < size - 1
                found = here if found is None else jnp.logical_and(found, here)
        return found

    def when_inside(ox, oy, act):
        @pl.when(inside(ox, oy))
        def _():
            act()

    def signal_to(ox, oy):
        pl.semaphore_signal(
            barrier, inc=1, device_id=device_at(ox, oy), device_id_type=MESH
        )

    barrier = pltpu.get_barrier_semaphore()
    for k in FARTHEST:
        when_inside(*ALL[k], functools.partial(signal_to, *ALL[k]))
    beside_x = jnp.where(mx > 0, 1, 0) + jnp.where(mx < gx - 1, 1, 0)
    beside_y = jnp.where(my > 0, 1, 0) + jnp.where(my < gy - 1, 1, 0)
    partners = (1 + beside_x) * (1 + beside_y) - 1

    pairs = [
        (feat, staged),
        (cell_hbm, cell),
        (nbr_hbm, nbr),
        (b1_hbm, b1),
        (w1, w1p.at[0:3, :, :, 0:128]),
        (w1, w1p.at[1:4, :, :, 128:256]),
        (w2, w2p.at[0:3, :, :, 0:128]),
        (w2, w2p.at[1:4, :, :, 128:256]),
        (b2_hbm, b2),
        (wc, wcv),
        (wl, wlv),
        (bc_hbm, bc),
    ]
    copies = [
        pltpu.make_async_copy(src, dst, local_sem.at[k])
        for k, (src, dst) in enumerate(pairs)
    ]
    rims = [
        pltpu.make_async_copy(
            feat.at[:, :, 48 * d : 48 * d + 16], staged_rim.at[d], rim_sem.at[d]
        )
        for d in (0, 1)
    ]
    for copy in rims + copies[:4]:
        copy.start()

    def clear_weights(wp):
        wp[3, :, :, 0:128] = jnp.zeros((3, 384, 128), BF16)
        wp[0, :, :, 128:256] = jnp.zeros((3, 384, 128), BF16)

    def clear_ends(z):
        z[:, :, 0] = jnp.zeros((2, 4, 32, 384), BF16)
        z[:, :, 9] = jnp.zeros((2, 4, 32, 384), BF16)

    clear_weights(w1p)
    clear_ends(zin)
    field[4] = jnp.zeros((4, 2, 8, 8, 128), F32)
    for d in range(4):
        sides[0][d][8] = jnp.zeros((64, 128), BF16)
        edge_src[d, 16] = jnp.zeros((1, 8, 128), F32)

    def clear_later():
        clear_weights(w2p)
        clear_ends(zhid)
        hidden[4] = jnp.zeros((4, 2, 8, 8, 128), F32)
        coarse_field[4] = jnp.zeros((4, 4, 8, 128), F32)
        for d in range(4):
            for number, rows in ((1, 64), (2, 32)):
                sides[number][d][4 if number == 2 else 8] = jnp.zeros(
                    (rows, 128), BF16
                )
            cedge_src[d, 16] = jnp.zeros((1, 8, 128), F32)
        for side in range(2):
            for end in (0, 9):
                zx[side, end] = jnp.zeros((32, 384), BF16)
            for end in (0, 5):
                zcx[side, end] = jnp.zeros((32, 384), BF16)
        for end in (0, 5):
            zc[end] = jnp.zeros((6, 32, 384), BF16)
            zc[:, end] = jnp.zeros((6, 32, 384), BF16)

    for copy in rims:
        copy.wait()
    for copy in copies[4:6]:
        copy.start()

    def plane(source, s, x):
        if source is coarse_field:
            return source[s, x]
        return source[s, x // 2, x % 2]

    def across(source, s, y):
        if source is coarse_field:
            return source[s, :, y]
        if source is field:
            d = y // 7
            return staged_rim[d, s].astype(F32)[:, 8 * d : 8 * d + 8]
        return source[s, :, :, y].reshape(8, 8, 128)

    def column(source, s, x, y):
        if source is coarse_field:
            return source[s, x, y]
        if source is field:
            d = y // 7
            return staged_rim[d, s, x].astype(F32)[8 * d : 8 * d + 8]
        return source[s, x // 2, x % 2, y]

    def pack_side(number, source, last, d):
        ox, oy = SIDES[d]
        faces = []
        for s in range(4):
            if oy == 0:
                faces.append(plane(source, s, edge_of(ox, last)))
            else:
                faces.append(across(source, s, edge_of(oy, last)))
        if number == 2:
            even = lax.broadcasted_iota(jnp.int32, faces[0].shape, 1) % 2 == 0
            faces = [
                jnp.where(even, faces[2 * k], faces[2 * k + 1]) for k in (0, 1)
            ]
        for k, value in enumerate(faces):
            sides[number][d][k] = value.reshape(8 * (last + 1), 128).astype(BF16)

    def doubled(value, parity):
        axis = value.ndim - 2
        row = lax.broadcasted_iota(jnp.int32, value.shape, axis) % 2
        after = pltpu.roll(value, 1, axis)
        before = pltpu.roll(value, 7, axis)
        return jnp.where(
            row == parity, value, jnp.where(row == 1, after, before)
        )

    def pack_edges(source, last, edges, oy):
        for d, (ox, oy) in edges_on(oy):
            edges[d] = jnp.concatenate(
                [
                    column(source, s, edge_of(ox, last), edge_of(oy, last))
                    for s in range(4)
                ],
                axis=0,
            ).astype(BF16)

    def describe(number, edges, redges):
        described = {}
        for k in FARTHEST:
            ox, oy = ALL[k]
            if k < 4:
                count = 2 if number == 2 else 4
                src = sides[number][k].at[0:count]
                dst = sides[number][k].at[count : 2 * count]
                if number == 0 and oy == 0:
                    src = feat.at[:, edge_of(ox, 7)]
            else:
                src, dst = edges.at[k - 4], redges.at[k - 4]
            described[ox, oy] = pltpu.make_async_remote_copy(
                src_ref=src,
                dst_ref=dst,
                send_sem=send_sem.at[number, k],
                recv_sem=recv_sem.at[number, k],
                device_id=device_at(-ox, -oy),
                device_id_type=MESH,
            )
        return described

    def start(described, directions):
        for ox, oy in directions:
            when_inside(-ox, -oy, described[ox, oy].start)

    def left(described):
        for (ox, oy), copy in described.items():
            when_inside(-ox, -oy, copy.wait_send)

    def leave_y(number, described, source, last, edges, d):
        oy = 1 - 2 * d
        pack_edges(source, last, edges, oy)
        pack_side(number, source, last, 3 - d)
        start(described, [edge for _, edge in edges_on(oy)] + [(0, oy)])

    def leave_x(number, described, source, last):
        for d in (0, 1):
            pack_side(number, source, last, d)
        start(described, SIDES[:2])

    def arrive(described, directions):
        for ox, oy in directions:
            when_inside(ox, oy, described[ox, oy].wait_recv)

    sent = describe(0, send_edge.at[0], recv_edge.at[0])
    for oy in (-1, 1):
        pack_edges(field, 7, send_edge.at[0], oy)
    for d in (2, 3):
        pack_side(0, field, 7, d)
    pl.semaphore_wait(barrier, partners)
    start(sent, EDGES + SIDES[2:] + SIDES[:2])
    copies[0].wait()
    for s in range(4):
        for x in range(8):
            field[s, x // 2, x % 2] = staged[s, x].astype(F32).reshape(8, 8, 128)
        for d in (0, 1):
            sides[0][d][s] = staged[s, edge_of(SIDES[d][0], 7)]

    for k in (1, 2, 3):
        copies[k].wait()
    live = [jnp.where(cell[s] >= 0, 1.0, 0.0).astype(F32) for s in range(4)]

    def index(s, ox, oy, oz):
        if (ox, oy, oz) == (0, 0, 0):
            return s
        entry = nbr[s, NUMBER[ox, oy, oz]]
        safe = jnp.maximum(entry, 0)
        block = lax.shift_right_logical(safe, 2)
        slot = lax.bitwise_and(safe, 3)
        if (ox, oy) == (0, 0):
            return jnp.where(entry < 0, 4, slot)
        if ox == 0 or oy == 0:
            place = slot + jnp.where(block == 4, 0, 4)
            return jnp.where(entry < 0, 8, place)
        beside_x = (ox + 1) * 3 + 1
        beside_y = 3 + (oy + 1)
        place = slot + jnp.where(
            block == 4,
            0,
            jnp.where(block == beside_x, 4, jnp.where(block == beside_y, 8, 12)),
        )
        return jnp.where(entry < 0, 16, place)

    where = {
        (s, 0, 0, oz): index(s, 0, 0, oz) for s in range(4) for oz in (-1, 0, 1)
    }

    def index_rims():
        for s in range(4):
            for ox, oy in ALL:
                for oz in (-1, 0, 1):
                    where[s, ox, oy, oz] = index(s, ox, oy, oz)

    def shifted(low, own, high, step):
        row = lax.broadcasted_iota(jnp.int32, own.shape, own.ndim - 2)
        axis = own.ndim - 2
        down = pltpu.roll(jnp.where(row >= 8 - step, low, own), step, axis)
        up = pltpu.roll(jnp.where(row < step, high, own), 8 - step, axis)
        return down, own, up

    def pair(fetch, ox, oy, step):
        for half in (0, 1):
            parts = [
                shifted(*[fetch(where[s, ox, oy, oz]) for oz in (-1, 0, 1)], step)
                for s in (2 * half, 2 * half + 1)
            ]
            for kz in range(3):
                both = jnp.concatenate([parts[0][kz], parts[1][kz]], axis=-2)
                yield slice(16 * half, 16 * half + 16), slice(
                    128 * kz, 128 * kz + 128
                ), both.astype(BF16)

    def fine_centre(source, z):
        for m in range(4):
            for h in (0, 1):
                for rows, lanes, value in pair(lambda q: source[q, m, h], 0, 0, 1):
                    z[h, m, 1:9, rows, lanes] = value

    def face(number, d):
        def fetch(q):
            if number == 2:
                value = sides[2][d][lax.shift_right_logical(q, 1)].astype(F32)
                return doubled(value.reshape(4, 8, 128), lax.bitwise_and(q, 1))
            return sides[number][d][q].astype(F32).reshape(8, 8, 128)

        return fetch

    def own_edges(source, last, edges):
        for d, (ox, oy) in enumerate(EDGES):
            for s in range(4):
                edges[d, s, 0] = column(
                    source, s, edge_of(ox, last), edge_of(oy, last)
                )

    def end_of(number, d, s, step):
        ref = sides[number][d]
        at = 2 + s // 2 if number == 2 else 4 + s
        if step < 0:
            rows = ref.shape[1]
            value = ref[at, rows - 16 : rows].astype(F32)[8:16]
        else:
            value = ref[at, 0:16].astype(F32)[0:8]
        return doubled(value, s % 2) if number == 2 else value

    def edges_beside_x(number, edges):
        for k, (ox, oy) in enumerate(EDGES):
            for s in range(4):
                edges[k, 4 + s, 0] = end_of(number, SIDES.index((ox, 0)), s, oy)

    def edges_beside_y(number, edges, redges, d):
        for k, (ox, oy) in edges_on(2 * d - 1):
            far = redges[k].astype(F32)
            for s in range(4):
                edges[k, 8 + s, 0] = end_of(number, d + 2, s, ox)
                edges[k, 12 + s, 0] = far[8 * s : 8 * s + 8]

    def y_rim(number, step, last, edges, rim, d):
        for rows, lanes, value in pair(face(number, d + 2), *SIDES[d + 2], step):
            rim[d, 1 : last + 2, rows, lanes] = value
        for k, (ox, oy) in edges_on(2 * d - 1):
            x = 0 if ox < 0 else last + 2
            for rows, lanes, value in pair(lambda q: edges[k, q], ox, oy, step):
                rim[d, x, rows, lanes] = value[0]

    def arrive_y(described, d):
        arrive(described, [edge for _, edge in edges_on(2 * d - 1)] + [SIDES[d + 2]])

    def by_turns(step):
        far_low = lax.rem(my, 4) == 0

        @pl.when(far_low)
        def _():
            step(1)

        step(0)

        @pl.when(jnp.logical_not(far_low))
        def _():
            step(1)

    def x_rim(number, step, last, rim):
        for d in (0, 1):
            for rows, lanes, value in pair(face(number, d), *SIDES[d], step):
                rim[d, 1 : last + 2, rows, lanes] = value

    def centre_conv(z, wp, i):
        planes = [(1, i - 1), (0, i), (1, i), (0, i + 1)]
        used = [p for p in range(4) if 0 <= planes[p][1] < 4]
        lhs = jnp.concatenate(
            [
                z[planes[p][0], planes[p][1], ky : ky + 8].reshape(256, 384)
                for ky in range(3)
                for p in used
            ],
            axis=1,
        )
        rhs = jnp.concatenate([wp[p, ky] for ky in range(3) for p in used], axis=0)
        return jnp.dot(lhs, rhs, preferred_element_type=F32)

    def convolve(z, wp, finish):
        for i in range(4):
            acc = centre_conv(z, wp, i)
            for h in (0, 1):
                part = acc[:, 128 * h : 128 * h + 128].reshape(8, 32, 128)
                total[i, h] = part
                if 0 < 2 * i + h < 7:
                    inner = part[1:7].reshape(6, 4, 8, 128)
                    for s in range(4):
                        finish(s, (i, h, slice(1, 7)), inner[:, s])

    def add_x(number, described, wp, finish):
        arrive(described, SIDES[:2])
        x_rim(number, 1, 7, zx)
        edges_beside_x(number, edge_src)
        for d in (0, 1):
            i, h, p = (0, 0, 0) if d == 0 else (3, 1, 3)
            lhs = jnp.concatenate(
                [zx[d, ky : ky + 8].reshape(256, 384) for ky in range(3)], axis=1
            )
            rhs = jnp.concatenate(
                [wp[p, ky][:, 128 * h : 128 * h + 128] for ky in range(3)], axis=0
            )
            add = jnp.dot(lhs, rhs, preferred_element_type=F32).reshape(8, 32, 128)
            part = total[i, h] + add
            for y in (0, 7):
                total[i, h, y] = part[y]
            inner = part[1:7].reshape(6, 4, 8, 128)
            for s in range(4):
                finish(s, (i, h, slice(1, 7)), inner[:, s])

    def add_y(number, described, wp, finish, after):
        def step(d):
            arrive_y(described, d)
            edges_beside_y(number, edge_src, recv_edge.at[number], d)
            y_rim(number, 1, 7, edge_src, zy, d)
            y, ky = (0, 0) if d == 0 else (7, 2)
            lhs = jnp.concatenate(
                [zy[d, kx : kx + 8].reshape(256, 384) for kx in range(3)], axis=1
            )
            rhs = jnp.concatenate([wp[kx, ky][:, 0:128] for kx in range(3)], axis=0)
            add = jnp.dot(lhs, rhs, preferred_element_type=F32)
            part = total[:, :, y] + add.reshape(4, 2, 32, 128)
            part = part.reshape(4, 2, 4, 8, 128)
            for s in range(4):
                finish(s, (slice(0, 4), slice(0, 2), y), part[:, :, s])
            after(d)

        by_turns(step)

    copies[4].wait()
    copies[5].wait()
    for copy in copies[6:]:
        copy.start()
    fine_centre(field, zin)
    own_edges(field, 7, edge_src)
    index_rims()
    clear_later()

    def to_hidden(s, at, value):
        value = jnp.maximum(value + b1[...].reshape(1, 1, 128), 0.0) * live[s]
        hidden[(s,) + at] = value.astype(BF16).astype(F32)

    convolve(zin, w1p, to_hidden)
    add_x(0, sent, w1p, to_hidden)
    sent_hidden = describe(1, send_edge.at[1], recv_edge.at[1])
    add_y(
        0,
        sent,
        w1p,
        to_hidden,
        lambda d: leave_y(1, sent_hidden, hidden, 7, send_edge.at[1], d),
    )
    leave_x(1, sent_hidden, hidden, 7)
    for k in (6, 7, 8):
        copies[k].wait()
    own_edges(hidden, 7, edge_src)
    fine_centre(hidden, zhid)

    def to_fine(s, at, value):
        value = value + b2[...].reshape(1, 1, 128) + field[(s,) + at]
        out[(s,) + at] = value * live[s]

    def pooled(value):
        even = lax.broadcasted_iota(jnp.int32, value.shape, 1) % 2 == 0
        other = jnp.where(even, pltpu.roll(value, 7, 1), pltpu.roll(value, 1, 1))
        return ((value + other) * 0.125).astype(BF16).astype(F32)

    def pool(ys):
        for s in range(4):
            for y in ys:
                value = out[s, :, 0, 2 * y] + out[s, :, 1, 2 * y]
                value = value + out[s, :, 0, 2 * y + 1] + out[s, :, 1, 2 * y + 1]
                coarse_field[s, :, y] = pooled(value)

    convolve(zhid, w2p, to_fine)
    add_x(1, sent_hidden, w2p, to_fine)
    pool((1, 2))
    sent_coarse = describe(2, csend_edge, crecv_edge)

    def to_coarse(d):
        pool((3 * d,))
        leave_y(2, sent_coarse, coarse_field, 3, csend_edge, d)

    add_y(1, sent_hidden, w2p, to_fine, to_coarse)
    leave_x(2, sent_coarse, coarse_field, 3)

    own_edges(coarse_field, 3, cedge_src)
    for x in range(4):
        for rows, lanes, value in pair(lambda q: coarse_field[q, x], 0, 0, 2):
            zc[x + 1, 1:5, rows, lanes] = value
    for k in (9, 10, 11):
        copies[k].wait()
    lhs = jnp.concatenate(
        [
            zc[kx : kx + 4, ky : ky + 4].reshape(512, 384)
            for kx in range(3)
            for ky in range(3)
        ],
        axis=1,
    )
    acc = jnp.dot(lhs, wcv[...], preferred_element_type=F32)
    ctotal[...] = acc.reshape(4, 4, 32, 256)

    def join(ys):
        acc = jnp.concatenate([ctotal[:, y] for y in ys], axis=0)
        acc = jnp.maximum(acc.reshape(-1, 256) + bc[...], 0.0)
        acc = acc.reshape(4 * len(ys), 4, 8, 256)
        acc = jnp.concatenate(
            [(acc[:, s] * live[s])[:, None] for s in range(4)], axis=1
        )
        lifted = jnp.dot(
            acc.reshape(-1, 256).astype(BF16), wlv[...], preferred_element_type=F32
        ).reshape(len(ys), 4, 4, 8, 128)
        for k, y in enumerate(ys):
            for s in range(4):
                raised = lifted[k, :, s]
                for h in (0, 1):
                    for f in (0, 1):
                        at = (s, slice(0, 4), h, 2 * y + f)
                        out[at] = (out[at] + raised) * live[s]

    left(sent)
    left(sent_hidden)

    arrive(sent_coarse, SIDES[:2])
    x_rim(2, 2, 3, zcx)
    edges_beside_x(2, cedge_src)
    for d in (0, 1):
        lhs = jnp.concatenate(
            [zcx[d, ky : ky + 4].reshape(128, 384) for ky in range(3)], axis=1
        )
        rhs = wcv[2304 * d : 2304 * d + 1152]
        add = jnp.dot(lhs, rhs, preferred_element_type=F32)
        ctotal[3 * d] = ctotal[3 * d] + add.reshape(4, 32, 256)
    join((1, 2))
    left(sent_coarse)

    def coarse_y(d):
        arrive_y(sent_coarse, d)
        edges_beside_y(2, cedge_src, crecv_edge, d)
        y_rim(2, 2, 3, cedge_src, zcy, d)
        lhs = jnp.concatenate(
            [zcy[d, kx : kx + 4].reshape(128, 384) for kx in range(3)], axis=1
        )
        rhs = jnp.concatenate(
            [
                wcv[1152 * kx + 768 * d : 1152 * kx + 768 * d + 384]
                for kx in range(3)
            ],
            axis=0,
        )
        add = jnp.dot(lhs, rhs, preferred_element_type=F32)
        ctotal[:, 3 * d] = ctotal[:, 3 * d] + add.reshape(4, 32, 256)
        join((3 * d,))

    by_turns(coarse_y)


def local(gx, gy, features, slot_cell, neighbours, w1, b1, w2, b2, wc, bc, wl):
    operands = [
        pltpu.with_memory_space_constraint(operand, pltpu.HBM)
        for operand in (
            slot_cell.reshape(4),
            neighbours.reshape(4, 26),
            features.reshape(4, 8, 64, 128),
            w1.reshape(3, 3, 384, 128),
            b1.reshape(1, 128),
            w2.reshape(3, 3, 384, 128),
            b2.reshape(1, 128),
            wc.reshape(3456, 256),
            bc.reshape(1, 256),
            wl,
        )
    ]
    result = pl.pallas_call(
        functools.partial(kernel, gx, gy),
        out_shape=jax.ShapeDtypeStruct((4, 4, 2, 8, 8, 128), F32),
        in_specs=[pl.BlockSpec(memory_space=pl.ANY)] * 10,
        out_specs=pl.BlockSpec(memory_space=pltpu.VMEM),
        scratch_shapes=[
            pltpu.SMEM((4,), jnp.int32),
            pltpu.SMEM((4, 26), jnp.int32),
            pltpu.VMEM((1, 128), F32),
            pltpu.VMEM((1, 128), F32),
            pltpu.VMEM((1, 256), F32),
            pltpu.VMEM((4, 8, 64, 128), BF16),
            pltpu.VMEM((2, 4, 8, 16, 128), BF16),
            pltpu.VMEM((5, 4, 2, 8, 8, 128), F32),
            pltpu.VMEM((5, 4, 2, 8, 8, 128), F32),
            pltpu.VMEM((5, 4, 4, 8, 128), F32),
            pltpu.VMEM((4, 17, 1, 8, 128), F32),
            pltpu.VMEM((4, 17, 1, 8, 128), F32),
            pltpu.VMEM((2, 4, 10, 32, 384), BF16),
            pltpu.VMEM((2, 4, 10, 32, 384), BF16),
            pltpu.VMEM((2, 10, 32, 384), BF16),
            pltpu.VMEM((2, 10, 32, 384), BF16),
            pltpu.VMEM((6, 6, 32, 384), BF16),
            pltpu.VMEM((2, 6, 32, 384), BF16),
            pltpu.VMEM((2, 6, 32, 384), BF16),
            pltpu.VMEM((4, 3, 384, 256), BF16),
            pltpu.VMEM((4, 3, 384, 256), BF16),
            pltpu.VMEM((3456, 256), BF16),
            pltpu.VMEM((256, 128), BF16),
            pltpu.VMEM((4, 2, 8, 32, 128), F32),
            pltpu.VMEM((4, 4, 32, 256), F32),
            pltpu.VMEM((2, 4, 32, 128), BF16),
            pltpu.VMEM((2, 4, 32, 128), BF16),
            pltpu.VMEM((4, 32, 128), BF16),
            pltpu.VMEM((4, 32, 128), BF16),
            pltpu.SemaphoreType.DMA((12,)),
            pltpu.SemaphoreType.DMA((2,)),
            pltpu.SemaphoreType.DMA((3, 8)),
            pltpu.SemaphoreType.DMA((3, 8)),
        ]
        + [pltpu.VMEM((9, 64, 128), BF16)] * 8
        + [pltpu.VMEM((5, 32, 128), BF16)] * 4,
        compiler_params=pltpu.CompilerParams(
            collective_id=0, has_side_effects=True, vmem_limit_bytes=48 * 2**20
        ),
        cost_estimate=pl.CostEstimate(
            flops=8_000_000_000, bytes_accessed=8_000_000, transcendentals=0
        ),
        name="unet_window",
    )(*operands)
    return result.reshape(1, 1, 4, 512, 128)


def solution(mesh):
    placed = (
        P("gx", "gy", None, None, None),
        P("gx", "gy", None),
        P("gx", "gy", None, None),
    ) + (P(),) * 7
    return jax.shard_map(
        functools.partial(local, mesh.shape["gx"], mesh.shape["gy"]),
        mesh=mesh,
        in_specs=placed,
        out_specs=P("gx", "gy", None, None, None),
        check_vma=False,
    )
```

```python
import functools

import jax
import jax.numpy as jnp
from jax import lax
from jax.experimental import pallas as pl
from jax.experimental.pallas import tpu as pltpu
from jax.sharding import PartitionSpec as P

MESH = pl.DeviceIdType.MESH
F32 = jnp.float32
BF16 = jnp.bfloat16

OFFSETS = [
    (ox, oy, oz)
    for ox in (-1, 0, 1)
    for oy in (-1, 0, 1)
    for oz in (-1, 0, 1)
    if (ox, oy, oz) != (0, 0, 0)
]
NUMBER = {offset: k for k, offset in enumerate(OFFSETS)}
SIDES = [(-1, 0), (1, 0), (0, -1), (0, 1)]
EDGES = [(-1, -1), (-1, 1), (1, -1), (1, 1)]
ALL = SIDES + EDGES
FARTHEST = (4, 5, 6, 7, 2, 3, 0, 1)


def edges_on(oy):
    return [(k, edge) for k, edge in enumerate(EDGES) if edge[1] == oy]


def edge_of(step, last):
    return last if step < 0 else 0


def kernel(
    gx,
    gy,
    cell_hbm,
    nbr_hbm,
    feat,
    w1,
    b1_hbm,
    w2,
    b2_hbm,
    wc,
    bc_hbm,
    wl,
    out,
    cell,
    nbr,
    b1,
    b2,
    bc,
    staged,
    staged_rim,
    field,
    hidden,
    coarse_field,
    edge_src,
    cedge_src,
    zin,
    zhid,
    zx,
    zy,
    zc,
    zcx,
    zcy,
    w1p,
    w2p,
    wcv,
    wlv,
    total,
    ctotal,
    send_edge,
    recv_edge,
    csend_edge,
    crecv_edge,
    local_sem,
    rim_sem,
    send_sem,
    recv_sem,
    *side_refs,
):
    sides = [side_refs[4 * number : 4 * number + 4] for number in range(3)]
    mx = lax.axis_index("gx")
    my = lax.axis_index("gy")

    def device_at(ox, oy):
        return (lax.rem(mx + ox + gx, gx), lax.rem(my + oy + gy, gy))

    def inside(ox, oy):
        found = None
        for at, step, size in ((mx, ox, gx), (my, oy, gy)):
            if step != 0:
                here = at > 0 if step < 0 else at < size - 1
                found = here if found is None else jnp.logical_and(found, here)
        return found

    def when_inside(ox, oy, act):
        @pl.when(inside(ox, oy))
        def _():
            act()

    def signal_to(ox, oy):
        pl.semaphore_signal(
            barrier, inc=1, device_id=device_at(ox, oy), device_id_type=MESH
        )

    barrier = pltpu.get_barrier_semaphore()
    for k in FARTHEST:
        when_inside(*ALL[k], functools.partial(signal_to, *ALL[k]))
    beside_x = jnp.where(mx > 0, 1, 0) + jnp.where(mx < gx - 1, 1, 0)
    beside_y = jnp.where(my > 0, 1, 0) + jnp.where(my < gy - 1, 1, 0)
    partners = (1 + beside_x) * (1 + beside_y) - 1

    pairs = [
        (feat, staged),
        (cell_hbm, cell),
        (nbr_hbm, nbr),
        (b1_hbm, b1),
        (w1, w1p.at[0:3, :, :, 0:128]),
        (w1, w1p.at[1:4, :, :, 128:256]),
        (w2, w2p.at[0:3, :, :, 0:128]),
        (w2, w2p.at[1:4, :, :, 128:256]),
        (b2_hbm, b2),
        (wc, wcv),
        (wl, wlv),
        (bc_hbm, bc),
    ]
    copies = [
        pltpu.make_async_copy(src, dst, local_sem.at[k])
        for k, (src, dst) in enumerate(pairs)
    ]
    rims = [
        pltpu.make_async_copy(
            feat.at[:, :, 48 * d : 48 * d + 16], staged_rim.at[d], rim_sem.at[d]
        )
        for d in (0, 1)
    ]
    for copy in rims + copies[:4]:
        copy.start()

    def clear_weights(wp):
        wp[3, :, :, 0:128] = jnp.zeros((3, 384, 128), BF16)
        wp[0, :, :, 128:256] = jnp.zeros((3, 384, 128), BF16)

    def clear_ends(z):
        z[:, :, 0] = jnp.zeros((2, 4, 32, 384), BF16)
        z[:, :, 9] = jnp.zeros((2, 4, 32, 384), BF16)

    clear_weights(w1p)
    clear_ends(zin)
    field[4] = jnp.zeros((4, 2, 8, 8, 128), F32)
    for d in range(4):
        sides[0][d][8] = jnp.zeros((64, 128), BF16)
        edge_src[d, 16] = jnp.zeros((1, 8, 128), F32)

    def clear_later():
        clear_weights(w2p)
        clear_ends(zhid)
        hidden[4] = jnp.zeros((4, 2, 8, 8, 128), F32)
        coarse_field[4] = jnp.zeros((4, 4, 8, 128), F32)
        for d in range(4):
            for number, rows in ((1, 64), (2, 32)):
                sides[number][d][4 if number == 2 else 8] = jnp.zeros(
                    (rows, 128), BF16
                )
            cedge_src[d, 16] = jnp.zeros((1, 8, 128), F32)
        for side in range(2):
            for end in (0, 9):
                zx[side, end] = jnp.zeros((32, 384), BF16)
            for end in (0, 5):
                zcx[side, end] = jnp.zeros((32, 384), BF16)
        for end in (0, 5):
            zc[end] = jnp.zeros((6, 32, 384), BF16)
            zc[:, end] = jnp.zeros((6, 32, 384), BF16)

    for copy in rims:
        copy.wait()
    for copy in copies[4:6]:
        copy.start()

    def plane(source, s, x):
        if source is coarse_field:
            return source[s, x]
        return source[s, x // 2, x % 2]

    def across(source, s, y):
        if source is coarse_field:
            return source[s, :, y]
        if source is field:
            d = y // 7
            return staged_rim[d, s].astype(F32)[:, 8 * d : 8 * d + 8]
        return source[s, :, :, y].reshape(8, 8, 128)

    def column(source, s, x, y):
        if source is coarse_field:
            return source[s, x, y]
        if source is field:
            d = y // 7
            return staged_rim[d, s, x].astype(F32)[8 * d : 8 * d + 8]
        return source[s, x // 2, x % 2, y]

    def pack_side(number, source, last, d):
        ox, oy = SIDES[d]
        faces = []
        for s in range(4):
            if oy == 0:
                faces.append(plane(source, s, edge_of(ox, last)))
            else:
                faces.append(across(source, s, edge_of(oy, last)))
        if number == 2:
            even = lax.broadcasted_iota(jnp.int32, faces[0].shape, 1) % 2 == 0
            faces = [
                jnp.where(even, faces[2 * k], faces[2 * k + 1]) for k in (0, 1)
            ]
        for k, value in enumerate(faces):
            sides[number][d][k] = value.reshape(8 * (last + 1), 128).astype(BF16)

    def doubled(value, parity):
        axis = value.ndim - 2
        row = lax.broadcasted_iota(jnp.int32, value.shape, axis) % 2
        after = pltpu.roll(value, 1, axis)
        before = pltpu.roll(value, 7, axis)
        return jnp.where(
            row == parity, value, jnp.where(row == 1, after, before)
        )

    def pack_edges(source, last, edges, oy):
        for d, (ox, oy) in edges_on(oy):
            edges[d] = jnp.concatenate(
                [
                    column(source, s, edge_of(ox, last), edge_of(oy, last))
                    for s in range(4)
                ],
                axis=0,
            ).astype(BF16)

    def describe(number, edges, redges):
        described = {}
        for k in FARTHEST:
            ox, oy = ALL[k]
            if k < 4:
                count = 2 if number == 2 else 4
                src = sides[number][k].at[0:count]
                dst = sides[number][k].at[count : 2 * count]
                if number == 0 and oy == 0:
                    src = feat.at[:, edge_of(ox, 7)]
            else:
                src, dst = edges.at[k - 4], redges.at[k - 4]
            described[ox, oy] = pltpu.make_async_remote_copy(
                src_ref=src,
                dst_ref=dst,
                send_sem=send_sem.at[number, k],
                recv_sem=recv_sem.at[number, k],
                device_id=device_at(-ox, -oy),
                device_id_type=MESH,
            )
        return described

    def start(described, directions):
        for ox, oy in directions:
            when_inside(-ox, -oy, described[ox, oy].start)

    def left(described):
        for (ox, oy), copy in described.items():
            when_inside(-ox, -oy, copy.wait_send)

    def leave_y(number, described, source, last, edges, d):
        oy = 1 - 2 * d
        pack_edges(source, last, edges, oy)
        if number == 2:
            pack_side(number, source, last, 3 - d)
        start(described, [edge for _, edge in edges_on(oy)] + [(0, oy)])

    def leave_x(number, described, source, last):
        for d in (0, 1):
            pack_side(number, source, last, d)
        start(described, SIDES[:2])

    def arrive(described, directions):
        for ox, oy in directions:
            when_inside(ox, oy, described[ox, oy].wait_recv)

    sent = describe(0, send_edge.at[0], recv_edge.at[0])
    for oy in (-1, 1):
        pack_edges(field, 7, send_edge.at[0], oy)
    for d in (2, 3):
        pack_side(0, field, 7, d)
    pl.semaphore_wait(barrier, partners)
    start(sent, EDGES + SIDES[2:] + SIDES[:2])
    copies[0].wait()
    for s in range(4):
        for x in range(8):
            field[s, x // 2, x % 2] = staged[s, x].astype(F32).reshape(8, 8, 128)
        for d in (0, 1):
            sides[0][d][s] = staged[s, edge_of(SIDES[d][0], 7)]

    for k in (1, 2, 3):
        copies[k].wait()
    live = [jnp.where(cell[s] >= 0, 1.0, 0.0).astype(F32) for s in range(4)]

    def index(s, ox, oy, oz):
        if (ox, oy, oz) == (0, 0, 0):
            return s
        entry = nbr[s, NUMBER[ox, oy, oz]]
        safe = jnp.maximum(entry, 0)
        block = lax.shift_right_logical(safe, 2)
        slot = lax.bitwise_and(safe, 3)
        if (ox, oy) == (0, 0):
            return jnp.where(entry < 0, 4, slot)
        if ox == 0 or oy == 0:
            place = slot + jnp.where(block == 4, 0, 4)
            return jnp.where(entry < 0, 8, place)
        beside_x = (ox + 1) * 3 + 1
        beside_y = 3 + (oy + 1)
        place = slot + jnp.where(
            block == 4,
            0,
            jnp.where(block == beside_x, 4, jnp.where(block == beside_y, 8, 12)),
        )
        return jnp.where(entry < 0, 16, place)

    where = {
        (s, 0, 0, oz): index(s, 0, 0, oz) for s in range(4) for oz in (-1, 0, 1)
    }

    def index_rims():
        for s in range(4):
            for ox, oy in ALL:
                for oz in (-1, 0, 1):
                    where[s, ox, oy, oz] = index(s, ox, oy, oz)

    def shifted(low, own, high, step):
        row = lax.broadcasted_iota(jnp.int32, own.shape, own.ndim - 2)
        axis = own.ndim - 2
        down = pltpu.roll(jnp.where(row >= 8 - step, low, own), step, axis)
        up = pltpu.roll(jnp.where(row < step, high, own), 8 - step, axis)
        return down, own, up

    def pair(fetch, ox, oy, step):
        for half in (0, 1):
            parts = [
                shifted(*[fetch(where[s, ox, oy, oz]) for oz in (-1, 0, 1)], step)
                for s in (2 * half, 2 * half + 1)
            ]
            for kz in range(3):
                both = jnp.concatenate([parts[0][kz], parts[1][kz]], axis=-2)
                yield slice(16 * half, 16 * half + 16), slice(
                    128 * kz, 128 * kz + 128
                ), both.astype(BF16)

    def fine_centre(source, z):
        for m in range(4):
            for h in (0, 1):
                for rows, lanes, value in pair(lambda q: source[q, m, h], 0, 0, 1):
                    z[h, m, 1:9, rows, lanes] = value

    def face(number, d):
        def fetch(q):
            if number == 2:
                value = sides[2][d][lax.shift_right_logical(q, 1)].astype(F32)
                return doubled(value.reshape(4, 8, 128), lax.bitwise_and(q, 1))
            return sides[number][d][q].astype(F32).reshape(8, 8, 128)

        return fetch

    def own_edges(source, last, edges):
        for d, (ox, oy) in enumerate(EDGES):
            for s in range(4):
                edges[d, s, 0] = column(
                    source, s, edge_of(ox, last), edge_of(oy, last)
                )

    def end_of(number, d, s, step):
        ref = sides[number][d]
        at = 2 + s // 2 if number == 2 else 4 + s
        if step < 0:
            rows = ref.shape[1]
            value = ref[at, rows - 16 : rows].astype(F32)[8:16]
        else:
            value = ref[at, 0:16].astype(F32)[0:8]
        return doubled(value, s % 2) if number == 2 else value

    def edges_beside_x(number, edges):
        for k, (ox, oy) in enumerate(EDGES):
            for s in range(4):
                edges[k, 4 + s, 0] = end_of(number, SIDES.index((ox, 0)), s, oy)

    def edges_beside_y(number, edges, redges, d):
        for k, (ox, oy) in edges_on(2 * d - 1):
            far = redges[k].astype(F32)
            for s in range(4):
                edges[k, 8 + s, 0] = end_of(number, d + 2, s, ox)
                edges[k, 12 + s, 0] = far[8 * s : 8 * s + 8]

    def y_rim(number, step, last, edges, rim, d):
        for rows, lanes, value in pair(face(number, d + 2), *SIDES[d + 2], step):
            rim[d, 1 : last + 2, rows, lanes] = value
        for k, (ox, oy) in edges_on(2 * d - 1):
            x = 0 if ox < 0 else last + 2
            for rows, lanes, value in pair(lambda q: edges[k, q], ox, oy, step):
                rim[d, x, rows, lanes] = value[0]

    def arrive_y(described, d):
        arrive(described, [edge for _, edge in edges_on(2 * d - 1)] + [SIDES[d + 2]])

    def by_turns(step):
        far_low = lax.rem(my, 4) == 0

        @pl.when(far_low)
        def _():
            step(1)

        step(0)

        @pl.when(jnp.logical_not(far_low))
        def _():
            step(1)

    def x_rim(number, step, last, rim):
        for d in (0, 1):
            for rows, lanes, value in pair(face(number, d), *SIDES[d], step):
                rim[d, 1 : last + 2, rows, lanes] = value

    def centre_conv(z, wp, i):
        planes = [(1, i - 1), (0, i), (1, i), (0, i + 1)]
        used = [p for p in range(4) if 0 <= planes[p][1] < 4]
        lhs = jnp.concatenate(
            [
                z[planes[p][0], planes[p][1], ky : ky + 8].reshape(256, 384)
                for ky in range(3)
                for p in used
            ],
            axis=1,
        )
        rhs = jnp.concatenate([wp[p, ky] for ky in range(3) for p in used], axis=0)
        return jnp.dot(lhs, rhs, preferred_element_type=F32)

    def convolve(z, wp, finish):
        for i in range(4):
            acc = centre_conv(z, wp, i)
            for h in (0, 1):
                part = acc[:, 128 * h : 128 * h + 128].reshape(8, 32, 128)
                total[i, h] = part
                if 0 < 2 * i + h < 7:
                    inner = part[1:7].reshape(6, 4, 8, 128)
                    for s in range(4):
                        finish(s, (i, h, slice(1, 7)), inner[:, s])

    def add_x(number, described, wp, finish):
        arrive(described, SIDES[:2])
        x_rim(number, 1, 7, zx)
        edges_beside_x(number, edge_src)
        for d in (0, 1):
            i, h, p = (0, 0, 0) if d == 0 else (3, 1, 3)
            lhs = jnp.concatenate(
                [zx[d, ky : ky + 8].reshape(256, 384) for ky in range(3)], axis=1
            )
            rhs = jnp.concatenate(
                [wp[p, ky][:, 128 * h : 128 * h + 128] for ky in range(3)], axis=0
            )
            add = jnp.dot(lhs, rhs, preferred_element_type=F32).reshape(8, 32, 128)
            part = total[i, h] + add
            for y in (0, 7):
                total[i, h, y] = part[y]
            inner = part[1:7].reshape(6, 4, 8, 128)
            for s in range(4):
                finish(s, (i, h, slice(1, 7)), inner[:, s])

    def add_y(number, described, wp, finish, after):
        def step(d):
            arrive_y(described, d)
            edges_beside_y(number, edge_src, recv_edge.at[number], d)
            y_rim(number, 1, 7, edge_src, zy, d)
            y, ky = (0, 0) if d == 0 else (7, 2)
            lhs = jnp.concatenate(
                [zy[d, kx : kx + 8].reshape(256, 384) for kx in range(3)], axis=1
            )
            rhs = jnp.concatenate([wp[kx, ky][:, 0:128] for kx in range(3)], axis=0)
            add = jnp.dot(lhs, rhs, preferred_element_type=F32)
            part = total[:, :, y] + add.reshape(4, 2, 32, 128)
            part = part.reshape(4, 2, 4, 8, 128)
            for s in range(4):
                finish(s, (slice(0, 4), slice(0, 2), y), part[:, :, s])
            after(d)

        by_turns(step)

    copies[4].wait()
    copies[5].wait()
    for copy in copies[6:]:
        copy.start()
    fine_centre(field, zin)
    own_edges(field, 7, edge_src)
    index_rims()
    clear_later()

    def to_hidden(s, at, value):
        value = jnp.maximum(value + b1[...].reshape(1, 1, 128), 0.0) * live[s]
        value = value.astype(BF16)
        if at[2] == 0 or at[2] == 7:
            sides[1][3 if at[2] == 0 else 2][s] = value.reshape(64, 128)
        hidden[(s,) + at] = value.astype(F32)

    convolve(zin, w1p, to_hidden)
    add_x(0, sent, w1p, to_hidden)
    sent_hidden = describe(1, send_edge.at[1], recv_edge.at[1])
    add_y(
        0,
        sent,
        w1p,
        to_hidden,
        lambda d: leave_y(1, sent_hidden, hidden, 7, send_edge.at[1], d),
    )
    leave_x(1, sent_hidden, hidden, 7)
    for k in (6, 7, 8):
        copies[k].wait()
    own_edges(hidden, 7, edge_src)
    fine_centre(hidden, zhid)

    def to_fine(s, at, value):
        value = value + b2[...].reshape(1, 1, 128) + field[(s,) + at]
        out[(s,) + at] = value * live[s]

    def pooled(value):
        even = lax.broadcasted_iota(jnp.int32, value.shape, 1) % 2 == 0
        other = jnp.where(even, pltpu.roll(value, 7, 1), pltpu.roll(value, 1, 1))
        return ((value + other) * 0.125).astype(BF16).astype(F32)

    def pool(ys):
        for s in range(4):
            for y in ys:
                value = out[s, :, 0, 2 * y] + out[s, :, 1, 2 * y]
                value = value + out[s, :, 0, 2 * y + 1] + out[s, :, 1, 2 * y + 1]
                coarse_field[s, :, y] = pooled(value)

    convolve(zhid, w2p, to_fine)
    add_x(1, sent_hidden, w2p, to_fine)
    pool((1, 2))
    sent_coarse = describe(2, csend_edge, crecv_edge)

    def to_coarse(d):
        pool((3 * d,))
        leave_y(2, sent_coarse, coarse_field, 3, csend_edge, d)

    add_y(1, sent_hidden, w2p, to_fine, to_coarse)
    leave_x(2, sent_coarse, coarse_field, 3)

    own_edges(coarse_field, 3, cedge_src)
    for x in range(4):
        for rows, lanes, value in pair(lambda q: coarse_field[q, x], 0, 0, 2):
            zc[x + 1, 1:5, rows, lanes] = value
    for k in (9, 10, 11):
        copies[k].wait()
    lhs = jnp.concatenate(
        [
            zc[kx : kx + 4, ky : ky + 4].reshape(512, 384)
            for kx in range(3)
            for ky in range(3)
        ],
        axis=1,
    )
    acc = jnp.dot(lhs, wcv[...], preferred_element_type=F32)
    ctotal[...] = acc.reshape(4, 4, 32, 256)

    def join(ys):
        acc = jnp.concatenate([ctotal[:, y] for y in ys], axis=0)
        acc = jnp.maximum(acc.reshape(-1, 256) + bc[...], 0.0)
        acc = acc.reshape(4 * len(ys), 4, 8, 256)
        acc = jnp.concatenate(
            [(acc[:, s] * live[s])[:, None] for s in range(4)], axis=1
        )
        lifted = jnp.dot(
            acc.reshape(-1, 256).astype(BF16), wlv[...], preferred_element_type=F32
        ).reshape(len(ys), 4, 4, 8, 128)
        for k, y in enumerate(ys):
            for s in range(4):
                raised = lifted[k, :, s]
                for h in (0, 1):
                    for f in (0, 1):
                        at = (s, slice(0, 4), h, 2 * y + f)
                        out[at] = (out[at] + raised) * live[s]

    left(sent)
    left(sent_hidden)

    arrive(sent_coarse, SIDES[:2])
    x_rim(2, 2, 3, zcx)
    edges_beside_x(2, cedge_src)
    for d in (0, 1):
        lhs = jnp.concatenate(
            [zcx[d, ky : ky + 4].reshape(128, 384) for ky in range(3)], axis=1
        )
        rhs = wcv[2304 * d : 2304 * d + 1152]
        add = jnp.dot(lhs, rhs, preferred_element_type=F32)
        ctotal[3 * d] = ctotal[3 * d] + add.reshape(4, 32, 256)
    join((1, 2))
    left(sent_coarse)

    def coarse_y(d):
        arrive_y(sent_coarse, d)
        edges_beside_y(2, cedge_src, crecv_edge, d)
        y_rim(2, 2, 3, cedge_src, zcy, d)
        lhs = jnp.concatenate(
            [zcy[d, kx : kx + 4].reshape(128, 384) for kx in range(3)], axis=1
        )
        rhs = jnp.concatenate(
            [
                wcv[1152 * kx + 768 * d : 1152 * kx + 768 * d + 384]
                for kx in range(3)
            ],
            axis=0,
        )
        add = jnp.dot(lhs, rhs, preferred_element_type=F32)
        ctotal[:, 3 * d] = ctotal[:, 3 * d] + add.reshape(4, 32, 256)
        join((3 * d,))

    by_turns(coarse_y)


def local(gx, gy, features, slot_cell, neighbours, w1, b1, w2, b2, wc, bc, wl):
    operands = [
        pltpu.with_memory_space_constraint(operand, pltpu.HBM)
        for operand in (
            slot_cell.reshape(4),
            neighbours.reshape(4, 26),
            features.reshape(4, 8, 64, 128),
            w1.reshape(3, 3, 384, 128),
            b1.reshape(1, 128),
            w2.reshape(3, 3, 384, 128),
            b2.reshape(1, 128),
            wc.reshape(3456, 256),
            bc.reshape(1, 256),
            wl,
        )
    ]
    result = pl.pallas_call(
        functools.partial(kernel, gx, gy),
        out_shape=jax.ShapeDtypeStruct((4, 4, 2, 8, 8, 128), F32),
        in_specs=[pl.BlockSpec(memory_space=pl.ANY)] * 10,
        out_specs=pl.BlockSpec(memory_space=pltpu.VMEM),
        scratch_shapes=[
            pltpu.SMEM((4,), jnp.int32),
            pltpu.SMEM((4, 26), jnp.int32),
            pltpu.VMEM((1, 128), F32),
            pltpu.VMEM((1, 128), F32),
            pltpu.VMEM((1, 256), F32),
            pltpu.VMEM((4, 8, 64, 128), BF16),
            pltpu.VMEM((2, 4, 8, 16, 128), BF16),
            pltpu.VMEM((5, 4, 2, 8, 8, 128), F32),
            pltpu.VMEM((5, 4, 2, 8, 8, 128), F32),
            pltpu.VMEM((5, 4, 4, 8, 128), F32),
            pltpu.VMEM((4, 17, 1, 8, 128), F32),
            pltpu.VMEM((4, 17, 1, 8, 128), F32),
            pltpu.VMEM((2, 4, 10, 32, 384), BF16),
            pltpu.VMEM((2, 4, 10, 32, 384), BF16),
            pltpu.VMEM((2, 10, 32, 384), BF16),
            pltpu.VMEM((2, 10, 32, 384), BF16),
            pltpu.VMEM((6, 6, 32, 384), BF16),
            pltpu.VMEM((2, 6, 32, 384), BF16),
            pltpu.VMEM((2, 6, 32, 384), BF16),
            pltpu.VMEM((4, 3, 384, 256), BF16),
            pltpu.VMEM((4, 3, 384, 256), BF16),
            pltpu.VMEM((3456, 256), BF16),
            pltpu.VMEM((256, 128), BF16),
            pltpu.VMEM((4, 2, 8, 32, 128), F32),
            pltpu.VMEM((4, 4, 32, 256), F32),
            pltpu.VMEM((2, 4, 32, 128), BF16),
            pltpu.VMEM((2, 4, 32, 128), BF16),
            pltpu.VMEM((4, 32, 128), BF16),
            pltpu.VMEM((4, 32, 128), BF16),
            pltpu.SemaphoreType.DMA((12,)),
            pltpu.SemaphoreType.DMA((2,)),
            pltpu.SemaphoreType.DMA((3, 8)),
            pltpu.SemaphoreType.DMA((3, 8)),
        ]
        + [pltpu.VMEM((9, 64, 128), BF16)] * 8
        + [pltpu.VMEM((5, 32, 128), BF16)] * 4,
        compiler_params=pltpu.CompilerParams(
            collective_id=0, has_side_effects=True, vmem_limit_bytes=48 * 2**20
        ),
        cost_estimate=pl.CostEstimate(
            flops=8_000_000_000, bytes_accessed=8_000_000, transcendentals=0
        ),
        name="unet_window",
    )(*operands)
    return result.reshape(1, 1, 4, 512, 128)


def solution(mesh):
    placed = (
        P("gx", "gy", None, None, None),
        P("gx", "gy", None),
        P("gx", "gy", None, None),
    ) + (P(),) * 7
    return jax.shard_map(
        functools.partial(local, mesh.shape["gx"], mesh.shape["gy"]),
        mesh=mesh,
        in_specs=placed,
        out_specs=P("gx", "gy", None, None, None),
        check_vma=False,
    )
```

```python
import functools

import jax
import jax.numpy as jnp
from jax import lax
from jax.experimental import pallas as pl
from jax.experimental.pallas import tpu as pltpu
from jax.sharding import PartitionSpec as P

MESH = pl.DeviceIdType.MESH
F32 = jnp.float32
BF16 = jnp.bfloat16

OFFSETS = [
    (ox, oy, oz)
    for ox in (-1, 0, 1)
    for oy in (-1, 0, 1)
    for oz in (-1, 0, 1)
    if (ox, oy, oz) != (0, 0, 0)
]
NUMBER = {offset: k for k, offset in enumerate(OFFSETS)}
SIDES = [(-1, 0), (1, 0), (0, -1), (0, 1)]
EDGES = [(-1, -1), (-1, 1), (1, -1), (1, 1)]
ALL = SIDES + EDGES
FARTHEST = (4, 5, 6, 7, 2, 3, 0, 1)


def edges_on(oy):
    return [(k, edge) for k, edge in enumerate(EDGES) if edge[1] == oy]


def edge_of(step, last):
    return last if step < 0 else 0


def kernel(
    gx,
    gy,
    cell_hbm,
    nbr_hbm,
    feat,
    w1,
    b1_hbm,
    w2,
    b2_hbm,
    wc,
    bc_hbm,
    wl,
    out,
    cell,
    nbr,
    b1,
    b2,
    bc,
    staged,
    staged_rim,
    field,
    hidden,
    coarse_field,
    edge_src,
    cedge_src,
    zin,
    zhid,
    zx,
    zy,
    zc,
    zcx,
    zcy,
    w1p,
    w2p,
    wcv,
    wlv,
    total,
    ctotal,
    send_edge,
    recv_edge,
    csend_edge,
    crecv_edge,
    local_sem,
    rim_sem,
    send_sem,
    recv_sem,
    *side_refs,
):
    sides = [side_refs[4 * number : 4 * number + 4] for number in range(3)]
    mx = lax.axis_index("gx")
    my = lax.axis_index("gy")

    def device_at(ox, oy):
        return (lax.rem(mx + ox + gx, gx), lax.rem(my + oy + gy, gy))

    def inside(ox, oy):
        found = None
        for at, step, size in ((mx, ox, gx), (my, oy, gy)):
            if step != 0:
                here = at > 0 if step < 0 else at < size - 1
                found = here if found is None else jnp.logical_and(found, here)
        return found

    def when_inside(ox, oy, act):
        @pl.when(inside(ox, oy))
        def _():
            act()

    def signal_to(ox, oy):
        pl.semaphore_signal(
            barrier, inc=1, device_id=device_at(ox, oy), device_id_type=MESH
        )

    barrier = pltpu.get_barrier_semaphore()
    for k in FARTHEST:
        when_inside(*ALL[k], functools.partial(signal_to, *ALL[k]))
    beside_x = jnp.where(mx > 0, 1, 0) + jnp.where(mx < gx - 1, 1, 0)
    beside_y = jnp.where(my > 0, 1, 0) + jnp.where(my < gy - 1, 1, 0)
    partners = (1 + beside_x) * (1 + beside_y) - 1

    pairs = [
        (feat, staged),
        (cell_hbm, cell),
        (nbr_hbm, nbr),
        (b1_hbm, b1),
        (w1, w1p.at[0:3, :, :, 0:128]),
        (w1, w1p.at[1:4, :, :, 128:256]),
        (w2, w2p.at[0:3, :, :, 0:128]),
        (w2, w2p.at[1:4, :, :, 128:256]),
        (b2_hbm, b2),
        (wc, wcv),
        (wl, wlv),
        (bc_hbm, bc),
    ]
    copies = [
        pltpu.make_async_copy(src, dst, local_sem.at[k])
        for k, (src, dst) in enumerate(pairs)
    ]
    rims = [
        pltpu.make_async_copy(
            feat.at[:, :, 48 * d : 48 * d + 16], staged_rim.at[d], rim_sem.at[d]
        )
        for d in (0, 1)
    ]
    for copy in rims + copies[:4]:
        copy.start()

    def clear_weights(wp):
        wp[3, :, :, 0:128] = jnp.zeros((3, 384, 128), BF16)
        wp[0, :, :, 128:256] = jnp.zeros((3, 384, 128), BF16)

    def clear_ends(z):
        z[:, :, 0] = jnp.zeros((2, 4, 32, 384), BF16)
        z[:, :, 9] = jnp.zeros((2, 4, 32, 384), BF16)

    clear_weights(w1p)
    clear_ends(zin)
    field[4] = jnp.zeros((4, 2, 8, 8, 128), F32)
    for d in range(4):
        sides[0][d][8] = jnp.zeros((64, 128), BF16)
        edge_src[d, 16] = jnp.zeros((1, 8, 128), F32)

    def clear_later():
        clear_weights(w2p)
        clear_ends(zhid)
        hidden[4] = jnp.zeros((4, 2, 8, 8, 128), F32)
        coarse_field[4] = jnp.zeros((4, 4, 8, 128), F32)
        for d in range(4):
            for number, rows in ((1, 64), (2, 32)):
                sides[number][d][4 if number == 2 else 8] = jnp.zeros(
                    (rows, 128), BF16
                )
            cedge_src[d, 16] = jnp.zeros((1, 8, 128), F32)
        for side in range(2):
            for end in (0, 9):
                zx[side, end] = jnp.zeros((32, 384), BF16)
            for end in (0, 5):
                zcx[side, end] = jnp.zeros((32, 384), BF16)
        for end in (0, 5):
            zc[end] = jnp.zeros((6, 32, 384), BF16)
            zc[:, end] = jnp.zeros((6, 32, 384), BF16)

    for copy in rims:
        copy.wait()
    for copy in copies[4:6]:
        copy.start()

    def plane(source, s, x):
        if source is coarse_field:
            return source[s, x]
        return source[s, x // 2, x % 2]

    def across(source, s, y):
        if source is coarse_field:
            return source[s, :, y]
        if source is field:
            d = y // 7
            return staged_rim[d, s].astype(F32)[:, 8 * d : 8 * d + 8]
        return source[s, :, :, y].reshape(8, 8, 128)

    def column(source, s, x, y):
        if source is coarse_field:
            return source[s, x, y]
        if source is field:
            d = y // 7
            return staged_rim[d, s, x].astype(F32)[8 * d : 8 * d + 8]
        return source[s, x // 2, x % 2, y]

    def pack_side(number, source, last, d):
        ox, oy = SIDES[d]
        faces = []
        for s in range(4):
            if oy == 0:
                faces.append(plane(source, s, edge_of(ox, last)))
            else:
                faces.append(across(source, s, edge_of(oy, last)))
        if number == 2:
            even = lax.broadcasted_iota(jnp.int32, faces[0].shape, 1) % 2 == 0
            faces = [
                jnp.where(even, faces[2 * k], faces[2 * k + 1]) for k in (0, 1)
            ]
        for k, value in enumerate(faces):
            sides[number][d][k] = value.reshape(8 * (last + 1), 128).astype(BF16)

    def doubled(value, parity):
        axis = value.ndim - 2
        row = lax.broadcasted_iota(jnp.int32, value.shape, axis) % 2
        after = pltpu.roll(value, 1, axis)
        before = pltpu.roll(value, 7, axis)
        return jnp.where(
            row == parity, value, jnp.where(row == 1, after, before)
        )

    def pack_edges(source, last, edges, oy):
        for d, (ox, oy) in edges_on(oy):
            edges[d] = jnp.concatenate(
                [
                    column(source, s, edge_of(ox, last), edge_of(oy, last))
                    for s in range(4)
                ],
                axis=0,
            ).astype(BF16)

    def describe(number, edges, redges):
        described = {}
        for k in FARTHEST:
            ox, oy = ALL[k]
            if k < 4:
                count = 2 if number == 2 else 4
                src = sides[number][k].at[0:count]
                dst = sides[number][k].at[count : 2 * count]
                if number == 0 and oy == 0:
                    src = feat.at[:, edge_of(ox, 7)]
            else:
                src, dst = edges.at[k - 4], redges.at[k - 4]
            described[ox, oy] = pltpu.make_async_remote_copy(
                src_ref=src,
                dst_ref=dst,
                send_sem=send_sem.at[number, k],
                recv_sem=recv_sem.at[number, k],
                device_id=device_at(-ox, -oy),
                device_id_type=MESH,
            )
        return described

    def start(described, directions):
        for ox, oy in directions:
            when_inside(-ox, -oy, described[ox, oy].start)

    def left(described):
        for (ox, oy), copy in described.items():
            when_inside(-ox, -oy, copy.wait_send)

    def leave_y(number, described, source, last, edges, d):
        oy = 1 - 2 * d
        pack_edges(source, last, edges, oy)
        pack_side(number, source, last, 3 - d)
        start(described, [edge for _, edge in edges_on(oy)] + [(0, oy)])

    def leave_x(number, described, source, last):
        for d in (0, 1):
            pack_side(number, source, last, d)
        start(described, SIDES[:2])

    def arrive(described, directions):
        for ox, oy in directions:
            when_inside(ox, oy, described[ox, oy].wait_recv)

    sent = describe(0, send_edge.at[0], recv_edge.at[0])
    for oy in (-1, 1):
        pack_edges(field, 7, send_edge.at[0], oy)
    for d in (2, 3):
        pack_side(0, field, 7, d)
    pl.semaphore_wait(barrier, partners)
    start(sent, EDGES + SIDES[2:] + SIDES[:2])
    copies[0].wait()
    for s in range(4):
        for x in range(8):
            field[s, x // 2, x % 2] = staged[s, x].astype(F32).reshape(8, 8, 128)
        for d in (0, 1):
            sides[0][d][s] = staged[s, edge_of(SIDES[d][0], 7)]

    for k in (1, 2, 3):
        copies[k].wait()
    live = [jnp.where(cell[s] >= 0, 1.0, 0.0).astype(F32) for s in range(4)]

    def index(s, ox, oy, oz):
        if (ox, oy, oz) == (0, 0, 0):
            return s
        entry = nbr[s, NUMBER[ox, oy, oz]]
        safe = jnp.maximum(entry, 0)
        block = lax.shift_right_logical(safe, 2)
        slot = lax.bitwise_and(safe, 3)
        if (ox, oy) == (0, 0):
            return jnp.where(entry < 0, 4, slot)
        if ox == 0 or oy == 0:
            place = slot + jnp.where(block == 4, 0, 4)
            return jnp.where(entry < 0, 8, place)
        beside_x = (ox + 1) * 3 + 1
        beside_y = 3 + (oy + 1)
        place = slot + jnp.where(
            block == 4,
            0,
            jnp.where(block == beside_x, 4, jnp.where(block == beside_y, 8, 12)),
        )
        return jnp.where(entry < 0, 16, place)

    where = {
        (s, 0, 0, oz): index(s, 0, 0, oz) for s in range(4) for oz in (-1, 0, 1)
    }

    def index_rims():
        for s in range(4):
            for ox, oy in ALL:
                for oz in (-1, 0, 1):
                    where[s, ox, oy, oz] = index(s, ox, oy, oz)

    def shifted(low, own, high, step):
        row = lax.broadcasted_iota(jnp.int32, own.shape, own.ndim - 2)
        axis = own.ndim - 2
        down = pltpu.roll(jnp.where(row >= 8 - step, low, own), step, axis)
        up = pltpu.roll(jnp.where(row < step, high, own), 8 - step, axis)
        return down, own, up

    def pair(fetch, ox, oy, step):
        for half in (0, 1):
            parts = [
                shifted(*[fetch(where[s, ox, oy, oz]) for oz in (-1, 0, 1)], step)
                for s in (2 * half, 2 * half + 1)
            ]
            for kz in range(3):
                both = jnp.concatenate([parts[0][kz], parts[1][kz]], axis=-2)
                yield slice(16 * half, 16 * half + 16), slice(
                    128 * kz, 128 * kz + 128
                ), both.astype(BF16)

    def fine_centre(source, z):
        for m in range(4):
            for h in (0, 1):
                for rows, lanes, value in pair(lambda q: source[q, m, h], 0, 0, 1):
                    z[h, m, 1:9, rows, lanes] = value

    def face(number, d):
        def fetch(q):
            if number == 2:
                value = sides[2][d][lax.shift_right_logical(q, 1)].astype(F32)
                return doubled(value.reshape(4, 8, 128), lax.bitwise_and(q, 1))
            return sides[number][d][q].astype(F32).reshape(8, 8, 128)

        return fetch

    def own_edges(source, last, edges):
        for d, (ox, oy) in enumerate(EDGES):
            for s in range(4):
                edges[d, s, 0] = column(
                    source, s, edge_of(ox, last), edge_of(oy, last)
                )

    def end_of(number, d, s, step):
        ref = sides[number][d]
        at = 2 + s // 2 if number == 2 else 4 + s
        if step < 0:
            rows = ref.shape[1]
            value = ref[at, rows - 16 : rows].astype(F32)[8:16]
        else:
            value = ref[at, 0:16].astype(F32)[0:8]
        return doubled(value, s % 2) if number == 2 else value

    def edges_beside_x(number, edges):
        for k, (ox, oy) in enumerate(EDGES):
            for s in range(4):
                edges[k, 4 + s, 0] = end_of(number, SIDES.index((ox, 0)), s, oy)

    def edges_beside_y(number, edges, d):
        for k, (ox, oy) in edges_on(2 * d - 1):
            for s in range(4):
                edges[k, 8 + s, 0] = end_of(number, d + 2, s, ox)

    def y_rim(number, step, last, edges, rim, d):
        for rows, lanes, value in pair(face(number, d + 2), *SIDES[d + 2], step):
            rim[d, 1 : last + 2, rows, lanes] = value
        for k, (ox, oy) in edges_on(2 * d - 1):
            x = 0 if ox < 0 else last + 2
            for rows, lanes, value in pair(lambda q: edges[k, q], ox, oy, step):
                rim[d, x, rows, lanes] = value[0]

    def arrive_y(described, d, edges, redges):
        arrive(described, [edge for _, edge in edges_on(2 * d - 1)])
        for k, _ in edges_on(2 * d - 1):
            far = redges[k].astype(F32)
            for s in range(4):
                edges[k, 12 + s, 0] = far[8 * s : 8 * s + 8]
        arrive(described, [SIDES[d + 2]])

    def by_turns(step):
        far_low = lax.rem(my, 4) == 0

        @pl.when(far_low)
        def _():
            step(1)

        step(0)

        @pl.when(jnp.logical_not(far_low))
        def _():
            step(1)

    def x_rim(number, step, last, rim):
        for d in (0, 1):
            for rows, lanes, value in pair(face(number, d), *SIDES[d], step):
                rim[d, 1 : last + 2, rows, lanes] = value

    def centre_conv(z, wp, i):
        planes = [(1, i - 1), (0, i), (1, i), (0, i + 1)]
        used = [p for p in range(4) if 0 <= planes[p][1] < 4]
        lhs = jnp.concatenate(
            [
                z[planes[p][0], planes[p][1], ky : ky + 8].reshape(256, 384)
                for ky in range(3)
                for p in used
            ],
            axis=1,
        )
        rhs = jnp.concatenate([wp[p, ky] for ky in range(3) for p in used], axis=0)
        return jnp.dot(lhs, rhs, preferred_element_type=F32)

    def convolve(z, wp, finish):
        for i in range(4):
            acc = centre_conv(z, wp, i)
            for h in (0, 1):
                part = acc[:, 128 * h : 128 * h + 128].reshape(8, 32, 128)
                total[i, h] = part
                if 0 < 2 * i + h < 7:
                    inner = part[1:7].reshape(6, 4, 8, 128)
                    for s in range(4):
                        finish(s, (i, h, slice(1, 7)), inner[:, s])

    def add_x(number, described, wp, finish):
        arrive(described, SIDES[:2])
        x_rim(number, 1, 7, zx)
        edges_beside_x(number, edge_src)
        for d in (0, 1):
            i, h, p = (0, 0, 0) if d == 0 else (3, 1, 3)
            lhs = jnp.concatenate(
                [zx[d, ky : ky + 8].reshape(256, 384) for ky in range(3)], axis=1
            )
            rhs = jnp.concatenate(
                [wp[p, ky][:, 128 * h : 128 * h + 128] for ky in range(3)], axis=0
            )
            add = jnp.dot(lhs, rhs, preferred_element_type=F32).reshape(8, 32, 128)
            part = total[i, h] + add
            for y in (0, 7):
                total[i, h, y] = part[y]
            inner = part[1:7].reshape(6, 4, 8, 128)
            for s in range(4):
                finish(s, (i, h, slice(1, 7)), inner[:, s])

    def add_y(number, described, wp, finish, after):
        def step(d):
            arrive_y(described, d, edge_src, recv_edge.at[number])
            edges_beside_y(number, edge_src, d)
            y_rim(number, 1, 7, edge_src, zy, d)
            y, ky = (0, 0) if d == 0 else (7, 2)
            lhs = jnp.concatenate(
                [zy[d, kx : kx + 8].reshape(256, 384) for kx in range(3)], axis=1
            )
            rhs = jnp.concatenate([wp[kx, ky][:, 0:128] for kx in range(3)], axis=0)
            add = jnp.dot(lhs, rhs, preferred_element_type=F32)
            part = total[:, :, y] + add.reshape(4, 2, 32, 128)
            part = part.reshape(4, 2, 4, 8, 128)
            for s in range(4):
                finish(s, (slice(0, 4), slice(0, 2), y), part[:, :, s])
            after(d)

        by_turns(step)

    copies[4].wait()
    copies[5].wait()
    for copy in copies[6:]:
        copy.start()
    fine_centre(field, zin)
    own_edges(field, 7, edge_src)
    index_rims()
    clear_later()

    def to_hidden(s, at, value):
        value = jnp.maximum(value + b1[...].reshape(1, 1, 128), 0.0) * live[s]
        hidden[(s,) + at] = value.astype(BF16).astype(F32)

    convolve(zin, w1p, to_hidden)
    add_x(0, sent, w1p, to_hidden)
    sent_hidden = describe(1, send_edge.at[1], recv_edge.at[1])
    add_y(
        0,
        sent,
        w1p,
        to_hidden,
        lambda d: leave_y(1, sent_hidden, hidden, 7, send_edge.at[1], d),
    )
    leave_x(1, sent_hidden, hidden, 7)
    for k in (6, 7, 8):
        copies[k].wait()
    own_edges(hidden, 7, edge_src)
    fine_centre(hidden, zhid)

    def to_fine(s, at, value):
        value = value + b2[...].reshape(1, 1, 128) + field[(s,) + at]
        out[(s,) + at] = value * live[s]

    def pooled(value):
        even = lax.broadcasted_iota(jnp.int32, value.shape, 1) % 2 == 0
        other = jnp.where(even, pltpu.roll(value, 7, 1), pltpu.roll(value, 1, 1))
        return ((value + other) * 0.125).astype(BF16).astype(F32)

    def pool(ys):
        for s in range(4):
            for y in ys:
                value = out[s, :, 0, 2 * y] + out[s, :, 1, 2 * y]
                value = value + out[s, :, 0, 2 * y + 1] + out[s, :, 1, 2 * y + 1]
                coarse_field[s, :, y] = pooled(value)

    convolve(zhid, w2p, to_fine)
    add_x(1, sent_hidden, w2p, to_fine)
    pool((1, 2))
    sent_coarse = describe(2, csend_edge, crecv_edge)

    def to_coarse(d):
        pool((3 * d,))
        leave_y(2, sent_coarse, coarse_field, 3, csend_edge, d)

    add_y(1, sent_hidden, w2p, to_fine, to_coarse)
    leave_x(2, sent_coarse, coarse_field, 3)

    own_edges(coarse_field, 3, cedge_src)
    for x in range(4):
        for rows, lanes, value in pair(lambda q: coarse_field[q, x], 0, 0, 2):
            zc[x + 1, 1:5, rows, lanes] = value
    for k in (9, 10, 11):
        copies[k].wait()
    lhs = jnp.concatenate(
        [
            zc[kx : kx + 4, ky : ky + 4].reshape(512, 384)
            for kx in range(3)
            for ky in range(3)
        ],
        axis=1,
    )
    acc = jnp.dot(lhs, wcv[...], preferred_element_type=F32)
    ctotal[...] = acc.reshape(4, 4, 32, 256)

    def join(ys):
        acc = jnp.concatenate([ctotal[:, y] for y in ys], axis=0)
        acc = jnp.maximum(acc.reshape(-1, 256) + bc[...], 0.0)
        acc = acc.reshape(4 * len(ys), 4, 8, 256)
        acc = jnp.concatenate(
            [(acc[:, s] * live[s])[:, None] for s in range(4)], axis=1
        )
        lifted = jnp.dot(
            acc.reshape(-1, 256).astype(BF16), wlv[...], preferred_element_type=F32
        ).reshape(len(ys), 4, 4, 8, 128)
        for k, y in enumerate(ys):
            for s in range(4):
                raised = lifted[k, :, s]
                for h in (0, 1):
                    for f in (0, 1):
                        at = (s, slice(0, 4), h, 2 * y + f)
                        out[at] = (out[at] + raised) * live[s]

    left(sent)
    left(sent_hidden)

    arrive(sent_coarse, SIDES[:2])
    x_rim(2, 2, 3, zcx)
    edges_beside_x(2, cedge_src)
    for d in (0, 1):
        lhs = jnp.concatenate(
            [zcx[d, ky : ky + 4].reshape(128, 384) for ky in range(3)], axis=1
        )
        rhs = wcv[2304 * d : 2304 * d + 1152]
        add = jnp.dot(lhs, rhs, preferred_element_type=F32)
        ctotal[3 * d] = ctotal[3 * d] + add.reshape(4, 32, 256)
    join((1, 2))
    left(sent_coarse)

    def coarse_y(d):
        arrive_y(sent_coarse, d, cedge_src, crecv_edge)
        edges_beside_y(2, cedge_src, d)
        y_rim(2, 2, 3, cedge_src, zcy, d)
        lhs = jnp.concatenate(
            [zcy[d, kx : kx + 4].reshape(128, 384) for kx in range(3)], axis=1
        )
        rhs = jnp.concatenate(
            [
                wcv[1152 * kx + 768 * d : 1152 * kx + 768 * d + 384]
                for kx in range(3)
            ],
            axis=0,
        )
        add = jnp.dot(lhs, rhs, preferred_element_type=F32)
        ctotal[:, 3 * d] = ctotal[:, 3 * d] + add.reshape(4, 32, 256)
        join((3 * d,))

    by_turns(coarse_y)


def local(gx, gy, features, slot_cell, neighbours, w1, b1, w2, b2, wc, bc, wl):
    operands = [
        pltpu.with_memory_space_constraint(operand, pltpu.HBM)
        for operand in (
            slot_cell.reshape(4),
            neighbours.reshape(4, 26),
            features.reshape(4, 8, 64, 128),
            w1.reshape(3, 3, 384, 128),
            b1.reshape(1, 128),
            w2.reshape(3, 3, 384, 128),
            b2.reshape(1, 128),
            wc.reshape(3456, 256),
            bc.reshape(1, 256),
            wl,
        )
    ]
    result = pl.pallas_call(
        functools.partial(kernel, gx, gy),
        out_shape=jax.ShapeDtypeStruct((4, 4, 2, 8, 8, 128), F32),
        in_specs=[pl.BlockSpec(memory_space=pl.ANY)] * 10,
        out_specs=pl.BlockSpec(memory_space=pltpu.VMEM),
        scratch_shapes=[
            pltpu.SMEM((4,), jnp.int32),
            pltpu.SMEM((4, 26), jnp.int32),
            pltpu.VMEM((1, 128), F32),
            pltpu.VMEM((1, 128), F32),
            pltpu.VMEM((1, 256), F32),
            pltpu.VMEM((4, 8, 64, 128), BF16),
            pltpu.VMEM((2, 4, 8, 16, 128), BF16),
            pltpu.VMEM((5, 4, 2, 8, 8, 128), F32),
            pltpu.VMEM((5, 4, 2, 8, 8, 128), F32),
            pltpu.VMEM((5, 4, 4, 8, 128), F32),
            pltpu.VMEM((4, 17, 1, 8, 128), F32),
            pltpu.VMEM((4, 17, 1, 8, 128), F32),
            pltpu.VMEM((2, 4, 10, 32, 384), BF16),
            pltpu.VMEM((2, 4, 10, 32, 384), BF16),
            pltpu.VMEM((2, 10, 32, 384), BF16),
            pltpu.VMEM((2, 10, 32, 384), BF16),
            pltpu.VMEM((6, 6, 32, 384), BF16),
            pltpu.VMEM((2, 6, 32, 384), BF16),
            pltpu.VMEM((2, 6, 32, 384), BF16),
            pltpu.VMEM((4, 3, 384, 256), BF16),
            pltpu.VMEM((4, 3, 384, 256), BF16),
            pltpu.VMEM((3456, 256), BF16),
            pltpu.VMEM((256, 128), BF16),
            pltpu.VMEM((4, 2, 8, 32, 128), F32),
            pltpu.VMEM((4, 4, 32, 256), F32),
            pltpu.VMEM((2, 4, 32, 128), BF16),
            pltpu.VMEM((2, 4, 32, 128), BF16),
            pltpu.VMEM((4, 32, 128), BF16),
            pltpu.VMEM((4, 32, 128), BF16),
            pltpu.SemaphoreType.DMA((12,)),
            pltpu.SemaphoreType.DMA((2,)),
            pltpu.SemaphoreType.DMA((3, 8)),
            pltpu.SemaphoreType.DMA((3, 8)),
        ]
        + [pltpu.VMEM((9, 64, 128), BF16)] * 8
        + [pltpu.VMEM((5, 32, 128), BF16)] * 4,
        compiler_params=pltpu.CompilerParams(
            collective_id=0, has_side_effects=True, vmem_limit_bytes=48 * 2**20
        ),
        cost_estimate=pl.CostEstimate(
            flops=8_000_000_000, bytes_accessed=8_000_000, transcendentals=0
        ),
        name="unet_window",
    )(*operands)
    return result.reshape(1, 1, 4, 512, 128)


def solution(mesh):
    placed = (
        P("gx", "gy", None, None, None),
        P("gx", "gy", None),
        P("gx", "gy", None, None),
    ) + (P(),) * 7
    return jax.shard_map(
        functools.partial(local, mesh.shape["gx"], mesh.shape["gy"]),
        mesh=mesh,
        in_specs=placed,
        out_specs=P("gx", "gy", None, None, None),
        check_vma=False,
    )
```
